32 devices in a mesh: rep: 2 (over x), fsdp: 16 (over z, y, core).
Axes of the slice: x: 2, y: 2, z: 4, core: 2. Of those that a mesh axis runs over, the one named last changes fastest.
Arguments:
- activations: bfloat16 [2, 2, 2816, 2560], P('rep', None, 'fsdp'), may hold values from -6 to 6
- residual: bfloat16 [2, 2, 2816, 5120], P('rep', None, 'fsdp'), may hold values from -6 to 6
- upstream: bfloat16 [2, 2, 2816, 5120], P('rep', None, 'fsdp'), may hold values from -6 to 6
- norm_gain: float32 [5120], replicated, may hold values from 0.5 to 1.5
- params: float32 [2, 128, 40, 5, 128], P('rep', 'fsdp'), may hold values from -6 to 6
- momentum: float32 [2, 128, 40, 5, 128], P('rep', 'fsdp'), may hold values from -6 to 6
- pattern: int32 [40, 5], replicated, may hold values from 0 to 19, as said below
- step_index: int32 [1], replicated, may hold values from 0 to 2999
Outputs:
- params_out: float32 [2, 128, 40, 5, 128], P('rep', 'fsdp')
- momentum_out: float32 [2, 128, 40, 5, 128], P('rep', 'fsdp')
The draws below stay inside these ranges and needn't reach their ends.
Inputs may be any that keep to these rules, and one draw needn't show every extreme that they name: `pattern`: each output block column c lists 5 different input blocks, the first of them c mod 20.
All inputs are finite; a program needn't handle non-finite values.
Results may differ from the reference program's by a relative error of at most 0.012.
Values may be sent and summed in bfloat16 or wider, within the bound.
No kernel may reach another device: no remote copies, remote signals or barrier semaphores. Data moves between devices by JAX's collectives and lax.ppermute only.
A program may use at most 128 MiB of HBM per device.

```python
import math
import jax
import jax.numpy as jnp
from jax import lax

D = 5120
HK = 2560
BS = 128
TOK_DEV = 176
STEPS = 2
HB = 20
OB = 40
BPC = 5
TOKENS = 2816
REP = 2
N_FSDP = 16


def draw_pattern(key, part):
    column = jnp.arange(OB, dtype=jnp.int32)
    subkeys = jax.random.split(key, OB)
    offsets = jax.vmap(lambda sub: jax.random.permutation(sub, HB - 1)[:BPC - 1])(subkeys).astype(jnp.int32)
    anchor = column % HB
    chosen = (anchor[:, None] + 1 + offsets) % HB
    return jnp.concatenate([anchor[:, None], chosen], axis=1).astype(jnp.int32)


def shard_levels(key, extent, shards, least, top_value):
    def one(axis_at, shards_of):
        draws = jax.random.uniform(jax.random.fold_in(jax.random.fold_in(key, 6), axis_at), (shards_of,), jnp.float32, least / len(shards), top_value / len(shards))
        return jnp.repeat(jnp.exp(draws), extent[axis_at] // shards_of).reshape((-1,) + (1,) * (len(extent) - axis_at - 1))

    loudness = one(*shards[0])
    for cut in shards[1:]:
        loudness = loudness * one(*cut)
    return loudness


def bell_draw(stream_key, dims, spread, most, pieces=(), kind=jnp.bfloat16):
    level = shard_levels(stream_key, dims, pieces, -0.22, 0.18) if pieces else 1.0
    values = jax.random.normal(stream_key, dims, jnp.float32) * spread * level
    return jnp.minimum(jnp.maximum(values, -most), most).astype(kind)


def setup_inputs(seed: int = 0) -> dict:
    arg_keys = jax.random.split(jax.random.key(seed), 9)
    activations = bell_draw(arg_keys[0], (REP, STEPS, TOKENS, HK), 1.0, 6.0, ((0, 2), (2, 16)))
    residual = bell_draw(arg_keys[1], (REP, STEPS, TOKENS, D), 1.0, 6.0, ((0, 2), (2, 16)))
    upstream = bell_draw(arg_keys[2], (REP, STEPS, TOKENS, D), 1.0, 6.0, ((0, 2), (2, 16)))
    norm_gain = jnp.clip(1.0 + 0.1 * jax.random.normal(arg_keys[3], (D,), jnp.float32), 0.5, 1.5)
    params = bell_draw(arg_keys[4], (REP, BS, OB, BPC, BS), 1.0, 6.0, ((0, 2), (1, 16)), jnp.float32)
    momentum = bell_draw(arg_keys[5], (REP, BS, OB, BPC, BS), 1.0, 6.0, ((0, 2), (1, 16)), jnp.float32)
    pattern = draw_pattern(jax.random.fold_in(arg_keys[8], 71), 0)
    step_index = jax.random.randint(arg_keys[7], (1,), 0, 3000).astype(jnp.int32)
    return dict(activations=activations, residual=residual, upstream=upstream, norm_gain=norm_gain, params=params, momentum=momentum, pattern=pattern, step_index=step_index)


learn_rate = 0.1
momentum_beta = 0.9
decay_keep = 0.999
epsilon = 1e-06

def norm_backward(pre_norm, upstream_rows, gain):
    inv_rms = lax.rsqrt(lax.optimization_barrier(jnp.mean(pre_norm * pre_norm, axis=-1, keepdims=True)) + epsilon)
    weighted = gain * upstream_rows
    inner_mean = lax.optimization_barrier(jnp.mean(pre_norm * weighted, axis=-1, keepdims=True))
    return inv_rms * weighted - pre_norm * inv_rms * inv_rms * inv_rms * inner_mean

def reference(activations, residual, upstream, norm_gain, params, momentum, pattern, step_index):
    scaling = 1.0 / math.sqrt(BPC * BS)
    gain = norm_gain.astype(jnp.float32)

    def replica_grad(inputs):
        weights, acts_rep, resid_rep, upper_rep = inputs
        low_weights = lax.optimization_barrier(weights.astype(jnp.bfloat16)).astype(jnp.float32)

        def group_term(group):
            offset = (group * TOK_DEV).astype(jnp.int32)
            acts_grp = lax.dynamic_slice_in_dim(acts_rep, offset, TOK_DEV, 0)
            resid_grp = lax.dynamic_slice_in_dim(resid_rep, offset, TOK_DEV, 0)
            upper_grp = lax.dynamic_slice_in_dim(upper_rep, offset, TOK_DEV, 0)
            picked = acts_grp.reshape(TOK_DEV, HB, BS)[:, pattern].astype(jnp.float32)
            projected = jnp.einsum('tcki,icko->tco', picked, low_weights)
            pre_norm = resid_grp.astype(jnp.float32) + scaling * projected.reshape(TOK_DEV, D)
            grad_pre = norm_backward(pre_norm, upper_grp.astype(jnp.float32), gain)
            grad_low = lax.optimization_barrier(grad_pre.astype(jnp.bfloat16)).astype(jnp.float32)
            partial_sum = jnp.einsum('tcki,tco->icko', picked, grad_low.reshape(TOK_DEV, OB, BS))
            return lax.optimization_barrier(partial_sum.astype(jnp.bfloat16)).astype(jnp.float32)
        terms = lax.map(group_term, jnp.arange(N_FSDP, dtype=jnp.int32))
        return scaling * lax.optimization_barrier(jnp.sum(terms, axis=0))
    weights_now = params
    moment = momentum
    for step_num in range(STEPS):
        gradient = lax.map(replica_grad, (weights_now, activations[:, step_num], residual[:, step_num], upstream[:, step_num]))
        moment = momentum_beta * moment + gradient
        weights_now = decay_keep * weights_now - learn_rate * moment
        hop_table = jnp.array([1, 2, 4], dtype=jnp.int32)
        hop_size = hop_table[(step_index[0] + step_num) % 3]
        partner = (jnp.arange(REP, dtype=jnp.int32) - hop_size) % REP
        weights_now = 0.5 * (weights_now + weights_now[partner])
    return (weights_now, moment)
```

```python
import math
from functools import partial

import jax
import jax.numpy as jnp
from jax import lax
from jax.experimental import pallas as pl
from jax.experimental.pallas import tpu as pltpu
from jax.sharding import PartitionSpec as P

learn_rate = 0.1
momentum_beta = 0.9
decay_keep = 0.999
epsilon = 1e-06

f32 = jnp.float32
bf16 = jnp.bfloat16
VMEM_LIMIT = 48 * 2**20


def ring_order(chips):
    if chips % 2:
        return list(range(chips))
    return list(range(0, chips, 2)) + list(range(chips - 1, 0, -2))


def ring_place(chips, chip):
    if chips % 2:
        return chip
    return jnp.where(chip % 2 == 0, chip // 2, chips - 1 - chip // 2)


def chip_at(chips, place):
    if chips % 2:
        return place
    return jnp.where(place < chips // 2, 2 * place, 2 * (chips - 1 - place) + 1)


class Ring:
    def __init__(self, devices):
        self.chips = devices // 2
        order = ring_order(self.chips)
        n = self.chips
        self.to_right = [
            (2 * order[p] + k, 2 * order[(p + 1) % n] + k) for p in range(n) for k in (0, 1)
        ]
        self.to_left = [(b, a) for a, b in self.to_right]
        self.pair = [(i, i ^ 1) for i in range(devices)]

    def right(self, x):
        return lax.ppermute(x, "fsdp", self.to_right)

    def left(self, x):
        return lax.ppermute(x, "fsdp", self.to_left)

    def swap(self, x):
        return lax.ppermute(x, "fsdp", self.pair)

    def hops(self, half):
        n = self.chips
        short = (n - 1) // 2
        long = n - 1 - short
        return (long, short) if half == 0 else (short, long)

    def gather(self, halves):
        n = self.chips
        slots = [[None] * n for _ in halves]
        moving = []
        for h, x in enumerate(halves):
            slots[h][0] = x
            moving.append([x, x])
        for s in range(1, n // 2 + 1):
            for h in range(len(halves)):
                to_right, to_left = self.hops(h)
                if s <= to_right:
                    moving[h][0] = self.right(moving[h][0])
                    slots[h][n - s] = moving[h][0]
                if s <= to_left:
                    moving[h][1] = self.left(moving[h][1])
                    slots[h][s] = moving[h][1]
        return slots

    def scatter_sum(self, slots):
        n = self.chips
        totals = []
        moving = [[None, None] for _ in slots]
        for s in range(n // 2, 0, -1):
            for h in range(len(slots)):
                to_right, to_left = self.hops(h)
                if s <= to_right:
                    term = slots[h][s]
                    if moving[h][0] is not None:
                        term = add_low(moving[h][0], term)
                    moving[h][0] = self.right(term)
                if s <= to_left:
                    term = slots[h][n - s]
                    if moving[h][1] is not None:
                        term = add_low(moving[h][1], term)
                    moving[h][1] = self.left(term)
        for h in range(len(slots)):
            total = slots[h][0].astype(f32)
            for part in moving[h]:
                if part is not None:
                    total = total + part.astype(f32)
            totals.append(total)
        return totals


def add_low(a, b):
    return (a.astype(f32) + b.astype(f32)).astype(bf16)


def forward_kernel(
    per_col, scaling, half_steps, n, scal, act_own, act_sib, *refs
):
    slots_a, slots_b = refs[:n], refs[n : 2 * n]
    res_own, res_sib, up_own, up_sib, gain = refs[2 * n : 2 * n + 5]
    pre, stats = refs[2 * n + 5 : 2 * n + 7]
    weight, sums = refs[2 * n + 7 :]
    step = pl.program_id(0)
    cols, block = slots_a[0].shape[0], slots_a[0].shape[3]
    depth = n * slots_a[0].shape[2]

    @pl.when(step == 0)
    def _():
        sums[...] = jnp.zeros_like(sums)

    def place(slots):
        for r in range(n):
            weight[scal[1 + r]] = slots[r][...]

    @pl.when(step < half_steps)
    def _():
        place(slots_a)

    @pl.when(step >= half_steps)
    def _():
        place(slots_b)

    for j in range(cols):
        at = 1 + n + (step * cols + j) * per_col
        lanes = [pl.ds(pl.multiple_of(scal[at + k] * block, block), block) for k in range(per_col)]
        w = jnp.concatenate(
            [weight[:, j, k].reshape(depth, block) for k in range(per_col)], axis=0
        )
        cut = slice(j * block, (j + 1) * block)
        for t, (act, res, up) in enumerate(((act_own, res_own, up_own), (act_sib, res_sib, up_sib))):
            x = jnp.concatenate([act[0, :, lane] for lane in lanes], axis=1)
            proj = jnp.dot(x, w, preferred_element_type=f32)
            value = res[0, :, cut].astype(f32) + scaling * proj
            pre[t, :, cut] = value
            g = gain[j] * up[0, :, cut].astype(f32)
            sums[t, 0] += value * value
            sums[t, 1] += value * g

    @pl.when(step == pl.num_programs(0) - 1)
    def _():
        lane = lax.broadcasted_iota(jnp.int32, stats.shape[1:], 1)
        for t in range(2):
            square = jnp.sum(sums[t, 0], axis=1, keepdims=True)
            inner = jnp.sum(sums[t, 1], axis=1, keepdims=True)
            stats[t] = jnp.where(lane < block // 2, square, inner)


def backward_kernel(
    per_col, width, half_steps, n, scal, act_t, pre, up_own, up_sib, gain, own, other, *refs
):
    out_a, out_b = refs[:n], refs[n : 2 * n]
    scales, grad, terms = refs[2 * n :]
    step = pl.program_id(0)
    cols, block = out_a[0].shape[0], out_a[0].shape[3]
    rows = pre.shape[1]
    depth = n * out_a[0].shape[2]

    @pl.when(step == 0)
    def _():
        grad[...] = jnp.zeros_like(grad)
        for t in range(2):
            total = own[t] + other[1 - t]
            square, inner = total[:, 0:1], total[:, block // 2 : block // 2 + 1]
            inv = lax.rsqrt(square / width + epsilon)
            scales[t, 0] = jnp.broadcast_to(inv, scales.shape[2:])
            scales[t, 1] = jnp.broadcast_to(inv * inv * inv * (inner / width), scales.shape[2:])

    for j in range(cols):
        at = 1 + n + (step * cols + j) * per_col
        cut = slice(j * block, (j + 1) * block)
        for t, up in enumerate((up_own, up_sib)):
            g = gain[j] * up[0, :, cut].astype(f32)
            value = scales[t, 0] * g - pre[t, :, cut] * scales[t, 1]
            grad[t * rows : (t + 1) * rows] = value.astype(bf16)
        x = jnp.concatenate([act_t[scal[at + k]] for k in range(per_col)], axis=0)
        term = jnp.dot(x, grad[...], preferred_element_type=f32).astype(bf16)
        terms[j] = term.reshape(per_col, n, depth // n, block)

    def place(outs):
        for r in range(n):
            outs[r][...] = terms[:, :, scal[1 + r]]

    @pl.when(step < half_steps)
    def _():
        place(out_a)

    @pl.when(step >= half_steps)
    def _():
        place(out_b)


def step_columns(columns):
    half = columns // 2
    return max(c for c in range(1, 6) if half % c == 0)


def forward(scal, step_num, activations, act_sib, slots, residual, res_sib, upstream, up_sib, gain, scaling):
    n = len(slots[0])
    half_cols, per_col, rows_in, block = slots[0][0].shape
    columns = 2 * half_cols
    cols = step_columns(columns)
    half_steps = half_cols // cols
    grid = columns // cols
    rows, features = activations.shape[1:]
    wide = cols * block

    whole = lambda: pl.BlockSpec((1, rows, features), lambda i, s: (step_num, 0, 0))
    first = lambda: pl.BlockSpec(
        (cols, per_col, rows_in, block), lambda i, s: (jnp.minimum(i, half_steps - 1), 0, 0, 0)
    )
    second = lambda: pl.BlockSpec(
        (cols, per_col, rows_in, block), lambda i, s: (jnp.maximum(i - half_steps, 0), 0, 0, 0)
    )
    mine = lambda: pl.BlockSpec((1, rows, wide), lambda i, s: (step_num, 0, s[0] * grid + i))
    theirs = lambda: pl.BlockSpec((1, rows, wide), lambda i, s: (step_num, 0, i))
    flops = 4 * rows * columns * per_col * block * block
    return pl.pallas_call(
        partial(forward_kernel, per_col, scaling, half_steps, n),
        grid_spec=pltpu.PrefetchScalarGridSpec(
            num_scalar_prefetch=1,
            grid=(grid,),
            in_specs=[whole(), whole()]
            + [first() for _ in range(n)]
            + [second() for _ in range(n)]
            + [mine(), theirs(), mine(), theirs()]
            + [pl.BlockSpec((cols, 1, block), lambda i, s: (i, 0, 0))],
            out_specs=[
                pl.BlockSpec((2, rows, wide), lambda i, s: (0, 0, i)),
                pl.BlockSpec((2, rows, block), lambda i, s: (0, 0, 0)),
            ],
            scratch_shapes=[
                pltpu.VMEM((n, cols, per_col, rows_in, block), bf16),
                pltpu.VMEM((2, 2, rows, block), f32),
            ],
        ),
        out_shape=[
            jax.ShapeDtypeStruct((2, rows, columns * block), f32),
            jax.ShapeDtypeStruct((2, rows, block), f32),
        ],
        compiler_params=pltpu.CompilerParams(vmem_limit_bytes=VMEM_LIMIT),
        cost_estimate=pl.CostEstimate(flops=flops, bytes_accessed=16 * 2**20, transcendentals=0),
        name="forward",
    )(scal, activations, act_sib, *slots[0], *slots[1], residual, res_sib, upstream, up_sib, gain)


def backward(scal, step_num, act_t, pre, upstream, up_sib, gain, own, other, shard, width):
    half_cols, per_col, rows_in, block = shard
    n = block // rows_in
    columns = 2 * half_cols
    cols = step_columns(columns)
    half_steps = half_cols // cols
    grid = columns // cols
    rows = pre.shape[1]
    wide = cols * block
    in_blocks, _, tokens = act_t.shape

    first = lambda: pl.BlockSpec(
        (cols, per_col, rows_in, block), lambda i, s: (jnp.minimum(i, half_steps - 1), 0, 0, 0)
    )
    second = lambda: pl.BlockSpec(
        (cols, per_col, rows_in, block), lambda i, s: (jnp.maximum(i - half_steps, 0), 0, 0, 0)
    )
    sums = lambda: pl.BlockSpec((2, rows, block), lambda i, s: (0, 0, 0))
    flops = 4 * rows * columns * per_col * block * block
    out = pl.pallas_call(
        partial(backward_kernel, per_col, width, half_steps, n),
        grid_spec=pltpu.PrefetchScalarGridSpec(
            num_scalar_prefetch=1,
            grid=(grid,),
            in_specs=[
                pl.BlockSpec((in_blocks, block, tokens), lambda i, s: (0, 0, 0)),
                pl.BlockSpec((2, rows, wide), lambda i, s: (0, 0, i)),
                pl.BlockSpec((1, rows, wide), lambda i, s: (step_num, 0, s[0] * grid + i)),
                pl.BlockSpec((1, rows, wide), lambda i, s: (step_num, 0, i)),
                pl.BlockSpec((cols, 1, block), lambda i, s: (i, 0, 0)),
                sums(),
                sums(),
            ],
            out_specs=[first() for _ in range(n)] + [second() for _ in range(n)],
            scratch_shapes=[
                pltpu.VMEM((2, 2, rows, block), f32),
                pltpu.VMEM((tokens, block), bf16),
                pltpu.VMEM((cols, per_col, n, rows_in, block), bf16),
            ],
        ),
        out_shape=[jax.ShapeDtypeStruct(shard, bf16) for _ in range(2 * n)],
        compiler_params=pltpu.CompilerParams(vmem_limit_bytes=VMEM_LIMIT),
        cost_estimate=pl.CostEstimate(flops=flops, bytes_accessed=16 * 2**20, transcendentals=0),
        name="backward",
    )(scal, act_t, pre, upstream, up_sib, gain, own, other)
    return [out[:n], out[n:]]


def gossip_with(stride, halves):
    devices = lax.axis_size("rep")
    stride = stride % devices
    if stride == 0:
        return halves
    shift = [(i, (i + stride) % devices) for i in range(devices)]
    return [
        0.5 * (own + lax.ppermute(own.astype(bf16), "rep", shift).astype(f32)) for own in halves
    ]


def gossip(which, halves):
    return lax.switch(which, [partial(gossip_with, hop) for hop in (1, 2, 4)], halves)


def body(activations, residual, upstream, norm_gain, params, momentum, pattern, step_index):
    steps, rows, features = activations.shape[1:]
    width = residual.shape[3]
    own_rows, out_blocks, per_col, block = params.shape[1:]
    scaling = 1.0 / math.sqrt(per_col * block)
    ring = Ring(lax.axis_size("fsdp"))
    n = ring.chips
    columns = out_blocks // 2
    half_cols = columns // 2

    me = lax.axis_index("fsdp")
    core = me % 2
    place = ring_place(n, me // 2)
    slot_chip = chip_at(n, (place + jnp.arange(n, dtype=jnp.int32)) % n)
    mine = lax.dynamic_slice_in_dim(pattern, core * columns, columns, 0)
    scal = jnp.concatenate([core[None], slot_chip, mine.reshape(-1)]).astype(jnp.int32)

    def by_rows(first, second):
        return jnp.concatenate(
            [jnp.where(core == 0, first, second), jnp.where(core == 0, second, first)], axis=-2
        )

    def to_work(x):
        turned = x.transpose(1, 2, 0, 3)
        kept = lax.dynamic_slice_in_dim(turned, core * columns, columns, 0)
        given = ring.swap(lax.dynamic_slice_in_dim(turned, (1 - core) * columns, columns, 0))
        both = by_rows(kept, given)
        return [both[:half_cols], both[half_cols:]]

    def to_own(halves):
        x = jnp.concatenate(halves, axis=0)
        kept = lax.dynamic_slice_in_dim(x, core * own_rows, own_rows, 2)
        given = ring.swap(lax.dynamic_slice_in_dim(x, (1 - core) * own_rows, own_rows, 2))
        both = jnp.concatenate(
            [jnp.where(core == 0, kept, given), jnp.where(core == 0, given, kept)], axis=0
        )
        return both.transpose(2, 0, 1, 3)

    weights = to_work(params[0])
    low = [w.astype(bf16) for w in weights]
    moment = to_work(momentum[0])

    act, res, up = activations[0], residual[0], upstream[0]
    theirs = (1 - core) * (width // 2)
    act_sib = ring.swap(act)
    res_sib = ring.swap(lax.dynamic_slice_in_dim(res, theirs, width // 2, 2))
    up_sib = ring.swap(lax.dynamic_slice_in_dim(up, theirs, width // 2, 2))
    gain = lax.dynamic_slice_in_dim(norm_gain, core * (width // 2), width // 2, 0)
    gain = gain.reshape(columns, 1, block)
    pad = -(2 * rows) % block
    act_t = []
    for s in range(steps):
        tokens = jnp.concatenate([act[s], act_sib[s], jnp.zeros((pad, features), bf16)], axis=0)
        act_t.append(tokens.T.reshape(features // block, block, 2 * rows + pad))

    for s in range(steps):
        slots = ring.gather(low)
        pre, own = forward(scal, s, act, act_sib, slots, res, res_sib, up, up_sib, gain, scaling)
        other = ring.swap(own)
        terms = backward(
            scal, s, act_t[s], pre, up, up_sib, gain, own, other, low[0].shape, float(width)
        )
        which = (step_index[0] + s) % 3
        if s < steps - 1:
            gradient = [scaling * g for g in ring.scatter_sum(terms)]
            moment = [momentum_beta * m + g for m, g in zip(moment, gradient)]
            weights = [decay_keep * w - learn_rate * m for w, m in zip(weights, moment)]
            weights = gossip(which, weights)
            low = [w.astype(bf16) for w in weights]
    moment_base = to_own([momentum_beta * m for m in moment])
    weight_base = to_own(
        [decay_keep * w - learn_rate * momentum_beta * m for w, m in zip(weights, moment)]
    )
    gradient = scaling * to_own(ring.scatter_sum(terms))
    moment_out = moment_base + gradient
    weight_out = gossip(which, [weight_base - learn_rate * gradient])[0]
    return (weight_out[None], moment_out[None])


def solution(mesh):
    in_specs = (
        P("rep", None, "fsdp", None),
        P("rep", None, "fsdp", None),
        P("rep", None, "fsdp", None),
        P(),
        P("rep", "fsdp", None, None, None),
        P("rep", "fsdp", None, None, None),
        P(),
        P(),
    )
    out_specs = (P("rep", "fsdp", None, None, None), P("rep", "fsdp", None, None, None))
    return jax.shard_map(body, mesh=mesh, in_specs=in_specs, out_specs=out_specs, check_vma=False)
```

```python
import math
from functools import partial

import jax
import jax.numpy as jnp
import numpy as np
from jax import lax
from jax.experimental import pallas as pl
from jax.experimental.pallas import tpu as pltpu
from jax.sharding import PartitionSpec as P

learn_rate = 0.1
momentum_beta = 0.9
decay_keep = 0.999
epsilon = 1e-06

f32 = jnp.float32
bf16 = jnp.bfloat16
WHOLE = pl.BlockSpec(memory_space=pltpu.VMEM)
SCALARS = pl.BlockSpec(memory_space=pltpu.SMEM)
PARAMS = pltpu.CompilerParams(vmem_limit_bytes=16 * 2**20)


def vmem(x):
    return pltpu.with_memory_space_constraint(x, pltpu.VMEM)


def in_vmem(shape):
    return pltpu.VMEM(shape.shape, shape.dtype)


def after(x, *others):
    if not others:
        return x
    return lax.optimization_barrier((x, *others))[0]


def ring_order(chips):
    if chips % 2:
        return list(range(chips))
    return list(range(0, chips, 2)) + list(range(chips - 1, 0, -2))


def ring_place(chips, chip):
    if chips % 2:
        return chip
    return jnp.where(chip % 2 == 0, chip // 2, chips - 1 - chip // 2)


def chip_at(chips, place):
    if chips % 2:
        return place
    return jnp.where(place < chips // 2, 2 * place, 2 * (chips - 1 - place) + 1)


class Ring:
    def __init__(self, devices):
        self.chips = devices // 2
        order = ring_order(self.chips)
        n = self.chips
        self.to_right = [
            (2 * order[p] + k, 2 * order[(p + 1) % n] + k) for p in range(n) for k in (0, 1)
        ]
        self.to_left = [(b, a) for a, b in self.to_right]
        self.pair = [(i, i ^ 1) for i in range(devices)]

    def swap(self, x):
        return lax.ppermute(x, "fsdp", self.pair)

    def rounds(self):
        n = self.chips
        short = (n - 1) // 2
        rounds = []
        for s in range(1, n // 2 + 1):
            if s <= n - 1 - short:
                rounds.append([(0, 0, s), (1, 1, s)])
            if s <= short:
                rounds.append([(1, 0, s), (0, 1, s)])
        return rounds

    def move(self, x, direction):
        return lax.ppermute(x, "fsdp", self.to_left if direction else self.to_right)

    def gather(self, halves):
        n = self.chips
        slots = [[x] + [None] * (n - 1) for x in halves]
        for pair in self.rounds():
            for h, d, s in pair:
                x = slots[h][s - 1 if d else (1 - s) % n]
                slots[h][s if d else n - s] = self.move(x, d)
        return slots

    def scatter_sum(self, slots):
        n = self.chips
        moving = {}
        for pair in sorted(self.rounds(), key=lambda pair: -pair[0][2]):
            for h, d, s in pair:
                term = slots[h][n - s if d else s]
                if (h, d) in moving:
                    term = add_low(moving[h, d], term)
                moving[h, d] = self.move(term, d)
        return [
            [slots[h][0]] + [moving[h, d] for d in range(2) if (h, d) in moving]
            for h in range(len(slots))
        ]


def add_kernel(a, b, out):
    out[...] = (a[...].astype(f32) + b[...].astype(f32)).astype(bf16)


def add_low(a, b):
    return pl.pallas_call(
        add_kernel,
        in_specs=[WHOLE, WHOLE],
        out_specs=WHOLE,
        out_shape=in_vmem(a),
        compiler_params=PARAMS,
        cost_estimate=pl.CostEstimate(flops=a.size, bytes_accessed=6 * a.size, transcendentals=0),
        name="add",
    )(vmem(a), vmem(b))


def total(parts):
    return sum(part.astype(f32) for part in parts)


def split_kernel(rows, per_col, out_blocks, scal, x, kept, given):
    columns = kept.shape[0]

    def column(c, carry):
        for k in range(per_col):
            for out, core in ((kept, scal[0]), (given, 1 - scal[0])):
                start = k * out_blocks + core * columns + c
                out[c, k] = x[pl.ds(start, rows, stride=per_col * out_blocks), :]
        return carry

    lax.fori_loop(0, columns, column, 0, unroll=5 if columns % 5 == 0 else 1)


def split(scal, x):
    rows, out_blocks, per_col, block = x.shape
    flat = x.transpose(0, 2, 1, 3).reshape(-1, block)
    half = jax.ShapeDtypeStruct((out_blocks // 2, per_col, rows, block), f32)
    return pl.pallas_call(
        partial(split_kernel, rows, per_col, out_blocks),
        in_specs=[SCALARS, WHOLE],
        out_specs=[WHOLE, WHOLE],
        out_shape=[in_vmem(half), in_vmem(half)],
        compiler_params=PARAMS,
        cost_estimate=pl.CostEstimate(flops=0, bytes_accessed=2 * x.size * 4, transcendentals=0),
        name="split",
    )(scal, vmem(flat))


def pick_kernel(s, scal, acts, residual, upstream, given, kept, sems):
    wide = given.shape[2]
    theirs, ours = [pl.ds(pl.multiple_of(c * wide, wide), wide) for c in (1 - scal[0], scal[0])]
    copies = [
        pltpu.make_async_copy(source, to, sems.at[i])
        for i, (source, to) in enumerate(
            (
                (acts.at[0, s], given.at[0]),
                (residual.at[0, s, :, theirs], given.at[1]),
                (upstream.at[0, s, :, theirs], given.at[2]),
                (residual.at[0, s, :, ours], kept.at[0]),
                (upstream.at[0, s, :, ours], kept.at[1]),
            )
        )
    ]
    for copy in copies:
        copy.start()
    for copy in copies:
        copy.wait()


def pick(scal, s, acts, residual, upstream):
    rows, features = acts.shape[2:]
    shape = lambda count: in_vmem(jax.ShapeDtypeStruct((count, rows, features), bf16))
    return pl.pallas_call(
        partial(pick_kernel, s),
        in_specs=[SCALARS] + [pl.BlockSpec(memory_space=pl.ANY)] * 3,
        out_specs=[WHOLE, WHOLE],
        out_shape=[shape(3), shape(2)],
        scratch_shapes=[pltpu.SemaphoreType.DMA((5,))],
        compiler_params=PARAMS,
        cost_estimate=pl.CostEstimate(
            flops=0, bytes_accessed=20 * rows * features, transcendentals=0
        ),
        name="pick",
    )(scal, *[pltpu.with_memory_space_constraint(x, pltpu.HBM) for x in (acts, residual, upstream)])


def turn_kernel(own, sib, out):
    in_blocks, block, room = out.shape[1:]
    rows = own.shape[1]
    rest = jnp.zeros((room - rows, block), bf16)

    def one(p, carry):
        lane = pl.ds(pl.multiple_of(p * block, block), block)
        for t, x in enumerate((own, sib)):
            out[t, p] = jnp.concatenate([x[0, :, lane], rest], axis=0).T
        return carry

    lax.fori_loop(0, in_blocks, one, 0)


def turn(own, sib, block):
    _, rows, features = own.shape
    room = -(-rows // block) * block
    out = jax.ShapeDtypeStruct((2, features // block, block, room), bf16)
    return pl.pallas_call(
        turn_kernel,
        in_specs=[WHOLE, WHOLE],
        out_specs=WHOLE,
        out_shape=in_vmem(out),
        compiler_params=PARAMS,
        cost_estimate=pl.CostEstimate(flops=0, bytes_accessed=8 * rows * features, transcendentals=0),
        name="turn",
    )(vmem(own), vmem(sib))


def forward_kernel(per_col, scaling, n, scal, given, kept, sib, *refs):
    slots = refs[:n], refs[n : 2 * n]
    gain, pre, stats, weight, sums = refs[2 * n :]
    half_cols, _, rows_in, block = slots[0][0].shape
    depth = n * rows_in
    cols = weight.shape[1]
    sums[...] = jnp.zeros_like(sums)

    for h in range(2):

        def group(i, carry, h=h):
            for r in range(n):
                weight[scal[1 + r]] = slots[h][r][pl.ds(i * cols, cols)]
            for j in range(cols):
                c = h * half_cols + i * cols + j
                at = 1 + n + c * per_col
                lanes = [
                    pl.ds(pl.multiple_of(scal[at + k] * block, block), block)
                    for k in range(per_col)
                ]
                w = jnp.concatenate(
                    [weight[:, j, k].reshape(depth, block) for k in range(per_col)], axis=0
                )
                cut = pl.ds(pl.multiple_of(c * block, block), block)
                sides = ((given, kept, 0), (sib, sib, 1))
                for t, (act, beside, at) in enumerate(sides):
                    x = jnp.concatenate([act[0, :, lane] for lane in lanes], axis=1)
                    proj = jnp.dot(x, w, preferred_element_type=f32)
                    value = beside[at, :, cut].astype(f32) + scaling * proj
                    pre[t, :, cut] = value
                    g = gain[c] * beside[at + 1, :, cut].astype(f32)
                    sums[t, 0] += value * value
                    sums[t, 1] += value * g
            return carry

        lax.fori_loop(0, half_cols // cols, group, 0)

    lane = lax.broadcasted_iota(jnp.int32, stats.shape[1:], 1)
    for t in range(2):
        square = jnp.sum(sums[t, 0], axis=1, keepdims=True)
        inner = jnp.sum(sums[t, 1], axis=1, keepdims=True)
        stats[t] = jnp.where(lane < block // 2, square, inner)


def backward_kernel(
    per_col, width, n, scal, act_t, pre, kept, sib, gain, own, other, *refs
):
    outs = refs[:n], refs[n : 2 * n]
    scales, grad, terms = refs[2 * n :]
    half_cols, _, rows_in, block = outs[0][0].shape
    rows = pre.shape[1]
    cols = terms.shape[0]

    grad[...] = jnp.zeros_like(grad)
    for t in range(2):
        total = own[t] + other[1 - t]
        square, inner = total[:, 0:1], total[:, block // 2 : block // 2 + 1]
        inv = lax.rsqrt(square / width + epsilon)
        scales[t, 0] = jnp.broadcast_to(inv, scales.shape[2:])
        scales[t, 1] = jnp.broadcast_to(inv * inv * inv * (inner / width), scales.shape[2:])

    for h in range(2):

        def group(i, carry, h=h):
            for j in range(cols):
                c = h * half_cols + i * cols + j
                at = 1 + n + c * per_col
                cut = pl.ds(pl.multiple_of(c * block, block), block)
                for t, up in enumerate((kept.at[1], sib.at[2])):
                    g = gain[c] * up[:, cut].astype(f32)
                    value = scales[t, 0] * g - pre[t, :, cut] * scales[t, 1]
                    grad[j, t, :rows] = value.astype(bf16)
                term = None
                for t in range(2):
                    x = jnp.concatenate([act_t[t, scal[at + k]] for k in range(per_col)], axis=0)
                    part = jnp.dot(x, grad[j, t], preferred_element_type=f32)
                    term = part if term is None else term + part
                terms[j] = term.astype(bf16).reshape(per_col, n, rows_in, block)
            for r in range(n):
                outs[h][r][pl.ds(i * cols, cols)] = terms[:, :, scal[1 + r]]
            return carry

        lax.fori_loop(0, half_cols // cols, group, 0)


def group_columns(half_cols):
    return max(c for c in range(1, 6) if half_cols % c == 0)


def forward(scal, given, kept, sib, slots, gain, scaling):
    n = len(slots[0])
    half_cols, per_col, rows_in, block = slots[0][0].shape
    _, rows, wide = kept.shape
    cols = group_columns(half_cols)
    flops = 4 * rows * wide * per_col * block
    operands = [given, kept, sib, *slots[0], *slots[1], gain]
    return pl.pallas_call(
        partial(forward_kernel, per_col, scaling, n),
        in_specs=[SCALARS] + [WHOLE] * len(operands),
        out_specs=[WHOLE, WHOLE],
        out_shape=[
            in_vmem(jax.ShapeDtypeStruct((2, rows, wide), f32)),
            in_vmem(jax.ShapeDtypeStruct((2, rows, block), f32)),
        ],
        scratch_shapes=[
            pltpu.VMEM((n, cols, per_col, rows_in, block), bf16),
            pltpu.VMEM((2, 2, rows, block), f32),
        ],
        compiler_params=PARAMS,
        cost_estimate=pl.CostEstimate(flops=flops, bytes_accessed=16 * 2**20, transcendentals=0),
        name="forward",
    )(scal, *[vmem(x) for x in operands])


def backward(scal, act_t, pre, kept, sib, gain, own, other, shard, width):
    half_cols, per_col, rows_in, block = shard
    n = block // rows_in
    _, rows, wide = kept.shape
    room = act_t.shape[3]
    cols = group_columns(half_cols)
    flops = 4 * rows * wide * per_col * block
    operands = [act_t, pre, kept, sib, gain, own, other]
    out = pl.pallas_call(
        partial(backward_kernel, per_col, width, n),
        in_specs=[SCALARS] + [WHOLE] * len(operands),
        out_specs=[WHOLE] * (2 * n),
        out_shape=[in_vmem(jax.ShapeDtypeStruct(shard, bf16)) for _ in range(2 * n)],
        scratch_shapes=[
            pltpu.VMEM((2, 2, rows, block), f32),
            pltpu.VMEM((cols, 2, room, block), bf16),
            pltpu.VMEM((cols, per_col, n, rows_in, block), bf16),
        ],
        compiler_params=PARAMS,
        cost_estimate=pl.CostEstimate(flops=flops, bytes_accessed=16 * 2**20, transcendentals=0),
        name="backward",
    )(scal, *[vmem(x) for x in operands])
    return [out[:n], out[n:]]


def gossip_hops():
    devices = lax.axis_size("rep")
    hops = {}
    for entry, stride in enumerate((1, 2, 4)):
        if stride % devices:
            hops.setdefault(stride % devices, []).append(entry)
    return hops


def gossip(taken, weights):
    devices = lax.axis_size("rep")
    for hop, chosen in taken.items():
        shift = [(i, (i + hop) % devices) for i in range(devices)]

        def mixed(own, shift=shift):
            return 0.5 * (own + lax.ppermute(own.astype(bf16), "rep", shift).astype(f32))

        weights = lax.cond(chosen, mixed, lambda own: own, weights)
    return weights


def body(activations, residual, upstream, norm_gain, params, momentum, pattern, step_index):
    steps, rows, features = activations.shape[1:]
    width = residual.shape[3]
    own_rows, out_blocks, per_col, block = params.shape[1:]
    scaling = 1.0 / math.sqrt(per_col * block)
    ring = Ring(lax.axis_size("fsdp"))
    n = ring.chips
    columns = out_blocks // 2
    half_cols = columns // 2

    me = lax.axis_index("fsdp")
    core = me % 2
    place = ring_place(n, me // 2)
    slot_chip = chip_at(n, (place + jnp.arange(n, dtype=jnp.int32)) % n)
    mine = lax.dynamic_slice_in_dim(pattern, core * columns, columns, 0)
    gain = lax.dynamic_slice_in_dim(norm_gain, core * (width // 2), width // 2, 0)
    gain = gain.reshape(columns, 1, block)
    scal = jnp.concatenate([core[None], slot_chip, mine.reshape(-1)]).astype(jnp.int32)

    first = core == 0
    starts = {
        (mine, size): ((core if mine else 1 - core) * size).astype(jnp.uint32)
        for mine in (True, False)
        for size in (own_rows, width // 2)
    }
    taken = []
    for s in range(steps):
        entry = (step_index[0] + s) % 3
        taken.append(
            {
                hop: sum((entry == e).astype(jnp.int32) for e in entries) > 0
                for hop, entries in gossip_hops().items()
            }
        )

    def by_rows(one, other):
        return jnp.concatenate(
            [jnp.where(first, one, other), jnp.where(first, other, one)], axis=-2
        )

    def part(x, mine, size, axis):
        at = [np.uint32(0)] * x.ndim
        at[axis] = starts[mine, size]
        return lax.dynamic_slice(x, at, [size if i == axis else d for i, d in enumerate(x.shape)])

    class Back:
        def __init__(self, x):
            self.kept, self.given = part(x, True, own_rows, 2), part(x, False, own_rows, 2)

        def swap(self, *ahead):
            self.given = ring.swap(after(self.given, *ahead))
            return self.given

        def whole(self):
            low = jnp.where(first, self.kept, self.given)
            high = jnp.where(first, self.given, self.kept)
            return jnp.concatenate([low, high], axis=0).transpose(2, 0, 1, 3)

    kept_rows, given_rows = split(scal, params[0])
    kept_rows, scal, gain, first, starts, taken = lax.optimization_barrier(
        (kept_rows, scal, gain, first, starts, taken)
    )
    given_rows = ring.swap(given_rows)
    weights = by_rows(kept_rows, given_rows)
    low = weights.astype(bf16)
    halves = [low[:half_cols], low[half_cols:]]
    given, kept = pick(scal, 0, activations, residual, upstream)
    sib = ring.swap(after(given, given_rows))

    for s in range(steps):
        last = s == steps - 1
        slots = ring.gather(halves)
        act_t = turn(given, sib, block)
        ready = [act_t]
        if not last:
            later = pick(after(scal, slots[0][min(2, n // 2)]), s + 1, activations, residual, upstream)
            ready += later
        if s == 0:
            kept_rows, given_rows = split(after(scal, slots[0][1]), momentum[0])
            ready += [kept_rows, given_rows]
        if last:
            moment_back, weights_back = Back(moment), Back(weights)
            ready += [moment_back.given, weights_back.given]
        pre, own = forward(scal, given, kept, sib, slots, after(gain, *ready), scaling)
        other = ring.swap(own)
        terms = backward(
            scal, act_t, pre, kept, sib, gain, own, other, halves[0].shape, float(width)
        )
        terms = [list(t) for t in terms]
        beside = []
        if not last:
            given, kept = later
            sib = ring.swap(after(given, other))
            beside += [sib]
        if s == 0:
            given_rows = ring.swap(after(given_rows, other))
            beside += [given_rows]
        if last:
            beside += [moment_back.swap(other), weights_back.swap(other)]
        far = n // 2
        terms[0][far], terms[1][n - far] = lax.optimization_barrier(
            (terms[0][far], terms[1][n - far], *beside)
        )[:2]
        if s == 0:
            moment = by_rows(kept_rows, given_rows)
        parts = ring.scatter_sum(terms)
        gradient = jnp.concatenate([total(p) for p in parts], axis=0)
        if not last:
            moment = momentum_beta * moment + scaling * gradient
            weights = decay_keep * weights - learn_rate * moment
            weights = gossip(after(taken[s], weights), weights)
            low = weights.astype(bf16)
            halves = [low[:half_cols], low[half_cols:]]
    moment_base = momentum_beta * moment_back.whole()
    weight_base = decay_keep * weights_back.whole() - learn_rate * moment_base
    back = Back(gradient)
    back.swap()
    gradient = scaling * back.whole()
    moment_out = moment_base + gradient
    weight_out = gossip(taken[-1], weight_base - learn_rate * gradient)
    return (weight_out[None], moment_out[None])


def solution(mesh):
    in_specs = (
        P("rep", None, "fsdp", None),
        P("rep", None, "fsdp", None),
        P("rep", None, "fsdp", None),
        P(),
        P("rep", "fsdp", None, None, None),
        P("rep", "fsdp", None, None, None),
        P(),
        P(),
    )
    out_specs = (P("rep", "fsdp", None, None, None), P("rep", "fsdp", None, None, None))
    return jax.shard_map(body, mesh=mesh, in_specs=in_specs, out_specs=out_specs, check_vma=False)
```

```python
import math
from functools import partial

import jax
import jax.numpy as jnp
import numpy as np
from jax import lax
from jax.experimental import pallas as pl
from jax.experimental.pallas import tpu as pltpu
from jax.sharding import PartitionSpec as P

learn_rate = 0.1
momentum_beta = 0.9
decay_keep = 0.999
epsilon = 1e-06

f32 = jnp.float32
bf16 = jnp.bfloat16
WHOLE = pl.BlockSpec(memory_space=pltpu.VMEM)
SCALARS = pl.BlockSpec(memory_space=pltpu.SMEM)
PARAMS = pltpu.CompilerParams(vmem_limit_bytes=16 * 2**20)


def vmem(x):
    return pltpu.with_memory_space_constraint(x, pltpu.VMEM)


def in_vmem(shape):
    return pltpu.VMEM(shape.shape, shape.dtype)


def after(x, *others):
    if not others:
        return x
    return lax.optimization_barrier((x, *others))[0]


def ring_order(chips):
    if chips % 2:
        return list(range(chips))
    return list(range(0, chips, 2)) + list(range(chips - 1, 0, -2))


def ring_place(chips, chip):
    if chips % 2:
        return chip
    return jnp.where(chip % 2 == 0, chip // 2, chips - 1 - chip // 2)


def chip_at(chips, place):
    if chips % 2:
        return place
    return jnp.where(place < chips // 2, 2 * place, 2 * (chips - 1 - place) + 1)


class Ring:
    def __init__(self, devices):
        self.chips = devices // 2
        order = ring_order(self.chips)
        n = self.chips
        self.to_right = [
            (2 * order[p] + k, 2 * order[(p + 1) % n] + k) for p in range(n) for k in (0, 1)
        ]
        self.to_left = [(b, a) for a, b in self.to_right]
        self.pair = [(i, i ^ 1) for i in range(devices)]

    def swap(self, x):
        return lax.ppermute(x, "fsdp", self.pair)

    def rounds(self):
        n = self.chips
        short = (n - 1) // 2
        rounds = []
        for s in range(1, n // 2 + 1):
            if s <= n - 1 - short:
                rounds.append([(0, 0, s), (1, 1, s)])
            if s <= short:
                rounds.append([(1, 0, s), (0, 1, s)])
        return rounds

    def move(self, x, direction):
        return lax.ppermute(x, "fsdp", self.to_left if direction else self.to_right)

    def gather(self, halves, beside):
        n = self.chips
        slots = [[x] + [None] * (n - 1) for x in halves]
        arrived = []
        for i, pair in enumerate(self.rounds()):
            ready = beside[i](arrived[i - 3]) if i >= 3 and i in beside else []
            for h, d, s in pair:
                x = after(slots[h][s - 1 if d else (1 - s) % n], *ready)
                slots[h][s if d else n - s] = self.move(x, d)
                ready = []
            arrived.append(slots[pair[0][0]][n - pair[0][2]])
        return slots

    def scatter_sum(self, slots):
        n = self.chips
        moving = {}
        for pair in sorted(self.rounds(), key=lambda pair: -pair[0][2]):
            for h, d, s in pair:
                term = slots[h][n - s if d else s]
                if (h, d) in moving:
                    term = add_low(moving[h, d], term)
                moving[h, d] = self.move(term, d)
        return [
            [slots[h][0]] + [moving[h, d] for d in range(2) if (h, d) in moving]
            for h in range(len(slots))
        ]


def add_kernel(a, b, out):
    out[...] = (a[...].astype(f32) + b[...].astype(f32)).astype(bf16)


def add_low(a, b):
    return pl.pallas_call(
        add_kernel,
        in_specs=[WHOLE, WHOLE],
        out_specs=WHOLE,
        out_shape=in_vmem(a),
        compiler_params=PARAMS,
        cost_estimate=pl.CostEstimate(flops=a.size, bytes_accessed=6 * a.size, transcendentals=0),
        name="add",
    )(vmem(a), vmem(b))


def whole_call(kernel, name, operands, outs, scratch=(), scalars=(), raw=(), cost=(0, 0)):
    return pl.pallas_call(
        kernel,
        in_specs=[SCALARS] * len(scalars)
        + [pl.BlockSpec(memory_space=pl.ANY)] * len(raw)
        + [WHOLE] * len(operands),
        out_specs=[WHOLE] * len(outs),
        out_shape=[in_vmem(x) for x in outs],
        scratch_shapes=list(scratch),
        compiler_params=PARAMS,
        cost_estimate=pl.CostEstimate(flops=cost[0], bytes_accessed=cost[1], transcendentals=0),
        name=name,
    )(
        *scalars,
        *[pltpu.with_memory_space_constraint(x, pltpu.HBM) for x in raw],
        *[vmem(x) for x in operands],
    )


def by_core(body):
    core = lax.axis_index("fsdp") % 2
    for c in range(2):
        pl.when(core == c)(partial(body, c))


def columns_loop(columns, column):
    lax.fori_loop(0, columns, lambda c, _: column(c) or 0, 0, unroll=2 if columns % 2 == 0 else 1)


def halves_of(mine, theirs, core):
    return jnp.concatenate([theirs, mine] if core else [mine, theirs], axis=-2)


def rows_of(x, core):
    rows = x.shape[-2] // 2
    low, high = x[..., :rows, :], x[..., rows:, :]
    return (high, low) if core else (low, high)


def shapes_of(shard):
    half_cols, per_col, rows_in, block = shard
    rows = jax.ShapeDtypeStruct((2 * half_cols, per_col, rows_in // 2, block), f32)
    return rows, jax.ShapeDtypeStruct(shard, bf16)


def merge_kernel(mine, theirs, low_a, low_b):
    half_cols = low_a.shape[0]

    def body(core):
        for h, out in enumerate((low_a, low_b)):

            def column(c, h=h, out=out):
                at = h * half_cols + c
                out[c] = halves_of(mine[at], theirs[at], core).astype(bf16)

            columns_loop(half_cols, column)

    by_core(body)


def merge(mine, theirs, shard):
    low = shapes_of(shard)[1]
    return whole_call(merge_kernel, "merge", [mine, theirs], [low, low], cost=(0, mine.size * 12))


def gathered_sum(parts, c):
    return sum(part[c].astype(f32) for part in parts)


def update_kernel(count, scaling, *refs):
    parts = refs[:count], refs[count : 2 * count]
    moments, weights = refs[2 * count : 2 * count + 2], refs[2 * count + 2 : 2 * count + 4]
    far = refs[2 * count + 4 : 2 * count + 9]
    near, sems = refs[2 * count + 9 : 2 * count + 14], refs[-1]
    moments_out, weights_out, low = near[:2], near[2:4], near[4]
    half_cols = low.shape[0] // 2

    def body(core):
        for h in range(2):

            def column(c, h=h):
                at = h * half_cols + c
                news = []
                for r, gradient in enumerate(rows_of(gathered_sum(parts[h], c), core)):
                    moment = momentum_beta * moments[r][at] + scaling * gradient
                    moments_out[r][at] = moment
                    news.append(decay_keep * weights[r][at] - learn_rate * moment)
                    weights_out[r][at] = news[r]
                low[at] = halves_of(*news, core).astype(bf16)

            columns_loop(half_cols, column)

    by_core(body)
    copies = [pltpu.make_async_copy(near[i], far[i], sems.at[i]) for i in range(5)]
    for copy in copies:
        copy.start()
    for copy in copies:
        copy.wait()


def update(parts, moments, weights, scaling, shard):
    rows = shapes_of(shard)[0]
    low = jax.ShapeDtypeStruct((2 * shard[0], *shard[1:]), bf16)
    outs = [rows] * 4 + [low]
    operands = [*parts[0], *parts[1], *moments, *weights]
    out = pl.pallas_call(
        partial(update_kernel, len(parts[0]), scaling),
        in_specs=[WHOLE] * len(operands),
        out_specs=[pl.BlockSpec(memory_space=pl.ANY)] * 5,
        out_shape=[pltpu.HBM(x.shape, x.dtype) for x in outs],
        scratch_shapes=[pltpu.VMEM(x.shape, x.dtype) for x in outs]
        + [pltpu.SemaphoreType.DMA((5,))],
        compiler_params=PARAMS,
        cost_estimate=pl.CostEstimate(
            flops=rows.size * 20, bytes_accessed=rows.size * 60, transcendentals=0
        ),
        name="update",
    )(*[vmem(x) for x in operands])
    return out[:2], out[2:4], out[4]


def blend_kernel(keep, *refs):
    far, outs, (low_a, low_b) = refs[:3], refs[3:5], refs[5:7]
    near, sems = refs[7:10], refs[10]
    mine, theirs, part = near
    half_cols = low_a.shape[0]
    share = keep[0]
    copies = [pltpu.make_async_copy(far[i], near[i], sems.at[i]) for i in range(3)]
    for copy in copies:
        copy.start()
    for copy in copies:
        copy.wait()

    def body(core):
        for h, low in enumerate((low_a, low_b)):

            def column(c, h=h, low=low):
                at = h * half_cols + c
                news = []
                for own, to, other in zip(
                    (mine, theirs), outs, rows_of(part[at].astype(f32), core)
                ):
                    news.append(share * own[at] + (1.0 - share) * other)
                    to[at] = news[-1]
                low[c] = halves_of(*news, core).astype(bf16)

            columns_loop(half_cols, column)

    by_core(body)


def blend(keep, weights, partner, shard):
    rows, low = shapes_of(shard)
    outs = [rows, rows, low, low]
    raw = pl.BlockSpec(memory_space=pl.ANY)
    out = pl.pallas_call(
        blend_kernel,
        in_specs=[SCALARS] + [raw] * 3,
        out_specs=[WHOLE] * 4,
        out_shape=[in_vmem(x) for x in outs],
        scratch_shapes=[
            pltpu.VMEM(rows.shape, f32),
            pltpu.VMEM(rows.shape, f32),
            pltpu.VMEM(partner.shape, bf16),
            pltpu.SemaphoreType.DMA((3,)),
        ],
        compiler_params=PARAMS,
        cost_estimate=pl.CostEstimate(
            flops=rows.size * 6, bytes_accessed=rows.size * 24, transcendentals=0
        ),
        name="blend",
    )(keep, *[pltpu.with_memory_space_constraint(x, pltpu.HBM) for x in (*weights, partner)])
    return out[:2], list(out[2:])


def last_sum_kernel(count, *refs):
    parts = refs[:count], refs[count : 2 * count]
    outs = refs[2 * count :]
    half_cols = parts[0][0].shape[0]

    def body(core):
        for h in range(2):

            def column(c, h=h):
                for out, rows in zip(outs, rows_of(gathered_sum(parts[h], c), core)):
                    out[h * half_cols + c] = rows

            columns_loop(half_cols, column)

    by_core(body)


def last_sum(parts, shard):
    rows = shapes_of(shard)[0]
    return whole_call(
        partial(last_sum_kernel, len(parts[0])),
        "last_sum",
        [*parts[0], *parts[1]],
        [rows, rows],
        cost=(rows.size * 4, rows.size * 20),
    )


def finish_kernel(out_blocks, scaling, *refs):
    gradients, moments, weights = refs[:2], refs[2:4], refs[4:6]
    moment_out, weight_out = refs[6:]
    columns, per_col, rows = gradients[0].shape[:3]
    core = lax.axis_index("fsdp") % 2

    def column(c):
        for side, owner in enumerate((core, 1 - core)):
            for k in range(per_col):
                at = pl.ds(k * out_blocks + owner * columns + c, rows, stride=per_col * out_blocks)
                moment = momentum_beta * moments[side][c, k] + scaling * gradients[side][c, k]
                moment_out[at, :] = moment
                weight_out[at, :] = decay_keep * weights[side][c, k] - learn_rate * moment

    columns_loop(columns, column)


def finish(gradients, moments, weights, scaling):
    columns, per_col, rows, block = gradients[0].shape
    out = jax.ShapeDtypeStruct((rows * per_col * 2 * columns, block), f32)
    operands = [*gradients, *moments, *weights]
    moment, weight = pl.pallas_call(
        partial(finish_kernel, 2 * columns, scaling),
        in_specs=[WHOLE] * len(operands),
        out_specs=[WHOLE, WHOLE],
        out_shape=[out, out],
        compiler_params=PARAMS,
        cost_estimate=pl.CostEstimate(flops=out.size * 6, bytes_accessed=out.size * 40, transcendentals=0),
        name="finish",
    )(*[vmem(x) for x in operands])
    shape = (rows, per_col, 2 * columns, block)
    return [x.reshape(shape).transpose(0, 2, 1, 3) for x in (weight, moment)]


def split_kernel(out_blocks, raw, kept, given, x, sem):
    columns, per_col, rows = kept.shape[:3]
    core = lax.axis_index("fsdp") % 2
    copy = pltpu.make_async_copy(raw, x, sem)
    copy.start()
    copy.wait()

    def column(c):
        for k in range(per_col):
            for out, owner in ((given, 1 - core), (kept, core)):
                start = k * out_blocks + owner * columns + c
                out[c, k] = x[pl.ds(start, rows, stride=per_col * out_blocks), :]

    columns_loop(columns, column)


def split(x):
    rows, out_blocks, per_col, block = x.shape
    flat = x.transpose(0, 2, 1, 3).reshape(-1, block)
    half = jax.ShapeDtypeStruct((out_blocks // 2, per_col, rows, block), f32)
    return whole_call(
        partial(split_kernel, out_blocks),
        "split",
        [],
        [half, half],
        scratch=[pltpu.VMEM(flat.shape, f32), pltpu.SemaphoreType.DMA(())],
        raw=[flat],
        cost=(0, 8 * x.size),
    )


def row_cuts(rows):
    if rows % 16:
        return [pl.ds(0, rows)]
    tiles = rows // 16
    pieces = min(4, tiles)
    edges = [16 * (tiles * i // pieces) for i in range(pieces + 1)]
    return [pl.ds(a, b - a) for a, b in zip(edges, edges[1:])]


def pick_kernel(s, mine, raws, outs, sems):
    core = lax.axis_index("fsdp") % 2
    half = core if mine else 1 - core
    copies = []
    _, rows, wide = outs.shape
    for i, raw in enumerate(raws):
        lanes = pl.ds(0, wide)
        if raw.shape[3] != wide:
            lanes = pl.ds(pl.multiple_of(half * wide, wide), wide)
        for j, cut in enumerate(row_cuts(rows)):
            copies.append(
                pltpu.make_async_copy(raw.at[0, s, cut, lanes], outs.at[i, cut], sems.at[i, j])
            )
    for copy in copies:
        copy.start()
    for copy in copies:
        copy.wait()


def pick(s, mine, wide, *raws):
    rows = raws[0].shape[2]
    count = len(raws)

    def kernel(*refs):
        pick_kernel(s, mine, refs[:count], refs[count], refs[count + 1])

    (out,) = whole_call(
        kernel,
        "pick",
        [],
        [jax.ShapeDtypeStruct((count, rows, wide), bf16)],
        scratch=[pltpu.SemaphoreType.DMA((count, len(row_cuts(rows))))],
        raw=raws,
        cost=(0, 4 * count * rows * wide),
    )
    return out


def turn_kernel(own, sib, out):
    in_blocks, block, room = out.shape[1:]
    rows = own.shape[1]
    rest = jnp.zeros((room - rows, block), bf16)

    def one(p, carry):
        lane = pl.ds(pl.multiple_of(p * block, block), block)
        for t, x in enumerate((own, sib)):
            out[t, p] = jnp.concatenate([x[0, :, lane], rest], axis=0).T
        return carry

    lax.fori_loop(0, in_blocks, one, 0)


def turn(own, sib, block):
    _, rows, features = own.shape
    room = -(-rows // block) * block
    out = jax.ShapeDtypeStruct((2, features // block, block, room), bf16)
    return pl.pallas_call(
        turn_kernel,
        in_specs=[WHOLE, WHOLE],
        out_specs=WHOLE,
        out_shape=in_vmem(out),
        compiler_params=PARAMS,
        cost_estimate=pl.CostEstimate(flops=0, bytes_accessed=8 * rows * features, transcendentals=0),
        name="turn",
    )(vmem(own), vmem(sib))


def forward_kernel(per_col, scaling, n, scal, given, kept, sib, *refs):
    slots = refs[:n], refs[n : 2 * n]
    gain, pre, stats, weight, sums = refs[2 * n :]
    half_cols, _, rows_in, block = slots[0][0].shape
    depth = n * rows_in
    cols = weight.shape[1]
    sums[...] = jnp.zeros_like(sums)

    for h in range(2):

        def group(i, carry, h=h):
            for r in range(n):
                weight[scal[r]] = slots[h][r][pl.ds(i * cols, cols)]
            for j in range(cols):
                c = h * half_cols + i * cols + j
                lanes = [
                    pl.ds(pl.multiple_of(scal[n + c * per_col + k] * block, block), block)
                    for k in range(per_col)
                ]
                w = jnp.concatenate(
                    [weight[:, j, k].reshape(depth, block) for k in range(per_col)], axis=0
                )
                cut = pl.ds(pl.multiple_of(c * block, block), block)
                sides = ((given, kept, 0), (sib, sib, 1))
                for t, (act, beside, at) in enumerate(sides):
                    x = jnp.concatenate([act[0, :, lane] for lane in lanes], axis=1)
                    proj = jnp.dot(x, w, preferred_element_type=f32)
                    value = beside[at, :, cut].astype(f32) + scaling * proj
                    pre[t, :, cut] = value
                    g = gain[c] * beside[at + 1, :, cut].astype(f32)
                    sums[t, 0] += value * value
                    sums[t, 1] += value * g
            return carry

        lax.fori_loop(0, half_cols // cols, group, 0)

    lane = lax.broadcasted_iota(jnp.int32, stats.shape[1:], 1)
    for t in range(2):
        square = jnp.sum(sums[t, 0], axis=1, keepdims=True)
        inner = jnp.sum(sums[t, 1], axis=1, keepdims=True)
        stats[t] = jnp.where(lane < block // 2, square, inner)


def backward_kernel(
    per_col, width, n, scal, act_t, pre, kept, sib, gain, own, other, *refs
):
    outs = refs[:n], refs[n : 2 * n]
    scales, grad, terms = refs[2 * n :]
    half_cols, _, rows_in, block = outs[0][0].shape
    rows = pre.shape[1]
    cols = terms.shape[0]

    grad[...] = jnp.zeros_like(grad)
    for t in range(2):
        total = own[t] + other[1 - t]
        square, inner = total[:, 0:1], total[:, block // 2 : block // 2 + 1]
        inv = lax.rsqrt(square / width + epsilon)
        scales[t, 0] = jnp.broadcast_to(inv, scales.shape[2:])
        scales[t, 1] = jnp.broadcast_to(inv * inv * inv * (inner / width), scales.shape[2:])

    for h in range(2):

        def group(i, carry, h=h):
            for j in range(cols):
                c = h * half_cols + i * cols + j
                cut = pl.ds(pl.multiple_of(c * block, block), block)
                for t, up in enumerate((kept.at[1], sib.at[2])):
                    g = gain[c] * up[:, cut].astype(f32)
                    value = scales[t, 0] * g - pre[t, :, cut] * scales[t, 1]
                    grad[j, t, :rows] = value.astype(bf16)
                term = None
                for t in range(2):
                    x = jnp.concatenate([act_t[t, scal[n + c * per_col + k]] for k in range(per_col)], axis=0)
                    part = jnp.dot(x, grad[j, t], preferred_element_type=f32)
                    term = part if term is None else term + part
                terms[j] = term.astype(bf16).reshape(per_col, n, rows_in, block)
            for r in range(n):
                outs[h][r][pl.ds(i * cols, cols)] = terms[:, :, scal[r]]
            return carry

        lax.fori_loop(0, half_cols // cols, group, 0)


def group_columns(half_cols):
    return max(c for c in range(1, 6) if half_cols % c == 0)


def forward(scal, given, kept, sib, slots, gain, scaling):
    n = len(slots[0])
    half_cols, per_col, rows_in, block = slots[0][0].shape
    _, rows, wide = kept.shape
    cols = group_columns(half_cols)
    flops = 4 * rows * wide * per_col * block
    operands = [given, kept, sib, *slots[0], *slots[1], gain]
    return pl.pallas_call(
        partial(forward_kernel, per_col, scaling, n),
        in_specs=[SCALARS] + [WHOLE] * len(operands),
        out_specs=[WHOLE, WHOLE],
        out_shape=[
            in_vmem(jax.ShapeDtypeStruct((2, rows, wide), f32)),
            in_vmem(jax.ShapeDtypeStruct((2, rows, block), f32)),
        ],
        scratch_shapes=[
            pltpu.VMEM((n, cols, per_col, rows_in, block), bf16),
            pltpu.VMEM((2, 2, rows, block), f32),
        ],
        compiler_params=PARAMS,
        cost_estimate=pl.CostEstimate(flops=flops, bytes_accessed=16 * 2**20, transcendentals=0),
        name="forward",
    )(scal, *[vmem(x) for x in operands])


def backward(scal, act_t, pre, kept, sib, gain, own, other, shard, width):
    half_cols, per_col, rows_in, block = shard
    n = block // rows_in
    _, rows, wide = kept.shape
    room = act_t.shape[3]
    cols = group_columns(half_cols)
    flops = 4 * rows * wide * per_col * block
    operands = [act_t, pre, kept, sib, gain, own, other]
    out = pl.pallas_call(
        partial(backward_kernel, per_col, width, n),
        in_specs=[SCALARS] + [WHOLE] * len(operands),
        out_specs=[WHOLE] * (2 * n),
        out_shape=[in_vmem(jax.ShapeDtypeStruct(shard, bf16)) for _ in range(2 * n)],
        scratch_shapes=[
            pltpu.VMEM((2, 2, rows, block), f32),
            pltpu.VMEM((cols, 2, room, block), bf16),
            pltpu.VMEM((cols, per_col, n, rows_in, block), bf16),
        ],
        compiler_params=PARAMS,
        cost_estimate=pl.CostEstimate(flops=flops, bytes_accessed=16 * 2**20, transcendentals=0),
        name="backward",
    )(scal, *[vmem(x) for x in operands])
    return [out[:n], out[n:]]


def gossip_hops():
    devices = lax.axis_size("rep")
    hops = {}
    for entry, stride in enumerate((1, 2, 4)):
        if stride % devices:
            hops.setdefault(stride % devices, []).append(entry)
    return hops


def partner_of(taken, low):
    devices = lax.axis_size("rep")
    partner = None
    for hop, chosen in taken.items():
        shift = [(i, (i + hop) % devices) for i in range(devices)]
        moved = lambda x, last, shift=shift: lax.ppermute(x, "rep", shift)
        if partner is None:
            partner = lax.cond(chosen, moved, lambda x, last: jnp.zeros_like(x), low, 0)
        else:
            partner = lax.cond(chosen, moved, lambda x, last: last, low, partner)
    return low if partner is None else partner


def mixed(taken, weight):
    devices = lax.axis_size("rep")
    for hop, chosen in taken.items():
        shift = [(i, (i + hop) % devices) for i in range(devices)]

        def mean(own, shift=shift):
            return 0.5 * (own + lax.ppermute(own.astype(bf16), "rep", shift).astype(f32))

        weight = lax.cond(chosen, mean, lambda own: own, weight)
    return weight


def body(activations, residual, upstream, norm_gain, params, momentum, pattern, step_index):
    steps, rows, features = activations.shape[1:]
    width = residual.shape[3]
    own_rows, out_blocks, per_col, block = params.shape[1:]
    scaling = 1.0 / math.sqrt(per_col * block)
    ring = Ring(lax.axis_size("fsdp"))
    n = ring.chips
    columns = out_blocks // 2
    half_cols = columns // 2

    me = lax.axis_index("fsdp")
    core = me % 2
    chips = chip_at(n, (ring_place(n, me // 2) + jnp.arange(n, dtype=jnp.int32)) % n)
    used = lax.dynamic_slice_in_dim(pattern, core * columns, columns, 0)
    scal = jnp.concatenate([chips, used.reshape(-1)]).astype(jnp.int32)
    gain = lax.dynamic_slice_in_dim(norm_gain, core * (width // 2), width // 2, 0)
    gain = gain.reshape(columns, 1, block)

    taken, keeps = [], []
    for s in range(steps):
        entry = (step_index[0] + s) % 3
        taken.append(
            {
                hop: sum((entry == e).astype(jnp.int32) for e in entries) > 0
                for hop, entries in gossip_hops().items()
            }
        )
        moved = sum([hop.astype(jnp.int32) for hop in taken[s].values()], jnp.int32(0)) > 0
        keeps.append(jnp.where(moved, 0.5, 1.0).astype(f32).reshape(1))

    shard = (half_cols, per_col, 2 * own_rows, block)
    mine, theirs = split(params[0])
    theirs = ring.swap(theirs)
    weights = [mine, theirs]
    halves = list(merge(*weights, shard))
    halves[0], scal, gain, taken, keeps = lax.optimization_barrier(
        (halves[0], scal, gain, taken, keeps)
    )
    tokens = (activations, residual, upstream)

    def picked(s, mine, arrived):
        arrays = tokens[1:] if mine else tokens
        return pick(s, mine, features, *[after(x, arrived) for x in arrays])

    given = picked(0, False, halves[0])
    sib = ring.swap(given)
    state = {}

    def keep(name, make):
        def work(arrived):
            state[name] = make(arrived)
            return jax.tree.leaves(state[name])

        return work

    for s in range(steps):
        last = s == steps - 1
        beside = {}
        if s == 0:
            beside[3] = keep("moments", lambda arrived: split(after(momentum, arrived)[0]))
        beside[4] = keep("kept", lambda arrived: picked(s, True, arrived))
        if not last:
            beside[5] = keep("later", lambda arrived: picked(s + 1, False, arrived))
        slots = ring.gather(halves, beside)
        for i, work in beside.items():
            if i >= len(ring.rounds()):
                work(halves[0])
        kept = state["kept"]
        act_t = turn(given, sib, block)
        pre, own = forward(scal, given, kept, sib, slots, after(gain, act_t), scaling)
        other = ring.swap(own)
        terms = backward(scal, act_t, pre, kept, sib, gain, own, other, shard, float(width))
        ready = []
        if not last:
            given = state["later"]
            sib = ring.swap(after(given, other))
            ready += [sib]
        if s == 0:
            moments = state["moments"]
            moments = [moments[0], ring.swap(after(moments[1], other))]
            ready += [moments[1]]
        if last:
            moments = [moments[0], ring.swap(after(moments[1], other))]
            weights = [weights[0], ring.swap(after(weights[1], other))]
            ready += [moments[1], weights[1]]
        far = n // 2
        terms = [list(t) for t in terms]
        terms[0][far], terms[1][n - far] = lax.optimization_barrier(
            (terms[0][far], terms[1][n - far], *ready)
        )[:2]
        parts = ring.scatter_sum(terms)
        if not last:
            moments, weights, low = update(parts, moments, weights, scaling, shard)
            partner = partner_of(after(taken[s], low), low)
            weights, halves = blend(keeps[s], weights, partner, shard)
    mine, theirs = last_sum(parts, shard)
    weight, moment = finish([mine, ring.swap(theirs)], moments, weights, scaling)
    return (mixed(after(taken[-1], weight), weight)[None], moment[None])


def solution(mesh):
    in_specs = (
        P("rep", None, "fsdp", None),
        P("rep", None, "fsdp", None),
        P("rep", None, "fsdp", None),
        P(),
        P("rep", "fsdp", None, None, None),
        P("rep", "fsdp", None, None, None),
        P(),
        P(),
    )
    out_specs = (P("rep", "fsdp", None, None, None), P("rep", "fsdp", None, None, None))
    return jax.shard_map(body, mesh=mesh, in_specs=in_specs, out_specs=out_specs, check_vma=False)
```

```python
import functools
import math
from functools import partial

import jax
import jax.numpy as jnp
import numpy as np
from jax import lax
from jax.experimental import pallas as pl
from jax.experimental.pallas import tpu as pltpu
from jax.sharding import PartitionSpec as P

learn_rate = 0.1
momentum_beta = 0.9
decay_keep = 0.999
epsilon = 1e-06

f32 = jnp.float32
bf16 = jnp.bfloat16
WHOLE = pl.BlockSpec(memory_space=pltpu.VMEM)
SCALARS = pl.BlockSpec(memory_space=pltpu.SMEM)
PARAMS = pltpu.CompilerParams(vmem_limit_bytes=16 * 2**20)


def vmem(x):
    return pltpu.with_memory_space_constraint(x, pltpu.VMEM)


def in_vmem(shape):
    return pltpu.VMEM(shape.shape, shape.dtype)


def after(x, *others):
    if not others:
        return x
    return lax.optimization_barrier((x, *others))[0]


def ring_order(chips):
    if chips % 2:
        return list(range(chips))
    return list(range(0, chips, 2)) + list(range(chips - 1, 0, -2))


def ring_place(chips, chip):
    if chips % 2:
        return chip
    up = lax.div(chip, jnp.int32(2))
    return jnp.where(lax.rem(chip, jnp.int32(2)) == 0, up, chips - 1 - up)


def chip_at(chips, place):
    if chips % 2:
        return place
    return jnp.where(place < chips // 2, 2 * place, 2 * (chips - 1 - place) + 1)


def this_core():
    return lax.rem(lax.axis_index("fsdp"), jnp.int32(2))


class Ring:
    def __init__(self, devices):
        self.chips = devices // 2
        order = ring_order(self.chips)
        n = self.chips
        self.to_right = [
            (2 * order[p] + k, 2 * order[(p + 1) % n] + k) for p in range(n) for k in (0, 1)
        ]
        self.to_left = [(b, a) for a, b in self.to_right]
        self.pair = [(i, i ^ 1) for i in range(devices)]

    def swap(self, x):
        return lax.ppermute(x, "fsdp", self.pair)

    def rounds(self):
        n = self.chips
        short = (n - 1) // 2
        rounds = []
        for s in range(1, n // 2 + 1):
            if s <= n - 1 - short:
                rounds.append([(0, 0, s), (1, 1, s)])
            if s <= short:
                rounds.append([(1, 0, s), (0, 1, s)])
        return rounds

    def move(self, x, direction):
        return lax.ppermute(x, "fsdp", self.to_left if direction else self.to_right)

    def gather(self, halves, beside):
        n = self.chips
        slots = [[x] + [None] * (n - 1) for x in halves]
        arrived = []
        for i, pair in enumerate(self.rounds()):
            ready = beside[i](arrived[i - 3]) if i >= 3 and i in beside else []
            for h, d, s in pair:
                x = after(slots[h][s - 1 if d else (1 - s) % n], *ready)
                slots[h][s if d else n - s] = self.move(x, d)
                ready = []
            arrived.append(slots[pair[0][0]][n - pair[0][2]])
        return slots

    def scatter_sum(self, slots):
        n = self.chips
        moving = {}
        for pair in sorted(self.rounds(), key=lambda pair: -pair[0][2]):
            for h, d, s in pair:
                term = slots[h][n - s if d else s]
                if (h, d) in moving:
                    term = add_low(moving[h, d], term)
                moving[h, d] = self.move(term, d)
        return [
            [slots[h][0]] + [moving[h, d] for d in range(2) if (h, d) in moving]
            for h in range(len(slots))
        ]


def add_kernel(a, b, out):
    out[...] = (a[...].astype(f32) + b[...].astype(f32)).astype(bf16)


def add_low(a, b):
    return pl.pallas_call(
        add_kernel,
        in_specs=[WHOLE, WHOLE],
        out_specs=WHOLE,
        out_shape=in_vmem(a),
        compiler_params=PARAMS,
        cost_estimate=pl.CostEstimate(flops=a.size, bytes_accessed=6 * a.size, transcendentals=0),
        name="add",
    )(vmem(a), vmem(b))


def whole_call(kernel, name, operands, outs, scratch=(), scalars=(), raw=(), cost=(0, 0)):
    return pl.pallas_call(
        kernel,
        in_specs=[SCALARS] * len(scalars)
        + [pl.BlockSpec(memory_space=pl.ANY)] * len(raw)
        + [WHOLE] * len(operands),
        out_specs=[WHOLE] * len(outs),
        out_shape=[in_vmem(x) for x in outs],
        scratch_shapes=list(scratch),
        compiler_params=PARAMS,
        cost_estimate=pl.CostEstimate(flops=cost[0], bytes_accessed=cost[1], transcendentals=0),
        name=name,
    )(
        *scalars,
        *[pltpu.with_memory_space_constraint(x, pltpu.HBM) for x in raw],
        *[vmem(x) for x in operands],
    )


def by_core(body):
    core = this_core()
    for c in range(2):
        pl.when(core == c)(partial(body, c))


def columns_loop(columns, column):
    lax.fori_loop(0, columns, lambda c, _: column(c) or 0, 0, unroll=2 if columns % 2 == 0 else 1)


def halves_of(mine, theirs, core):
    return jnp.concatenate([theirs, mine] if core else [mine, theirs], axis=-2)


def rows_of(x, core):
    rows = x.shape[-2] // 2
    low, high = x[..., :rows, :], x[..., rows:, :]
    return (high, low) if core else (low, high)


def shapes_of(shard):
    half_cols, per_col, rows_in, block = shard
    rows = jax.ShapeDtypeStruct((2 * half_cols, per_col, rows_in // 2, block), f32)
    return rows, jax.ShapeDtypeStruct(shard, bf16)


def merge_kernel(mine, theirs, low_a, low_b):
    half_cols = low_a.shape[0]

    def body(core):
        for h, out in enumerate((low_a, low_b)):

            def column(c, h=h, out=out):
                at = h * half_cols + c
                out[c] = halves_of(mine[at], theirs[at], core).astype(bf16)

            columns_loop(half_cols, column)

    by_core(body)


def merge(mine, theirs, shard):
    low = shapes_of(shard)[1]
    return whole_call(merge_kernel, "merge", [mine, theirs], [low, low], cost=(0, mine.size * 12))


def gathered_sum(parts, c):
    return sum(part[c].astype(f32) for part in parts)


def update_kernel(count, scaling, *refs):
    parts = refs[:count], refs[count : 2 * count]
    moments, weights = refs[2 * count : 2 * count + 2], refs[2 * count + 2 : 2 * count + 4]
    far = refs[2 * count + 4 : 2 * count + 9]
    near, sems = refs[2 * count + 9 : 2 * count + 14], refs[-1]
    moments_out, weights_out, low = near[:2], near[2:4], near[4]
    half_cols = low.shape[0] // 2

    def body(core):
        for h in range(2):

            def column(c, h=h):
                at = h * half_cols + c
                news = []
                for r, gradient in enumerate(rows_of(gathered_sum(parts[h], c), core)):
                    moment = momentum_beta * moments[r][at] + scaling * gradient
                    moments_out[r][at] = moment
                    news.append(decay_keep * weights[r][at] - learn_rate * moment)
                    weights_out[r][at] = news[r]
                low[at] = halves_of(*news, core).astype(bf16)

            columns_loop(half_cols, column)

    by_core(body)
    copies = [pltpu.make_async_copy(near[i], far[i], sems.at[i]) for i in range(5)]
    for copy in copies:
        copy.start()
    for copy in copies:
        copy.wait()


def update(parts, moments, weights, scaling, shard):
    rows = shapes_of(shard)[0]
    low = jax.ShapeDtypeStruct((2 * shard[0], *shard[1:]), bf16)
    outs = [rows] * 4 + [low]
    operands = [*parts[0], *parts[1], *moments, *weights]
    out = pl.pallas_call(
        partial(update_kernel, len(parts[0]), scaling),
        in_specs=[WHOLE] * len(operands),
        out_specs=[pl.BlockSpec(memory_space=pl.ANY)] * 5,
        out_shape=[pltpu.HBM(x.shape, x.dtype) for x in outs],
        scratch_shapes=[pltpu.VMEM(x.shape, x.dtype) for x in outs]
        + [pltpu.SemaphoreType.DMA((5,))],
        compiler_params=PARAMS,
        cost_estimate=pl.CostEstimate(
            flops=rows.size * 20, bytes_accessed=rows.size * 60, transcendentals=0
        ),
        name="update",
    )(*[vmem(x) for x in operands])
    return out[:2], out[2:4], out[4]


def blend_kernel(keep, *refs):
    far, outs, (low_a, low_b) = refs[:3], refs[3:5], refs[5:7]
    near, sems = refs[7:10], refs[10]
    mine, theirs, part = near
    half_cols = low_a.shape[0]
    share = keep[0]
    copies = [pltpu.make_async_copy(far[i], near[i], sems.at[i]) for i in range(3)]
    for copy in copies:
        copy.start()
    for copy in copies:
        copy.wait()

    def body(core):
        for h, low in enumerate((low_a, low_b)):

            def column(c, h=h, low=low):
                at = h * half_cols + c
                news = []
                for own, to, other in zip(
                    (mine, theirs), outs, rows_of(part[at].astype(f32), core)
                ):
                    news.append(share * own[at] + (1.0 - share) * other)
                    to[at] = news[-1]
                low[c] = halves_of(*news, core).astype(bf16)

            columns_loop(half_cols, column)

    by_core(body)


def blend(keep, weights, partner, shard):
    rows, low = shapes_of(shard)
    outs = [rows, rows, low, low]
    raw = pl.BlockSpec(memory_space=pl.ANY)
    out = pl.pallas_call(
        blend_kernel,
        in_specs=[SCALARS] + [raw] * 3,
        out_specs=[WHOLE] * 4,
        out_shape=[in_vmem(x) for x in outs],
        scratch_shapes=[
            pltpu.VMEM(rows.shape, f32),
            pltpu.VMEM(rows.shape, f32),
            pltpu.VMEM(partner.shape, bf16),
            pltpu.SemaphoreType.DMA((3,)),
        ],
        compiler_params=PARAMS,
        cost_estimate=pl.CostEstimate(
            flops=rows.size * 6, bytes_accessed=rows.size * 24, transcendentals=0
        ),
        name="blend",
    )(keep, *[pltpu.with_memory_space_constraint(x, pltpu.HBM) for x in (*weights, partner)])
    return out[:2], list(out[2:])


def last_sum_kernel(count, *refs):
    parts = refs[:count], refs[count : 2 * count]
    outs = refs[2 * count :]
    half_cols = parts[0][0].shape[0]

    def body(core):
        for h in range(2):

            def column(c, h=h):
                for out, rows in zip(outs, rows_of(gathered_sum(parts[h], c), core)):
                    out[h * half_cols + c] = rows

            columns_loop(half_cols, column)

    by_core(body)


def last_sum(parts, shard):
    rows = shapes_of(shard)[0]
    return whole_call(
        partial(last_sum_kernel, len(parts[0])),
        "last_sum",
        [*parts[0], *parts[1]],
        [rows, rows],
        cost=(rows.size * 4, rows.size * 20),
    )


def finish_kernel(scaling, *refs):
    gradients, moments, weights = refs[:2], refs[2:4], refs[4:6]
    outs, near, sems = refs[6:8], refs[8:10], refs[10]
    columns, per_col, rows = gradients[0].shape[:3]
    core = this_core()
    copies = []
    for k in range(per_col):

        def column(c, k=k):
            for side, owner in enumerate((core, 1 - core)):
                at = pl.ds(owner * columns + c, rows, stride=2 * columns)
                moment = momentum_beta * moments[side][c, k] + scaling * gradients[side][c, k]
                near[0][k, at, :] = decay_keep * weights[side][c, k] - learn_rate * moment
                near[1][k, at, :] = moment

        columns_loop(columns, column)
        for i in range(2):
            for r in range(rows):
                rows_of_k = near[i].at[k, pl.ds(r * 2 * columns, 2 * columns)]
                copy = pltpu.make_async_copy(rows_of_k, outs[i].at[r, k], sems.at[i, k])
                copy.start()
                copies.append(copy)
    for copy in copies:
        copy.wait()


def finish(gradients, moments, weights, scaling):
    columns, per_col, rows, block = gradients[0].shape
    operands = [*gradients, *moments, *weights]
    out = pltpu.HBM((rows, per_col, 2 * columns, block), f32)
    weight, moment = pl.pallas_call(
        partial(finish_kernel, scaling),
        in_specs=[WHOLE] * len(operands),
        out_specs=[pl.BlockSpec(memory_space=pl.ANY)] * 2,
        out_shape=[out, out],
        scratch_shapes=[pltpu.VMEM((per_col, rows * 2 * columns, block), f32)] * 2
        + [pltpu.SemaphoreType.DMA((2, per_col))],
        compiler_params=PARAMS,
        cost_estimate=pl.CostEstimate(
            flops=12 * gradients[0].size, bytes_accessed=80 * gradients[0].size, transcendentals=0
        ),
        name="finish",
    )(*[vmem(x) for x in operands])
    return [x.transpose(0, 2, 1, 3) for x in (weight, moment)]


def split_kernel(out_blocks, raw, kept, given, x, sem):
    columns, per_col, rows = kept.shape[:3]
    core = this_core()
    copy = pltpu.make_async_copy(raw, x, sem)
    copy.start()
    copy.wait()

    def column(c):
        for k in range(per_col):
            for out, owner in ((given, 1 - core), (kept, core)):
                start = k * out_blocks + owner * columns + c
                out[c, k] = x[pl.ds(start, rows, stride=per_col * out_blocks), :]

    columns_loop(columns, column)


def split(x):
    rows, out_blocks, per_col, block = x.shape
    flat = x.transpose(0, 2, 1, 3).reshape(-1, block)
    half = jax.ShapeDtypeStruct((out_blocks // 2, per_col, rows, block), f32)
    return whole_call(
        partial(split_kernel, out_blocks),
        "split",
        [],
        [half, half],
        scratch=[pltpu.VMEM(flat.shape, f32), pltpu.SemaphoreType.DMA(())],
        raw=[flat],
        cost=(0, 8 * x.size),
    )


def row_cuts(rows):
    if rows % 16:
        return [pl.ds(0, rows)]
    tiles = rows // 16
    pieces = min(4, tiles)
    edges = [16 * (tiles * i // pieces) for i in range(pieces + 1)]
    return [pl.ds(a, b - a) for a, b in zip(edges, edges[1:])]


def pick_kernel(s, mine, raws, outs, sems):
    core = this_core()
    half = core if mine else 1 - core
    copies = []
    _, rows, wide = outs.shape
    for i, raw in enumerate(raws):
        lanes = pl.ds(0, wide)
        if raw.shape[3] != wide:
            lanes = pl.ds(pl.multiple_of(half * wide, wide), wide)
        for j, cut in enumerate(row_cuts(rows)):
            copies.append(
                pltpu.make_async_copy(raw.at[0, s, cut, lanes], outs.at[i, cut], sems.at[i, j])
            )
    for copy in copies:
        copy.start()
    for copy in copies:
        copy.wait()


def pick(s, mine, wide, *raws):
    rows = raws[0].shape[2]
    count = len(raws)

    def kernel(*refs):
        pick_kernel(s, mine, refs[:count], refs[count], refs[count + 1])

    (out,) = whole_call(
        kernel,
        "pick",
        [],
        [jax.ShapeDtypeStruct((count, rows, wide), bf16)],
        scratch=[pltpu.SemaphoreType.DMA((count, len(row_cuts(rows))))],
        raw=raws,
        cost=(0, 4 * count * rows * wide),
    )
    return out


def turn_kernel(n, scal, own, sib, out, turned):
    in_blocks, block, room = out.shape
    rows = own.shape[1]
    rest = jnp.zeros((room - 2 * rows, block), bf16)
    piece = block // n

    def one(p, carry):
        lane = pl.ds(pl.multiple_of(p * block, block), block)
        x = jnp.concatenate([own[0, :, lane], sib[0, :, lane], rest], axis=0)
        turned[p % 2] = x.T.reshape(n, piece, room)
        for r in range(n):
            out[p, r * piece : (r + 1) * piece] = turned[p % 2, scal[r]]
        return carry

    lax.fori_loop(0, in_blocks, one, 0, unroll=2 if in_blocks % 2 == 0 else 1)


def turn(scal, own, sib, block, n):
    _, rows, features = own.shape
    room = -(-2 * rows // block) * block
    (out,) = whole_call(
        partial(turn_kernel, n),
        "turn",
        [own, sib],
        [jax.ShapeDtypeStruct((features // block, block, room), bf16)],
        scratch=[pltpu.VMEM((2, n, block // n, room), bf16)],
        scalars=[scal],
        cost=(0, 8 * rows * features),
    )
    return out


def forward_kernel(per_col, scaling, n, scal, given, kept, sib, *refs):
    slots = refs[:n], refs[n : 2 * n]
    gain, pre, stats, weight, sums = refs[2 * n :]
    half_cols, _, rows_in, block = slots[0][0].shape
    depth = n * rows_in
    cols = weight.shape[1]
    sums[...] = jnp.zeros_like(sums)
    base = scal[n + 2 * half_cols * per_col]

    for h in range(2):

        def group(i, carry, h=h):
            for r in range(n):
                weight[scal[r]] = slots[h][r][pl.ds(i * cols, cols)]
            for j in range(cols):
                c = h * half_cols + i * cols + j
                lanes = [
                    pl.ds(pl.multiple_of(scal[n + c * per_col + k] * block, block), block)
                    for k in range(per_col)
                ]
                w = jnp.concatenate(
                    [weight[:, j, k].reshape(depth, block) for k in range(per_col)], axis=0
                )
                cut = pl.ds(pl.multiple_of(c * block, block), block)
                sides = ((given, kept, 0), (sib, sib, 1))
                x = jnp.concatenate(
                    [
                        jnp.concatenate([act[0, :, lane] for lane in lanes], axis=1)
                        for act, _, _ in sides
                    ],
                    axis=0,
                )
                proj = scaling * jnp.dot(x, w, preferred_element_type=f32)
                rows = pre.shape[1]
                for t, (_, beside, at) in enumerate(sides):
                    value = beside[at, :, cut].astype(f32) + proj[t * rows : (t + 1) * rows]
                    pre[t, :, cut] = value
                    g = gain[base + c] * beside[at + 1, :, cut].astype(f32)
                    sums[t, 0] += value * value
                    sums[t, 1] += value * g
            return carry

        lax.fori_loop(0, half_cols // cols, group, 0)

    lane = lax.broadcasted_iota(jnp.int32, stats.shape[1:], 1)
    for t in range(2):
        square = jnp.sum(sums[t, 0], axis=1, keepdims=True)
        inner = jnp.sum(sums[t, 1], axis=1, keepdims=True)
        stats[t] = jnp.where(lane < block // 2, square, inner)


def interleaved(main, side):
    done = 0
    for i, step in enumerate(main):
        step()
        upto = len(side) * (i + 1) // len(main)
        for other in side[done:upto]:
            other()
        done = upto


def backward_kernel(per_col, width, n, scal, act_t, pre, kept, sib, gain, own, other, *refs):
    outs = refs[:n], refs[n : 2 * n]
    scales, grad = refs[2 * n :]
    half_cols, _, rows_in, block = outs[0][0].shape
    rows = pre.shape[1]
    cols = grad.shape[1]
    groups = half_cols // cols
    size = 16 if rows % 16 == 0 else rows
    base = scal[n + 2 * half_cols * per_col]

    for t in range(2):
        total = own[t] + other[1 - t]
        square, inner = total[:, 0:1], total[:, block // 2 : block // 2 + 1]
        inv = lax.rsqrt(square / width + epsilon)
        scales[t, 0] = jnp.broadcast_to(inv, scales.shape[2:])
        scales[t, 1] = jnp.broadcast_to(inv * inv * inv * (inner / width), scales.shape[2:])
    for b in range(2):
        grad[b, :, 2 * rows :] = jnp.zeros((cols, grad.shape[2] - 2 * rows, block), bf16)

    def gradients(g, t, at):
        up = sib.at[2] if t else kept.at[1]
        chunk = slice(at, at + size)
        inv, inner = scales[t, 0, chunk], scales[t, 1, chunk]
        for j in range(cols):
            c = g * cols + j
            cut = slice(c * block, (c + 1) * block)
            weighted = gain[base + c] * up[chunk, cut].astype(f32)
            to = slice(t * rows + at, t * rows + at + size)
            grad[g % 2, j, to] = (inv * weighted - pre[t, chunk, cut] * inner).astype(bf16)

    def all_gradients(g):
        if g >= 2 * groups:
            return []
        return [partial(gradients, g, t, at) for t in range(2) for at in range(0, rows, size)]

    def product(g, j):
        at = n + (g * cols + j) * per_col
        x = jnp.concatenate([act_t[scal[at + k]] for k in range(per_col)], axis=0)
        term = jnp.dot(x, grad[g % 2, j], preferred_element_type=f32).astype(bf16)
        term = term.reshape(per_col, n, rows_in, block)
        for r in range(n):
            outs[g // groups][r][g % groups * cols + j] = term[:, r]

    for step in all_gradients(0):
        step()
    for g in range(2 * groups):
        interleaved([partial(product, g, j) for j in range(cols)], all_gradients(g + 1))


def group_columns(half_cols):
    return max(c for c in range(1, 6) if half_cols % c == 0)


def forward(scal, given, kept, sib, slots, gain, scaling):
    n = len(slots[0])
    half_cols, per_col, rows_in, block = slots[0][0].shape
    _, rows, wide = kept.shape
    cols = group_columns(half_cols)
    flops = 4 * rows * wide * per_col * block
    operands = [given, kept, sib, *slots[0], *slots[1], gain]
    return pl.pallas_call(
        partial(forward_kernel, per_col, scaling, n),
        in_specs=[SCALARS] + [WHOLE] * len(operands),
        out_specs=[WHOLE, WHOLE],
        out_shape=[
            in_vmem(jax.ShapeDtypeStruct((2, rows, wide), f32)),
            in_vmem(jax.ShapeDtypeStruct((2, rows, block), f32)),
        ],
        scratch_shapes=[
            pltpu.VMEM((n, cols, per_col, rows_in, block), bf16),
            pltpu.VMEM((2, 2, rows, block), f32),
        ],
        compiler_params=PARAMS,
        cost_estimate=pl.CostEstimate(flops=flops, bytes_accessed=16 * 2**20, transcendentals=0),
        name="forward",
    )(scal, *[vmem(x) for x in operands])


def backward(scal, act_t, pre, kept, sib, gain, own, other, shard, width):
    half_cols, per_col, rows_in, block = shard
    n = block // rows_in
    _, rows, wide = kept.shape
    room = act_t.shape[2]
    cols = group_columns(half_cols)
    flops = 4 * rows * wide * per_col * block
    operands = [act_t, pre, kept, sib, gain, own, other]
    out = pl.pallas_call(
        partial(backward_kernel, per_col, width, n),
        in_specs=[SCALARS] + [WHOLE] * len(operands),
        out_specs=[WHOLE] * (2 * n),
        out_shape=[in_vmem(jax.ShapeDtypeStruct(shard, bf16)) for _ in range(2 * n)],
        scratch_shapes=[
            pltpu.VMEM((2, 2, rows, block), f32),
            pltpu.VMEM((2, cols, room, block), bf16),
        ],
        compiler_params=PARAMS,
        cost_estimate=pl.CostEstimate(flops=flops, bytes_accessed=16 * 2**20, transcendentals=0),
        name="backward",
    )(scal, *[vmem(x) for x in operands])
    return [out[:n], out[n:]]


def gossip_hops():
    devices = lax.axis_size("rep")
    hops = {}
    for entry, stride in enumerate((1, 2, 4)):
        if stride % devices:
            hops.setdefault(stride % devices, []).append(entry)
    return hops


def partner_of(taken, low):
    devices = lax.axis_size("rep")
    partner = None
    for hop, chosen in taken.items():
        shift = [(i, (i + hop) % devices) for i in range(devices)]
        moved = lambda x, last, shift=shift: lax.ppermute(x, "rep", shift)
        if partner is None:
            partner = lax.cond(chosen, moved, lambda x, last: jnp.zeros_like(x), low, 0)
        else:
            partner = lax.cond(chosen, moved, lambda x, last: last, low, partner)
    return low if partner is None else partner


def mixed(taken, weight):
    devices = lax.axis_size("rep")
    for hop, chosen in taken.items():
        shift = [(i, (i + hop) % devices) for i in range(devices)]

        def mean(own, shift=shift):
            return 0.5 * (own + lax.ppermute(own.astype(bf16), "rep", shift).astype(f32))

        weight = lax.cond(chosen, mean, lambda own: own, weight)
    return weight


def body(activations, residual, upstream, norm_gain, params, momentum, pattern, step_index):
    steps, rows, features = activations.shape[1:]
    width = residual.shape[3]
    own_rows, out_blocks, per_col, block = params.shape[1:]
    scaling = 1.0 / math.sqrt(per_col * block)
    ring = Ring(lax.axis_size("fsdp"))
    n = ring.chips
    columns = out_blocks // 2
    half_cols = columns // 2

    core = this_core()
    place = ring_place(n, lax.div(lax.axis_index("fsdp"), jnp.int32(2)))
    places = place + jnp.arange(n, dtype=jnp.int32)
    chips = chip_at(n, jnp.where(places < n, places, places - n))
    used = lax.dynamic_slice_in_dim(pattern, core * columns, columns, 0)
    scal = jnp.concatenate([chips, used.reshape(-1), core[None] * columns]).astype(jnp.int32)
    gain = norm_gain.reshape(out_blocks, 1, block)

    taken, keeps = [], []
    hops = gossip_hops()
    for s in range(steps):
        entry = lax.rem(step_index[0] + s, jnp.int32(3))
        chosen = {hop: [entry == e for e in entries] for hop, entries in hops.items()}
        taken.append({hop: functools.reduce(jnp.logical_or, flags) for hop, flags in chosen.items()})
        moved = functools.reduce(jnp.logical_or, taken[s].values(), jnp.bool_(False))
        keeps.append(jnp.where(moved, 0.5, 1.0).astype(f32).reshape(1))

    shard = (half_cols, per_col, 2 * own_rows, block)
    mine, theirs = split(params[0])
    theirs = ring.swap(theirs)
    weights = [mine, theirs]
    scal, gain, taken, keeps = lax.optimization_barrier((scal, gain, taken, keeps))
    tokens = (activations, residual, upstream)

    def picked(s, mine, arrived):
        arrays = tokens[1:] if mine else tokens
        return pick(s, mine, features, *[after(x, arrived) for x in arrays])

    given = picked(0, False, scal)
    halves = list(merge(*weights, shard))
    halves[0] = after(halves[0], scal)
    sib = ring.swap(after(given, theirs))
    state = {}

    def keep(name, make):
        def work(arrived):
            state[name] = make(arrived)
            return jax.tree.leaves(state[name])

        return work

    for s in range(steps):
        last = s == steps - 1
        beside = {}
        if s == 0:
            beside[3] = keep("moments", lambda arrived: split(after(momentum, arrived)[0]))
        beside[4] = keep("kept", lambda arrived: picked(s, True, arrived))
        if not last:
            beside[5] = keep("later", lambda arrived: picked(s + 1, False, arrived))
        slots = ring.gather(halves, beside)
        for i, work in beside.items():
            if i >= len(ring.rounds()):
                work(halves[0])
        kept = state["kept"]
        act_t = turn(scal, given, sib, block, n)
        pre, own = forward(scal, given, kept, sib, slots, after(gain, act_t), scaling)
        other = ring.swap(own)
        terms = backward(scal, act_t, pre, kept, sib, gain, own, other, shard, float(width))
        ready = []
        if not last:
            given = state["later"]
            sib = ring.swap(after(given, other))
        if s == 0:
            moments = state["moments"]
            moments = [moments[0], ring.swap(after(moments[1], other))]
        if last:
            moments = [moments[0], ring.swap(after(moments[1], other))]
            weights = [weights[0], ring.swap(after(weights[1], other))]
            ready += [moments[1], weights[1]]
        far = n // 2
        terms = [list(t) for t in terms]
        terms[0][far], terms[1][n - far] = lax.optimization_barrier(
            (terms[0][far], terms[1][n - far], *ready)
        )[:2]
        if not last:
            third = max(far - 1, 1)
            terms[0][third] = after(terms[0][third], sib, moments[1])
        parts = ring.scatter_sum(terms)
        if not last:
            moments, weights, low = update(parts, moments, weights, scaling, shard)
            partner = partner_of(after(taken[s], low), low)
            weights, halves = blend(keeps[s], weights, partner, shard)
    mine, theirs = last_sum(parts, shard)
    weight, moment = finish([mine, ring.swap(theirs)], moments, weights, scaling)
    return (mixed(after(taken[-1], weight), weight)[None], moment[None])


def solution(mesh):
    in_specs = (
        P("rep", None, "fsdp", None),
        P("rep", None, "fsdp", None),
        P("rep", None, "fsdp", None),
        P(),
        P("rep", "fsdp", None, None, None),
        P("rep", "fsdp", None, None, None),
        P(),
        P(),
    )
    out_specs = (P("rep", "fsdp", None, None, None), P("rep", "fsdp", None, None, None))
    return jax.shard_map(body, mesh=mesh, in_specs=in_specs, out_specs=out_specs, check_vma=False)
```

```python
import functools
import math
from functools import partial

import jax
import jax.numpy as jnp
import numpy as np
from jax import lax
from jax.experimental import pallas as pl
from jax.experimental.pallas import tpu as pltpu
from jax.sharding import PartitionSpec as P

learn_rate = 0.1
momentum_beta = 0.9
decay_keep = 0.999
epsilon = 1e-06

f32 = jnp.float32
bf16 = jnp.bfloat16
WHOLE = pl.BlockSpec(memory_space=pltpu.VMEM)
SCALARS = pl.BlockSpec(memory_space=pltpu.SMEM)
PARAMS = pltpu.CompilerParams(vmem_limit_bytes=16 * 2**20)


def vmem(x):
    return pltpu.with_memory_space_constraint(x, pltpu.VMEM)


def in_vmem(shape):
    return pltpu.VMEM(shape.shape, shape.dtype)


def after(x, *others):
    if not others:
        return x
    return lax.optimization_barrier((x, *others))[0]


def ring_order(chips):
    if chips % 2:
        return list(range(chips))
    return list(range(0, chips, 2)) + list(range(chips - 1, 0, -2))


def ring_place(chips, chip):
    if chips % 2:
        return chip
    up = lax.div(chip, jnp.int32(2))
    return jnp.where(lax.rem(chip, jnp.int32(2)) == 0, up, chips - 1 - up)


def chip_at(chips, place):
    if chips % 2:
        return place
    return jnp.where(place < chips // 2, 2 * place, 2 * (chips - 1 - place) + 1)


def this_core():
    return lax.rem(lax.axis_index("fsdp"), jnp.int32(2))


class Ring:
    def __init__(self, devices):
        self.chips = devices // 2
        order = ring_order(self.chips)
        n = self.chips
        self.to_right = [
            (2 * order[p] + k, 2 * order[(p + 1) % n] + k) for p in range(n) for k in (0, 1)
        ]
        self.to_left = [(b, a) for a, b in self.to_right]
        self.pair = [(i, i ^ 1) for i in range(devices)]

    def swap(self, x):
        return lax.ppermute(x, "fsdp", self.pair)

    def rounds(self):
        n = self.chips
        short = (n - 1) // 2
        rounds = []
        for s in range(1, n // 2 + 1):
            if s <= n - 1 - short:
                rounds.append([(0, 0, s), (1, 1, s)])
            if s <= short:
                rounds.append([(1, 0, s), (0, 1, s)])
        return rounds

    def move(self, x, direction):
        return lax.ppermute(x, "fsdp", self.to_left if direction else self.to_right)

    def gather(self, halves, beside):
        n = self.chips
        slots = [[x] + [None] * (n - 1) for x in halves]
        arrived = []
        for i, pair in enumerate(self.rounds()):
            ready = beside[i](arrived[i - 3] if i >= 3 else halves[0]) if i in beside else []
            for h, d, s in pair:
                x = after(slots[h][s - 1 if d else (1 - s) % n], *ready)
                slots[h][s if d else n - s] = self.move(x, d)
                ready = []
            arrived.append(slots[pair[0][0]][n - pair[0][2]])
        return slots

    def scatter_sum(self, slots):
        n = self.chips
        moving = {}
        for pair in sorted(self.rounds(), key=lambda pair: -pair[0][2]):
            for h, d, s in pair:
                term = slots[h][n - s if d else s]
                if (h, d) in moving:
                    term = add_low(moving[h, d], term)
                moving[h, d] = self.move(term, d)
        return [
            [slots[h][0]] + [moving[h, d] for d in range(2) if (h, d) in moving]
            for h in range(len(slots))
        ]


def add_kernel(a, b, out):
    out[...] = (a[...].astype(f32) + b[...].astype(f32)).astype(bf16)


def add_low(a, b):
    return pl.pallas_call(
        add_kernel,
        in_specs=[WHOLE, WHOLE],
        out_specs=WHOLE,
        out_shape=in_vmem(a),
        compiler_params=PARAMS,
        cost_estimate=pl.CostEstimate(flops=a.size, bytes_accessed=6 * a.size, transcendentals=0),
        name="add",
    )(vmem(a), vmem(b))


def whole_call(kernel, name, operands, outs, scratch=(), scalars=(), raw=(), cost=(0, 0)):
    return pl.pallas_call(
        kernel,
        in_specs=[SCALARS] * len(scalars)
        + [pl.BlockSpec(memory_space=pl.ANY)] * len(raw)
        + [WHOLE] * len(operands),
        out_specs=[WHOLE] * len(outs),
        out_shape=[in_vmem(x) for x in outs],
        scratch_shapes=list(scratch),
        compiler_params=PARAMS,
        cost_estimate=pl.CostEstimate(flops=cost[0], bytes_accessed=cost[1], transcendentals=0),
        name=name,
    )(
        *scalars,
        *[pltpu.with_memory_space_constraint(x, pltpu.HBM) for x in raw],
        *[vmem(x) for x in operands],
    )


def by_core(body):
    core = this_core()
    for c in range(2):
        pl.when(core == c)(partial(body, c))


def columns_loop(columns, column):
    lax.fori_loop(0, columns, lambda c, _: column(c) or 0, 0, unroll=2 if columns % 2 == 0 else 1)


def halves_of(mine, theirs, core):
    return jnp.concatenate([theirs, mine] if core else [mine, theirs], axis=-2)


def rows_of(x, core):
    rows = x.shape[-2] // 2
    low, high = x[..., :rows, :], x[..., rows:, :]
    return (high, low) if core else (low, high)


def shapes_of(shard):
    half_cols, per_col, rows_in, block = shard
    rows = jax.ShapeDtypeStruct((2 * half_cols, per_col, rows_in // 2, block), f32)
    return rows, jax.ShapeDtypeStruct(shard, bf16)


def merge_kernel(mine, theirs, low_a, low_b):
    half_cols = low_a.shape[0]

    def body(core):
        for h, out in enumerate((low_a, low_b)):

            def column(c, h=h, out=out):
                at = h * half_cols + c
                out[c] = halves_of(mine[at], theirs[at], core).astype(bf16)

            columns_loop(half_cols, column)

    by_core(body)


def merge(mine, theirs, shard):
    low = shapes_of(shard)[1]
    return whole_call(merge_kernel, "merge", [mine, theirs], [low, low], cost=(0, mine.size * 12))


def gathered_sum(parts, c):
    return sum(part[c].astype(f32) for part in parts)


def update_kernel(count, scaling, *refs):
    parts = refs[:count], refs[count : 2 * count]
    moments, weights = refs[2 * count : 2 * count + 2], refs[2 * count + 2 : 2 * count + 4]
    far = refs[2 * count + 4 : 2 * count + 9]
    near, sems = refs[2 * count + 9 : 2 * count + 14], refs[-1]
    moments_out, weights_out, low = near[:2], near[2:4], near[4]
    half_cols = low.shape[0] // 2

    def body(core):
        for h in range(2):

            def column(c, h=h):
                at = h * half_cols + c
                news = []
                for r, gradient in enumerate(rows_of(gathered_sum(parts[h], c), core)):
                    moment = momentum_beta * moments[r][at] + scaling * gradient
                    moments_out[r][at] = moment
                    news.append(decay_keep * weights[r][at] - learn_rate * moment)
                    weights_out[r][at] = news[r]
                low[at] = halves_of(*news, core).astype(bf16)

            columns_loop(half_cols, column)

    by_core(body)
    copies = [pltpu.make_async_copy(near[i], far[i], sems.at[i]) for i in range(5)]
    for copy in copies:
        copy.start()
    for copy in copies:
        copy.wait()


def update(parts, moments, weights, scaling, shard):
    rows = shapes_of(shard)[0]
    low = jax.ShapeDtypeStruct((2 * shard[0], *shard[1:]), bf16)
    outs = [rows] * 4 + [low]
    operands = [*parts[0], *parts[1], *moments, *weights]
    out = pl.pallas_call(
        partial(update_kernel, len(parts[0]), scaling),
        in_specs=[WHOLE] * len(operands),
        out_specs=[pl.BlockSpec(memory_space=pl.ANY)] * 5,
        out_shape=[pltpu.HBM(x.shape, x.dtype) for x in outs],
        scratch_shapes=[pltpu.VMEM(x.shape, x.dtype) for x in outs]
        + [pltpu.SemaphoreType.DMA((5,))],
        compiler_params=PARAMS,
        cost_estimate=pl.CostEstimate(
            flops=rows.size * 20, bytes_accessed=rows.size * 60, transcendentals=0
        ),
        name="update",
    )(*[vmem(x) for x in operands])
    return out[:2], out[2:4], out[4]


def blend_kernel(keep, *refs):
    far, outs, (low_a, low_b) = refs[:3], refs[3:5], refs[5:7]
    near, sems = refs[7:10], refs[10]
    mine, theirs, part = near
    half_cols = low_a.shape[0]
    share = keep[0]
    copies = [pltpu.make_async_copy(far[i], near[i], sems.at[i]) for i in range(3)]
    for copy in copies:
        copy.start()
    for copy in copies:
        copy.wait()

    def body(core):
        for h, low in enumerate((low_a, low_b)):

            def column(c, h=h, low=low):
                at = h * half_cols + c
                news = []
                for own, to, other in zip(
                    (mine, theirs), outs, rows_of(part[at].astype(f32), core)
                ):
                    news.append(share * own[at] + (1.0 - share) * other)
                    to[at] = news[-1]
                low[c] = halves_of(*news, core).astype(bf16)

            columns_loop(half_cols, column)

    by_core(body)


def blend(keep, weights, partner, shard):
    rows, low = shapes_of(shard)
    outs = [rows, rows, low, low]
    raw = pl.BlockSpec(memory_space=pl.ANY)
    out = pl.pallas_call(
        blend_kernel,
        in_specs=[SCALARS] + [raw] * 3,
        out_specs=[WHOLE] * 4,
        out_shape=[in_vmem(x) for x in outs],
        scratch_shapes=[
            pltpu.VMEM(rows.shape, f32),
            pltpu.VMEM(rows.shape, f32),
            pltpu.VMEM(partner.shape, bf16),
            pltpu.SemaphoreType.DMA((3,)),
        ],
        compiler_params=PARAMS,
        cost_estimate=pl.CostEstimate(
            flops=rows.size * 6, bytes_accessed=rows.size * 24, transcendentals=0
        ),
        name="blend",
    )(keep, *[pltpu.with_memory_space_constraint(x, pltpu.HBM) for x in (*weights, partner)])
    return out[:2], list(out[2:])


def last_sum_kernel(count, *refs):
    parts = refs[:count], refs[count : 2 * count]
    outs = refs[2 * count :]
    half_cols = parts[0][0].shape[0]

    def body(core):
        for h in range(2):

            def column(c, h=h):
                for out, rows in zip(outs, rows_of(gathered_sum(parts[h], c), core)):
                    out[h * half_cols + c] = rows

            columns_loop(half_cols, column)

    by_core(body)


def last_sum(parts, shard):
    rows = shapes_of(shard)[0]
    return whole_call(
        partial(last_sum_kernel, len(parts[0])),
        "last_sum",
        [*parts[0], *parts[1]],
        [rows, rows],
        cost=(rows.size * 4, rows.size * 20),
    )


def finish_kernel(scaling, *refs):
    gradients, moments, weights = refs[:2], refs[2:4], refs[4:6]
    outs, near, sems = refs[6:8], refs[8:10], refs[10]
    columns, per_col, rows = gradients[0].shape[:3]
    core = this_core()
    copies = []
    for k in range(per_col):

        def column(c, k=k):
            for side, owner in enumerate((core, 1 - core)):
                at = pl.ds(owner * columns + c, rows, stride=2 * columns)
                moment = momentum_beta * moments[side][c, k] + scaling * gradients[side][c, k]
                near[0][k, at, :] = decay_keep * weights[side][c, k] - learn_rate * moment
                near[1][k, at, :] = moment

        columns_loop(columns, column)
        for i in range(2):
            for r in range(rows):
                rows_of_k = near[i].at[k, pl.ds(r * 2 * columns, 2 * columns)]
                copy = pltpu.make_async_copy(rows_of_k, outs[i].at[r, k], sems.at[i, k])
                copy.start()
                copies.append(copy)
    for copy in copies:
        copy.wait()


def finish(gradients, moments, weights, scaling):
    columns, per_col, rows, block = gradients[0].shape
    operands = [*gradients, *moments, *weights]
    out = pltpu.HBM((rows, per_col, 2 * columns, block), f32)
    weight, moment = pl.pallas_call(
        partial(finish_kernel, scaling),
        in_specs=[WHOLE] * len(operands),
        out_specs=[pl.BlockSpec(memory_space=pl.ANY)] * 2,
        out_shape=[out, out],
        scratch_shapes=[pltpu.VMEM((per_col, rows * 2 * columns, block), f32)] * 2
        + [pltpu.SemaphoreType.DMA((2, per_col))],
        compiler_params=PARAMS,
        cost_estimate=pl.CostEstimate(
            flops=12 * gradients[0].size, bytes_accessed=80 * gradients[0].size, transcendentals=0
        ),
        name="finish",
    )(*[vmem(x) for x in operands])
    return [x.transpose(0, 2, 1, 3) for x in (weight, moment)]


def split_kernel(out_blocks, raw, kept, given, x, sem):
    columns, per_col, rows = kept.shape[:3]
    core = this_core()
    copy = pltpu.make_async_copy(raw, x, sem)
    copy.start()
    copy.wait()

    def column(c):
        for k in range(per_col):
            for out, owner in ((given, 1 - core), (kept, core)):
                start = k * out_blocks + owner * columns + c
                out[c, k] = x[pl.ds(start, rows, stride=per_col * out_blocks), :]

    columns_loop(columns, column)


def split(x):
    rows, out_blocks, per_col, block = x.shape
    flat = x.transpose(0, 2, 1, 3).reshape(-1, block)
    half = jax.ShapeDtypeStruct((out_blocks // 2, per_col, rows, block), f32)
    return whole_call(
        partial(split_kernel, out_blocks),
        "split",
        [],
        [half, half],
        scratch=[pltpu.VMEM(flat.shape, f32), pltpu.SemaphoreType.DMA(())],
        raw=[flat],
        cost=(0, 8 * x.size),
    )


def row_cuts(rows):
    if rows % 16:
        return [pl.ds(0, rows)]
    tiles = rows // 16
    pieces = min(4, tiles)
    edges = [16 * (tiles * i // pieces) for i in range(pieces + 1)]
    return [pl.ds(a, b - a) for a, b in zip(edges, edges[1:])]


def pick_kernel(s, mine, raws, outs, sems):
    core = this_core()
    half = core if mine else 1 - core
    copies = []
    _, rows, wide = outs.shape
    for i, raw in enumerate(raws):
        lanes = pl.ds(0, wide)
        if raw.shape[3] != wide:
            lanes = pl.ds(pl.multiple_of(half * wide, wide), wide)
        for j, cut in enumerate(row_cuts(rows)):
            copies.append(
                pltpu.make_async_copy(raw.at[0, s, cut, lanes], outs.at[i, cut], sems.at[i, j])
            )
    for copy in copies:
        copy.start()
    for copy in copies:
        copy.wait()


def pick(s, mine, wide, *raws):
    rows = raws[0].shape[2]
    count = len(raws)

    def kernel(*refs):
        pick_kernel(s, mine, refs[:count], refs[count], refs[count + 1])

    (out,) = whole_call(
        kernel,
        "pick",
        [],
        [jax.ShapeDtypeStruct((count, rows, wide), bf16)],
        scratch=[pltpu.SemaphoreType.DMA((count, len(row_cuts(rows))))],
        raw=raws,
        cost=(0, 4 * count * rows * wide),
    )
    return out


def turn_kernel(n, scal, own, sib, out, turned):
    in_blocks, block, room = out.shape
    rows = own.shape[1]
    rest = jnp.zeros((room - 2 * rows, block), bf16)
    piece = block // n

    def one(p, carry):
        lane = pl.ds(pl.multiple_of(p * block, block), block)
        x = jnp.concatenate([own[0, :, lane], sib[0, :, lane], rest], axis=0)
        turned[p % 2] = x.T.reshape(n, piece, room)
        for r in range(n):
            out[p, r * piece : (r + 1) * piece] = turned[p % 2, scal[r]]
        return carry

    lax.fori_loop(0, in_blocks, one, 0, unroll=2 if in_blocks % 2 == 0 else 1)


def turn(scal, own, sib, block, n):
    _, rows, features = own.shape
    room = -(-2 * rows // block) * block
    (out,) = whole_call(
        partial(turn_kernel, n),
        "turn",
        [own, sib],
        [jax.ShapeDtypeStruct((features // block, block, room), bf16)],
        scratch=[pltpu.VMEM((2, n, block // n, room), bf16)],
        scalars=[scal],
        cost=(0, 8 * rows * features),
    )
    return out


def far_slots(n):
    return n // 2, n - n // 2


def features_of(act_t, scal, n, at, per_col, slots):
    piece = act_t.shape[1] // n
    runs = []
    for r in slots:
        if runs and runs[-1][1] == r * piece:
            runs[-1][1] += piece
        else:
            runs.append([r * piece, (r + 1) * piece])
    return jnp.concatenate(
        [act_t[scal[n + at * per_col + k], a:b] for k in range(per_col) for a, b in runs], axis=0
    )


def project(act_t, scal, n, at, weights, j):
    per_col = weights[min(weights)].shape[1]
    x = features_of(act_t, scal, n, at, per_col, sorted(weights))
    w = jnp.concatenate(
        [weights[r][j, k] for k in range(per_col) for r in sorted(weights)], axis=0
    )
    return lax.dot_general(x, w, (((0,), (0,)), ((), ())), preferred_element_type=f32)


def forward_kernel(scaling, n, scal, act_t, kept, sib, *refs):
    near = [[r for r in range(n) if r != f] for f in far_slots(n)]
    slots = [dict(zip(near[0], refs)), dict(zip(near[1], refs[n - 1 :]))]
    part = refs[-1]
    half_cols, _, _, block = refs[0].shape
    rows = part.shape[1]
    cols = group_columns(half_cols)

    for h in range(2):

        def group(i, carry, h=h):
            for j in range(cols):
                c = h * half_cols + i * cols + j
                cut = pl.ds(pl.multiple_of(c * block, block), block)
                out = scaling * project(act_t, scal, n, c, slots[h], i * cols + j)
                for t, res in enumerate((kept.at[0], sib.at[1])):
                    value = res[:, cut].astype(f32) + out[t * rows : (t + 1) * rows]
                    part[t, :, cut] = value
            return carry

        lax.fori_loop(0, half_cols // cols, group, 0)


def interleaved(main, side):
    done = 0
    for i, step in enumerate(main):
        step()
        upto = len(side) * (i + 1) // len(main)
        for other in side[done:upto]:
            other()
        done = upto


def norm_kernel(per_col, scaling, n, scal, act_t, part, kept, sib, gain, far_a, far_b, *refs):
    pre, stats, sums, share = refs
    half_cols, _, _, block = far_a.shape
    rows = pre.shape[1]
    cols = group_columns(half_cols)
    base = scal[n + 2 * half_cols * per_col]
    sums[...] = jnp.zeros_like(sums)

    size = 16 if rows % 16 == 0 else rows

    def product(c):
        h = c // half_cols
        f, far = far_slots(n)[h], (far_a, far_b)[h]
        share[c // cols % 2, c % cols] = project(act_t, scal, n, c, {f: far}, c % half_cols)

    def add_up(g, t, at):
        chunk = slice(at, at + size)
        square, inner = sums[t, 0, chunk], sums[t, 1, chunk]
        for j in range(cols):
            c = g * cols + j
            cut = slice(c * block, (c + 1) * block)
            own = share[g % 2, j, t * rows + at : t * rows + at + size]
            value = part[t, chunk, cut] + scaling * own
            pre[t, chunk, cut] = value
            up = (sib.at[2] if t else kept.at[1])[chunk, cut].astype(f32)
            square += value * value
            inner += value * (gain[base + c] * up)
        sums[t, 0, chunk], sums[t, 1, chunk] = square, inner

    groups = 2 * half_cols // cols
    for g in range(groups + 1):
        side = []
        if g > 0:
            side = [partial(add_up, g - 1, t, at) for t in range(2) for at in range(0, rows, size)]
        main = [partial(product, c) for c in range(g * cols, (g + 1) * cols) if g < groups]
        interleaved(main or [lambda: None], side)

    lane = lax.broadcasted_iota(jnp.int32, stats.shape[1:], 1)
    for t in range(2):
        square = jnp.sum(sums[t, 0], axis=1, keepdims=True)
        inner = jnp.sum(sums[t, 1], axis=1, keepdims=True)
        stats[t] = jnp.where(lane < block // 2, square, inner)


def backward_kernel(per_col, width, n, scal, act_t, pre, kept, sib, gain, own, other, *refs):
    outs, grad, scales = refs[:2], refs[2], refs[3]
    half_cols, _, rows_in, block = outs[0].shape
    rows = pre.shape[1]
    cols = group_columns(half_cols)
    size = 16 if rows % 16 == 0 else rows
    base = scal[n + 2 * half_cols * per_col]

    for t in range(2):
        total = own[t] + other[1 - t]
        square, inner = total[:, 0:1], total[:, block // 2 : block // 2 + 1]
        inv = lax.rsqrt(square / width + epsilon)
        scales[t, 0] = jnp.broadcast_to(inv, scales.shape[2:])
        scales[t, 1] = jnp.broadcast_to(inv * inv * inv * (inner / width), scales.shape[2:])
    grad[:, 2 * rows :] = jnp.zeros((2 * half_cols, grad.shape[1] - 2 * rows, block), bf16)

    def gradients(g, t, at):
        up = sib.at[2] if t else kept.at[1]
        chunk = slice(at, at + size)
        inv, inner = scales[t, 0, chunk], scales[t, 1, chunk]
        for c in range(g * cols, (g + 1) * cols):
            cut = slice(c * block, (c + 1) * block)
            weighted = gain[base + c] * up[chunk, cut].astype(f32)
            to = slice(t * rows + at, t * rows + at + size)
            grad[c, to] = (inv * weighted - pre[t, chunk, cut] * inner).astype(bf16)

    def product(c):
        h = c // half_cols
        x = features_of(act_t, scal, n, c, per_col, [far_slots(n)[h]])
        term = jnp.dot(x, grad[c], preferred_element_type=f32).astype(bf16)
        outs[h][c % half_cols] = term.reshape(per_col, rows_in, block)

    groups = 2 * half_cols // cols
    for g in range(groups + 1):
        side = []
        if g < groups:
            side = [partial(gradients, g, t, at) for t in range(2) for at in range(0, rows, size)]
        main = [partial(product, c) for c in range(max(g - 1, 0) * cols, g * cols)]
        interleaved(main or [lambda: None], side)


def terms_kernel(per_col, n, scal, act_t, grad, *outs):
    near = [[r for r in range(n) if r != f] for f in far_slots(n)]
    outs = [dict(zip(near[0], outs)), dict(zip(near[1], outs[n - 1 :]))]
    half_cols, _, rows_in, block = outs[0][near[0][0]].shape
    for c in range(2 * half_cols):
        h, at = c // half_cols, c % half_cols
        x = features_of(act_t, scal, n, c, per_col, range(n))
        term = jnp.dot(x, grad[c], preferred_element_type=f32)
        term = term.astype(bf16).reshape(per_col, n, rows_in, block)
        for r in near[h]:
            outs[h][r][at] = term[:, r]


def group_columns(half_cols):
    return max(c for c in range(1, 6) if half_cols % c == 0)


def forward(scal, act_t, kept, sib, slots, scaling):
    n = len(slots[0])
    half_cols, per_col, rows_in, block = slots[0][0].shape
    _, rows, wide = kept.shape
    near = [x for h, f in enumerate(far_slots(n)) for r, x in enumerate(slots[h]) if r != f]
    (part,) = whole_call(
        partial(forward_kernel, scaling, n),
        "forward",
        [act_t, kept, sib, *near],
        [jax.ShapeDtypeStruct((2, rows, wide), f32)],
        scalars=[scal],
        cost=(4 * rows * wide * per_col * block, 16 * 2**20),
    )
    return part


def norm(scal, act_t, part, kept, sib, gain, slots, scaling):
    n = len(slots[0])
    half_cols, per_col, rows_in, block = slots[0][0].shape
    _, rows, wide = part.shape
    far = [slots[h][f] for h, f in enumerate(far_slots(n))]
    return whole_call(
        partial(norm_kernel, per_col, scaling, n),
        "norm",
        [act_t, part, kept, sib, gain, *far],
        [jax.ShapeDtypeStruct(part.shape, f32), jax.ShapeDtypeStruct((2, rows, block), f32)],
        scratch=[
            pltpu.VMEM((2, 2, rows, block), f32),
            pltpu.VMEM((2, group_columns(half_cols), act_t.shape[2], block), f32),
        ],
        scalars=[scal],
        cost=(4 * rows * wide * per_col * rows_in, 16 * 2**20),
    )


def backward(scal, act_t, pre, kept, sib, gain, own, other, shard, width):
    half_cols, per_col, rows_in, block = shard
    n = block // rows_in
    rows, wide = pre.shape[1:]
    term = jax.ShapeDtypeStruct(shard, bf16)
    grad = jax.ShapeDtypeStruct((2 * half_cols, act_t.shape[2], block), bf16)
    *far, grad = whole_call(
        partial(backward_kernel, per_col, width, n),
        "backward",
        [act_t, pre, kept, sib, gain, own, other],
        [term, term, grad],
        scratch=[pltpu.VMEM((2, 2, rows, block), f32)],
        scalars=[scal],
        cost=(4 * rows * wide * per_col * rows_in, 16 * 2**20),
    )
    return far, grad


def other_terms(scal, act_t, grad, far, shard):
    half_cols, per_col, rows_in, block = shard
    n = block // rows_in
    near = whole_call(
        partial(terms_kernel, per_col, n),
        "terms",
        [act_t, grad],
        [jax.ShapeDtypeStruct(shard, bf16)] * (2 * n - 2),
        scalars=[scal],
        cost=(2 * grad.size * per_col * block, 16 * 2**20),
    )
    slots = []
    for h, f in enumerate(far_slots(n)):
        mine = list(near[h * (n - 1) : (h + 1) * (n - 1)])
        slots.append(mine[:f] + [far[h]] + mine[f:])
    return slots


def gossip_hops():
    devices = lax.axis_size("rep")
    hops = {}
    for entry, stride in enumerate((1, 2, 4)):
        if stride % devices:
            hops.setdefault(stride % devices, []).append(entry)
    return hops


def partner_of(taken, low):
    devices = lax.axis_size("rep")
    partner = None
    for hop, chosen in taken.items():
        shift = [(i, (i + hop) % devices) for i in range(devices)]
        moved = lambda x, last, shift=shift: lax.ppermute(x, "rep", shift)
        if partner is None:
            partner = lax.cond(chosen, moved, lambda x, last: jnp.zeros_like(x), low, 0)
        else:
            partner = lax.cond(chosen, moved, lambda x, last: last, low, partner)
    return low if partner is None else partner


def mixed(taken, weight):
    devices = lax.axis_size("rep")
    for hop, chosen in taken.items():
        shift = [(i, (i + hop) % devices) for i in range(devices)]

        def mean(own, shift=shift):
            return 0.5 * (own + lax.ppermute(own.astype(bf16), "rep", shift).astype(f32))

        weight = lax.cond(chosen, mean, lambda own: own, weight)
    return weight


def body(activations, residual, upstream, norm_gain, params, momentum, pattern, step_index):
    steps, rows, features = activations.shape[1:]
    width = residual.shape[3]
    own_rows, out_blocks, per_col, block = params.shape[1:]
    scaling = 1.0 / math.sqrt(per_col * block)
    ring = Ring(lax.axis_size("fsdp"))
    n = ring.chips
    columns = out_blocks // 2
    half_cols = columns // 2

    core = this_core()
    place = ring_place(n, lax.div(lax.axis_index("fsdp"), jnp.int32(2)))
    places = place + jnp.arange(n, dtype=jnp.int32)
    chips = chip_at(n, jnp.where(places < n, places, places - n))
    used = lax.dynamic_slice_in_dim(pattern, core * columns, columns, 0)
    scal = jnp.concatenate([chips, used.reshape(-1), core[None] * columns]).astype(jnp.int32)
    gain = norm_gain.reshape(out_blocks, 1, block)

    taken, keeps = [], []
    hops = gossip_hops()
    for s in range(steps):
        entry = lax.rem(step_index[0] + s, jnp.int32(3))
        chosen = {hop: [entry == e for e in entries] for hop, entries in hops.items()}
        taken.append({hop: functools.reduce(jnp.logical_or, flags) for hop, flags in chosen.items()})
        moved = functools.reduce(jnp.logical_or, taken[s].values(), jnp.bool_(False))
        keeps.append(jnp.where(moved, 0.5, 1.0).astype(f32).reshape(1))

    shard = (half_cols, per_col, 2 * own_rows, block)
    mine, theirs = split(params[0])
    theirs = ring.swap(theirs)
    weights = [mine, theirs]
    scal, gain, taken, keeps = lax.optimization_barrier((scal, gain, taken, keeps))
    tokens = (activations, residual, upstream)

    def picked(s, mine, arrived):
        arrays = tokens[1:] if mine else tokens
        return pick(s, mine, features, *[after(x, arrived) for x in arrays])

    given = picked(0, False, scal)
    halves = list(merge(*weights, shard))
    halves[0] = after(halves[0], scal)
    sib = ring.swap(after(given, theirs))
    state = {}

    def keep(name, make):
        def work(arrived):
            state[name] = make(arrived)
            return jax.tree.leaves(state[name])

        return work

    for s in range(steps):
        last = s == steps - 1
        beside = {2: keep("kept", lambda arrived: picked(s, True, arrived))}
        if not last:
            beside[3] = keep("later", lambda arrived: picked(s + 1, False, arrived))
        beside[4] = keep("turned", lambda arrived: turn(after(scal, arrived), given, sib, block, n))
        slots = ring.gather(halves, beside)
        for i, work in beside.items():
            if i >= len(ring.rounds()):
                work(halves[0])
        kept, act_t = state["kept"], state["turned"]
        part = forward(scal, act_t, kept, sib, slots, scaling)
        pre, own = norm(scal, act_t, part, kept, sib, gain, slots, scaling)
        other = ring.swap(own)
        if s == 0:
            moments = split(after(momentum, own)[0])
            other = after(other, *moments)
        first, grad = backward(scal, act_t, pre, kept, sib, gain, own, other, shard, float(width))
        ready = []
        if not last:
            given = state["later"]
            sib = ring.swap(after(given, other))
        if s == 0:
            moments = [moments[0], ring.swap(after(moments[1], other))]
        if last:
            moments = [moments[0], ring.swap(after(moments[1], other))]
            weights = [weights[0], ring.swap(after(weights[1], other))]
            ready += [moments[1], weights[1]]
        if ready:
            first = lax.optimization_barrier((*first, *ready))[:2]
        terms = other_terms(scal, act_t, grad, first, shard)
        if not last:
            third = max(n // 2 - 1, 1)
            terms[0][third] = after(terms[0][third], sib, moments[1])
        parts = ring.scatter_sum(terms)
        if not last:
            moments, weights, low = update(parts, moments, weights, scaling, shard)
            partner = partner_of(after(taken[s], low), low)
            weights, halves = blend(keeps[s], weights, partner, shard)
    mine, theirs = last_sum(parts, shard)
    weight, moment = finish([mine, ring.swap(theirs)], moments, weights, scaling)
    return (mixed(after(taken[-1], weight), weight)[None], moment[None])


def solution(mesh):
    in_specs = (
        P("rep", None, "fsdp", None),
        P("rep", None, "fsdp", None),
        P("rep", None, "fsdp", None),
        P(),
        P("rep", "fsdp", None, None, None),
        P("rep", "fsdp", None, None, None),
        P(),
        P(),
    )
    out_specs = (P("rep", "fsdp", None, None, None), P("rep", "fsdp", None, None, None))
    return jax.shard_map(body, mesh=mesh, in_specs=in_specs, out_specs=out_specs, check_vma=False)
```

```python
import functools
import math
from functools import partial

import jax
import jax.numpy as jnp
import numpy as np
from jax import lax
from jax.experimental import pallas as pl
from jax.experimental.pallas import tpu as pltpu
from jax.sharding import PartitionSpec as P

learn_rate = 0.1
momentum_beta = 0.9
decay_keep = 0.999
epsilon = 1e-06

f32 = jnp.float32
bf16 = jnp.bfloat16
WHOLE = pl.BlockSpec(memory_space=pltpu.VMEM)
SCALARS = pl.BlockSpec(memory_space=pltpu.SMEM)
PARAMS = pltpu.CompilerParams(vmem_limit_bytes=16 * 2**20)


def vmem(x):
    return pltpu.with_memory_space_constraint(x, pltpu.VMEM)


def in_vmem(shape):
    return pltpu.VMEM(shape.shape, shape.dtype)


def after(x, *others):
    if not others:
        return x
    return lax.optimization_barrier((x, *others))[0]


def ring_order(chips):
    if chips % 2:
        return list(range(chips))
    return list(range(0, chips, 2)) + list(range(chips - 1, 0, -2))


def ring_place(chips, chip):
    if chips % 2:
        return chip
    up = lax.div(chip, jnp.int32(2))
    return jnp.where(lax.rem(chip, jnp.int32(2)) == 0, up, chips - 1 - up)


def chip_at(chips, place):
    if chips % 2:
        return place
    return jnp.where(place < chips // 2, 2 * place, 2 * (chips - 1 - place) + 1)


def this_core():
    return lax.rem(lax.axis_index("fsdp"), jnp.int32(2))


class Ring:
    def __init__(self, devices):
        self.chips = devices // 2
        order = ring_order(self.chips)
        n = self.chips
        self.to_right = [
            (2 * order[p] + k, 2 * order[(p + 1) % n] + k) for p in range(n) for k in (0, 1)
        ]
        self.to_left = [(b, a) for a, b in self.to_right]
        self.pair = [(i, i ^ 1) for i in range(devices)]

    def swap(self, x):
        return lax.ppermute(x, "fsdp", self.pair)

    def rounds(self):
        n = self.chips
        short = (n - 1) // 2
        rounds = []
        for s in range(1, n // 2 + 1):
            if s <= n - 1 - short:
                rounds.append([(0, 0, s), (1, 1, s)])
            if s <= short:
                rounds.append([(1, 0, s), (0, 1, s)])
        return rounds

    def move(self, x, direction):
        return lax.ppermute(x, "fsdp", self.to_left if direction else self.to_right)

    def gather(self, halves, beside):
        n = self.chips
        slots = [[x] + [None] * (n - 1) for x in halves]
        arrived = []
        for i, pair in enumerate(self.rounds()):
            ready = beside[i](arrived[i - 3] if i >= 3 else halves[0]) if i in beside else []
            for h, d, s in pair:
                x = after(slots[h][s - 1 if d else (1 - s) % n], *ready)
                slots[h][s if d else n - s] = self.move(x, d)
                ready = []
            arrived.append(slots[pair[0][0]][n - pair[0][2]])
        return slots

    def scatter_sum(self, slots):
        n = self.chips
        moving = {}
        for pair in sorted(self.rounds(), key=lambda pair: -pair[0][2]):
            for h, d, s in pair:
                term = slots[h][n - s if d else s]
                if (h, d) in moving:
                    term = add_low(moving[h, d], term)
                moving[h, d] = self.move(term, d)
        return [
            [slots[h][0]] + [moving[h, d] for d in range(2) if (h, d) in moving]
            for h in range(len(slots))
        ]


def add_kernel(a, b, out):
    out[...] = (a[...].astype(f32) + b[...].astype(f32)).astype(bf16)


def add_low(a, b):
    return pl.pallas_call(
        add_kernel,
        in_specs=[WHOLE, WHOLE],
        out_specs=WHOLE,
        out_shape=in_vmem(a),
        compiler_params=PARAMS,
        cost_estimate=pl.CostEstimate(flops=a.size, bytes_accessed=6 * a.size, transcendentals=0),
        name="add",
    )(vmem(a), vmem(b))


def whole_call(kernel, name, operands, outs, scratch=(), scalars=(), raw=(), cost=(0, 0)):
    return pl.pallas_call(
        kernel,
        in_specs=[SCALARS] * len(scalars)
        + [pl.BlockSpec(memory_space=pl.ANY)] * len(raw)
        + [WHOLE] * len(operands),
        out_specs=[WHOLE] * len(outs),
        out_shape=[in_vmem(x) for x in outs],
        scratch_shapes=list(scratch),
        compiler_params=PARAMS,
        cost_estimate=pl.CostEstimate(flops=cost[0], bytes_accessed=cost[1], transcendentals=0),
        name=name,
    )(
        *scalars,
        *[pltpu.with_memory_space_constraint(x, pltpu.HBM) for x in raw],
        *[vmem(x) for x in operands],
    )


def by_core(body):
    core = this_core()
    for c in range(2):
        pl.when(core == c)(partial(body, c))


def columns_loop(columns, column):
    lax.fori_loop(0, columns, lambda c, _: column(c) or 0, 0, unroll=2 if columns % 2 == 0 else 1)


def halves_of(mine, theirs, core):
    return jnp.concatenate([theirs, mine] if core else [mine, theirs], axis=-2)


def rows_of(x, core):
    rows = x.shape[-2] // 2
    low, high = x[..., :rows, :], x[..., rows:, :]
    return (high, low) if core else (low, high)


def shapes_of(shard):
    half_cols, per_col, rows_in, block = shard
    rows = jax.ShapeDtypeStruct((2 * half_cols, per_col, rows_in // 2, block), f32)
    return rows, jax.ShapeDtypeStruct(shard, bf16)


def merge_kernel(mine, theirs, low_a, low_b):
    half_cols = low_a.shape[0]

    def body(core):
        for h, out in enumerate((low_a, low_b)):

            def column(c, h=h, out=out):
                at = h * half_cols + c
                out[c] = halves_of(mine[at], theirs[at], core).astype(bf16)

            columns_loop(half_cols, column)

    by_core(body)


def merge(mine, theirs, shard):
    low = shapes_of(shard)[1]
    return whole_call(merge_kernel, "merge", [mine, theirs], [low, low], cost=(0, mine.size * 12))


def gathered_sum(parts, c):
    return sum(part[c].astype(f32) for part in parts)


def update_kernel(count, scaling, *refs):
    parts = refs[:count], refs[count : 2 * count]
    moments, weights = refs[2 * count : 2 * count + 2], refs[2 * count + 2 : 2 * count + 4]
    far = refs[2 * count + 4 : 2 * count + 9]
    near, sems = refs[2 * count + 9 : 2 * count + 14], refs[-1]
    moments_out, weights_out, low = near[:2], near[2:4], near[4]
    half_cols = low.shape[0] // 2

    cuts = [pl.ds(h * half_cols, half_cols) for h in range(2)]
    copies = [
        pltpu.make_async_copy(near[i].at[cut], far[i].at[cut], sems.at[i, h])
        for h, cut in enumerate(cuts)
        for i in range(5)
    ]

    def body(core):
        for h in range(2):

            def column(c, h=h):
                at = h * half_cols + c
                news = []
                for r, gradient in enumerate(rows_of(gathered_sum(parts[h], c), core)):
                    moment = momentum_beta * moments[r][at] + scaling * gradient
                    moments_out[r][at] = moment
                    news.append(decay_keep * weights[r][at] - learn_rate * moment)
                    weights_out[r][at] = news[r]
                low[at] = halves_of(*news, core).astype(bf16)

            columns_loop(half_cols, column)
            for copy in copies[5 * h : 5 * h + 5]:
                copy.start()

    by_core(body)
    for copy in copies:
        copy.wait()


def update(parts, moments, weights, scaling, shard):
    rows = shapes_of(shard)[0]
    low = jax.ShapeDtypeStruct((2 * shard[0], *shard[1:]), bf16)
    outs = [rows] * 4 + [low]
    operands = [*parts[0], *parts[1], *moments, *weights]
    out = pl.pallas_call(
        partial(update_kernel, len(parts[0]), scaling),
        in_specs=[WHOLE] * len(operands),
        out_specs=[pl.BlockSpec(memory_space=pl.ANY)] * 5,
        out_shape=[pltpu.HBM(x.shape, x.dtype) for x in outs],
        scratch_shapes=[pltpu.VMEM(x.shape, x.dtype) for x in outs]
        + [pltpu.SemaphoreType.DMA((5, 2))],
        compiler_params=PARAMS,
        cost_estimate=pl.CostEstimate(
            flops=rows.size * 20, bytes_accessed=rows.size * 60, transcendentals=0
        ),
        name="update",
    )(*[vmem(x) for x in operands])
    return out[:2], out[2:4], out[4]


def blend_kernel(keep, *refs):
    far, outs, (low_a, low_b) = refs[:3], refs[3:5], refs[5:7]
    near, sems = refs[7:10], refs[10]
    mine, theirs, part = near
    half_cols = low_a.shape[0]
    share = keep[0]
    copies = [pltpu.make_async_copy(far[i], near[i], sems.at[i]) for i in range(3)]
    for copy in copies:
        copy.start()
    for copy in copies:
        copy.wait()

    def body(core):
        for h, low in enumerate((low_a, low_b)):

            def column(c, h=h, low=low):
                at = h * half_cols + c
                news = []
                for own, to, other in zip(
                    (mine, theirs), outs, rows_of(part[at].astype(f32), core)
                ):
                    news.append(share * own[at] + (1.0 - share) * other)
                    to[at] = news[-1]
                low[c] = halves_of(*news, core).astype(bf16)

            columns_loop(half_cols, column)

    by_core(body)


def blend(keep, weights, partner, shard):
    rows, low = shapes_of(shard)
    outs = [rows, rows, low, low]
    raw = pl.BlockSpec(memory_space=pl.ANY)
    out = pl.pallas_call(
        blend_kernel,
        in_specs=[SCALARS] + [raw] * 3,
        out_specs=[WHOLE] * 4,
        out_shape=[in_vmem(x) for x in outs],
        scratch_shapes=[
            pltpu.VMEM(rows.shape, f32),
            pltpu.VMEM(rows.shape, f32),
            pltpu.VMEM(partner.shape, bf16),
            pltpu.SemaphoreType.DMA((3,)),
        ],
        compiler_params=PARAMS,
        cost_estimate=pl.CostEstimate(
            flops=rows.size * 6, bytes_accessed=rows.size * 24, transcendentals=0
        ),
        name="blend",
    )(keep, *[pltpu.with_memory_space_constraint(x, pltpu.HBM) for x in (*weights, partner)])
    return out[:2], list(out[2:])


def last_sum_kernel(count, *refs):
    parts = refs[:count], refs[count : 2 * count]
    outs = refs[2 * count :]
    half_cols = parts[0][0].shape[0]

    def body(core):
        for h in range(2):

            def column(c, h=h):
                for out, rows in zip(outs, rows_of(gathered_sum(parts[h], c), core)):
                    out[h * half_cols + c] = rows

            columns_loop(half_cols, column)

    by_core(body)


def last_sum(parts, shard):
    rows = shapes_of(shard)[0]
    return whole_call(
        partial(last_sum_kernel, len(parts[0])),
        "last_sum",
        [*parts[0], *parts[1]],
        [rows, rows],
        cost=(rows.size * 4, rows.size * 20),
    )


def finish_kernel(scaling, *refs):
    gradients, moments, weights = refs[:2], refs[2:4], refs[4:6]
    outs, near, sems = refs[6:8], refs[8:10], refs[10]
    columns, per_col, rows = gradients[0].shape[:3]
    core = this_core()
    copies = []
    for k in range(per_col):

        def column(c, k=k):
            for side, owner in enumerate((core, 1 - core)):
                at = pl.ds(owner * columns + c, rows, stride=2 * columns)
                moment = momentum_beta * moments[side][c, k] + scaling * gradients[side][c, k]
                near[0][k, at, :] = decay_keep * weights[side][c, k] - learn_rate * moment
                near[1][k, at, :] = moment

        columns_loop(columns, column)
        for i in range(2):
            for r in range(rows):
                rows_of_k = near[i].at[k, pl.ds(r * 2 * columns, 2 * columns)]
                copy = pltpu.make_async_copy(rows_of_k, outs[i].at[r, k], sems.at[i, k])
                copy.start()
                copies.append(copy)
    for copy in copies:
        copy.wait()


def finish(gradients, moments, weights, scaling):
    columns, per_col, rows, block = gradients[0].shape
    operands = [*gradients, *moments, *weights]
    out = pltpu.HBM((rows, per_col, 2 * columns, block), f32)
    weight, moment = pl.pallas_call(
        partial(finish_kernel, scaling),
        in_specs=[WHOLE] * len(operands),
        out_specs=[pl.BlockSpec(memory_space=pl.ANY)] * 2,
        out_shape=[out, out],
        scratch_shapes=[pltpu.VMEM((per_col, rows * 2 * columns, block), f32)] * 2
        + [pltpu.SemaphoreType.DMA((2, per_col))],
        compiler_params=PARAMS,
        cost_estimate=pl.CostEstimate(
            flops=12 * gradients[0].size, bytes_accessed=80 * gradients[0].size, transcendentals=0
        ),
        name="finish",
    )(*[vmem(x) for x in operands])
    return [x.transpose(0, 2, 1, 3) for x in (weight, moment)]


def split_kernel(out_blocks, raw, kept, given, x, sem):
    columns, per_col, rows = kept.shape[:3]
    core = this_core()
    copy = pltpu.make_async_copy(raw, x, sem)
    copy.start()
    copy.wait()

    def column(c):
        for k in range(per_col):
            for out, owner in ((given, 1 - core), (kept, core)):
                start = k * out_blocks + owner * columns + c
                out[c, k] = x[pl.ds(start, rows, stride=per_col * out_blocks), :]

    columns_loop(columns, column)


def split(x):
    rows, out_blocks, per_col, block = x.shape
    flat = x.transpose(0, 2, 1, 3).reshape(-1, block)
    half = jax.ShapeDtypeStruct((out_blocks // 2, per_col, rows, block), f32)
    return whole_call(
        partial(split_kernel, out_blocks),
        "split",
        [],
        [half, half],
        scratch=[pltpu.VMEM(flat.shape, f32), pltpu.SemaphoreType.DMA(())],
        raw=[flat],
        cost=(0, 8 * x.size),
    )


def row_cuts(rows):
    if rows % 16:
        return [pl.ds(0, rows)]
    tiles = rows // 16
    pieces = min(4, tiles)
    edges = [16 * (tiles * i // pieces) for i in range(pieces + 1)]
    return [pl.ds(a, b - a) for a, b in zip(edges, edges[1:])]


def pick_kernel(s, mine, raws, outs, sems):
    core = this_core()
    half = core if mine else 1 - core
    copies = []
    _, rows, wide = outs.shape
    for i, raw in enumerate(raws):
        lanes = pl.ds(0, wide)
        if raw.shape[3] != wide:
            lanes = pl.ds(pl.multiple_of(half * wide, wide), wide)
        for j, cut in enumerate(row_cuts(rows)):
            copies.append(
                pltpu.make_async_copy(raw.at[0, s, cut, lanes], outs.at[i, cut], sems.at[i, j])
            )
    for copy in copies:
        copy.start()
    for copy in copies:
        copy.wait()


def pick(s, mine, wide, *raws):
    rows = raws[0].shape[2]
    count = len(raws)

    def kernel(*refs):
        pick_kernel(s, mine, refs[:count], refs[count], refs[count + 1])

    (out,) = whole_call(
        kernel,
        "pick",
        [],
        [jax.ShapeDtypeStruct((count, rows, wide), bf16)],
        scratch=[pltpu.SemaphoreType.DMA((count, len(row_cuts(rows))))],
        raw=raws,
        cost=(0, 4 * count * rows * wide),
    )
    return out


def turn_kernel(n, scal, own, sib, out, turned):
    in_blocks, block, room = out.shape
    rows = own.shape[1]
    rest = jnp.zeros((room - 2 * rows, block), bf16)
    piece = block // n

    def one(p, carry):
        lane = pl.ds(pl.multiple_of(p * block, block), block)
        x = jnp.concatenate([own[0, :, lane], sib[0, :, lane], rest], axis=0)
        turned[p % 2] = x.T.reshape(n, piece, room)
        for r in range(n):
            out[p, r * piece : (r + 1) * piece] = turned[p % 2, scal[r]]
        return carry

    lax.fori_loop(0, in_blocks, one, 0, unroll=2 if in_blocks % 2 == 0 else 1)


def turn(scal, own, sib, block, n):
    _, rows, features = own.shape
    room = -(-2 * rows // block) * block
    (out,) = whole_call(
        partial(turn_kernel, n),
        "turn",
        [own, sib],
        [jax.ShapeDtypeStruct((features // block, block, room), bf16)],
        scratch=[pltpu.VMEM((2, n, block // n, room), bf16)],
        scalars=[scal],
        cost=(0, 8 * rows * features),
    )
    return out


def far_slots(n):
    return n // 2, n - n // 2


def features_of(act_t, scal, n, at, per_col, slots):
    piece = act_t.shape[1] // n
    runs = []
    for r in slots:
        if runs and runs[-1][1] == r * piece:
            runs[-1][1] += piece
        else:
            runs.append([r * piece, (r + 1) * piece])
    return jnp.concatenate(
        [act_t[scal[n + at * per_col + k], a:b] for k in range(per_col) for a, b in runs], axis=0
    )


def project(act_t, scal, n, at, weights, j):
    per_col = weights[min(weights)].shape[1]
    x = features_of(act_t, scal, n, at, per_col, sorted(weights))
    w = jnp.concatenate(
        [weights[r][j, k] for k in range(per_col) for r in sorted(weights)], axis=0
    )
    return lax.dot_general(x, w, (((0,), (0,)), ((), ())), preferred_element_type=f32)


def forward_kernel(scaling, n, scal, act_t, kept, sib, *refs):
    near = [[r for r in range(n) if r != f] for f in far_slots(n)]
    slots = [dict(zip(near[0], refs)), dict(zip(near[1], refs[n - 1 :]))]
    part = refs[-1]
    half_cols, _, _, block = refs[0].shape
    rows = part.shape[1]
    cols = group_columns(half_cols)

    for h in range(2):

        def group(i, carry, h=h):
            for j in range(cols):
                c = h * half_cols + i * cols + j
                cut = pl.ds(pl.multiple_of(c * block, block), block)
                out = scaling * project(act_t, scal, n, c, slots[h], i * cols + j)
                for t, res in enumerate((kept.at[0], sib.at[1])):
                    value = res[:, cut].astype(f32) + out[t * rows : (t + 1) * rows]
                    part[t, :, cut] = value
            return carry

        lax.fori_loop(0, half_cols // cols, group, 0)


def interleaved(main, side):
    done = 0
    for i, step in enumerate(main):
        step()
        upto = len(side) * (i + 1) // len(main)
        for other in side[done:upto]:
            other()
        done = upto


def norm_kernel(per_col, scaling, n, scal, act_t, part, kept, sib, gain, far_a, far_b, *refs):
    pre, stats, sums, share = refs
    half_cols, _, _, block = far_a.shape
    rows = pre.shape[1]
    cols = group_columns(half_cols)
    base = scal[n + 2 * half_cols * per_col]
    sums[...] = jnp.zeros_like(sums)

    size = 16 if rows % 16 == 0 else rows

    def product(c):
        h = c // half_cols
        f, far = far_slots(n)[h], (far_a, far_b)[h]
        share[c // cols % 2, c % cols] = project(act_t, scal, n, c, {f: far}, c % half_cols)

    def add_up(g, t, at):
        chunk = slice(at, at + size)
        square, inner = sums[t, 0, chunk], sums[t, 1, chunk]
        for j in range(cols):
            c = g * cols + j
            cut = slice(c * block, (c + 1) * block)
            own = share[g % 2, j, t * rows + at : t * rows + at + size]
            value = part[t, chunk, cut] + scaling * own
            pre[t, chunk, cut] = value
            up = (sib.at[2] if t else kept.at[1])[chunk, cut].astype(f32)
            square += value * value
            inner += value * (gain[base + c] * up)
        sums[t, 0, chunk], sums[t, 1, chunk] = square, inner

    groups = 2 * half_cols // cols
    for g in range(groups + 1):
        side = []
        if g > 0:
            side = [partial(add_up, g - 1, t, at) for t in range(2) for at in range(0, rows, size)]
        main = [partial(product, c) for c in range(g * cols, (g + 1) * cols) if g < groups]
        interleaved(main or [lambda: None], side)

    lane = lax.broadcasted_iota(jnp.int32, stats.shape[1:], 1)
    for t in range(2):
        square = jnp.sum(sums[t, 0], axis=1, keepdims=True)
        inner = jnp.sum(sums[t, 1], axis=1, keepdims=True)
        stats[t] = jnp.where(lane < block // 2, square, inner)


def backward_kernel(per_col, width, n, scal, act_t, pre, kept, sib, gain, own, other, *refs):
    outs, grad, scales = refs[:2], refs[2], refs[3]
    half_cols, _, rows_in, block = outs[0].shape
    rows = pre.shape[1]
    cols = group_columns(half_cols)
    size = 16 if rows % 16 == 0 else rows
    base = scal[n + 2 * half_cols * per_col]

    for t in range(2):
        total = own[t] + other[1 - t]
        square, inner = total[:, 0:1], total[:, block // 2 : block // 2 + 1]
        inv = lax.rsqrt(square / width + epsilon)
        scales[t, 0] = jnp.broadcast_to(inv, scales.shape[2:])
        scales[t, 1] = jnp.broadcast_to(inv * inv * inv * (inner / width), scales.shape[2:])
    grad[:, 2 * rows :] = jnp.zeros((2 * half_cols, grad.shape[1] - 2 * rows, block), bf16)

    def gradients(g, t, at):
        up = sib.at[2] if t else kept.at[1]
        chunk = slice(at, at + size)
        inv, inner = scales[t, 0, chunk], scales[t, 1, chunk]
        for c in range(g * cols, (g + 1) * cols):
            cut = slice(c * block, (c + 1) * block)
            weighted = gain[base + c] * up[chunk, cut].astype(f32)
            to = slice(t * rows + at, t * rows + at + size)
            grad[c, to] = (inv * weighted - pre[t, chunk, cut] * inner).astype(bf16)

    def product(c):
        h = c // half_cols
        x = features_of(act_t, scal, n, c, per_col, [far_slots(n)[h]])
        term = jnp.dot(x, grad[c], preferred_element_type=f32).astype(bf16)
        outs[h][c % half_cols] = term.reshape(per_col, rows_in, block)

    groups = 2 * half_cols // cols
    for g in range(groups + 1):
        side = []
        if g < groups:
            side = [partial(gradients, g, t, at) for t in range(2) for at in range(0, rows, size)]
        main = [partial(product, c) for c in range(max(g - 1, 0) * cols, g * cols)]
        interleaved(main or [lambda: None], side)


def terms_kernel(per_col, n, scal, act_t, grad, *outs):
    near = [[r for r in range(n) if r != f] for f in far_slots(n)]
    outs = [dict(zip(near[0], outs)), dict(zip(near[1], outs[n - 1 :]))]
    half_cols, _, rows_in, block = outs[0][near[0][0]].shape
    for c in range(2 * half_cols):
        h, at = c // half_cols, c % half_cols
        x = features_of(act_t, scal, n, c, per_col, range(n))
        term = jnp.dot(x, grad[c], preferred_element_type=f32)
        term = term.astype(bf16).reshape(per_col, n, rows_in, block)
        for r in near[h]:
            outs[h][r][at] = term[:, r]


def group_columns(half_cols):
    return max(c for c in range(1, 6) if half_cols % c == 0)


def forward(scal, act_t, kept, sib, slots, scaling):
    n = len(slots[0])
    half_cols, per_col, rows_in, block = slots[0][0].shape
    _, rows, wide = kept.shape
    near = [x for h, f in enumerate(far_slots(n)) for r, x in enumerate(slots[h]) if r != f]
    (part,) = whole_call(
        partial(forward_kernel, scaling, n),
        "forward",
        [act_t, kept, sib, *near],
        [jax.ShapeDtypeStruct((2, rows, wide), f32)],
        scalars=[scal],
        cost=(4 * rows * wide * per_col * block, 16 * 2**20),
    )
    return part


def norm(scal, act_t, part, kept, sib, gain, slots, scaling):
    n = len(slots[0])
    half_cols, per_col, rows_in, block = slots[0][0].shape
    _, rows, wide = part.shape
    far = [slots[h][f] for h, f in enumerate(far_slots(n))]
    return whole_call(
        partial(norm_kernel, per_col, scaling, n),
        "norm",
        [act_t, part, kept, sib, gain, *far],
        [jax.ShapeDtypeStruct(part.shape, f32), jax.ShapeDtypeStruct((2, rows, block), f32)],
        scratch=[
            pltpu.VMEM((2, 2, rows, block), f32),
            pltpu.VMEM((2, group_columns(half_cols), act_t.shape[2], block), f32),
        ],
        scalars=[scal],
        cost=(4 * rows * wide * per_col * rows_in, 16 * 2**20),
    )


def backward(scal, act_t, pre, kept, sib, gain, own, other, shard, width):
    half_cols, per_col, rows_in, block = shard
    n = block // rows_in
    rows, wide = pre.shape[1:]
    term = jax.ShapeDtypeStruct(shard, bf16)
    grad = jax.ShapeDtypeStruct((2 * half_cols, act_t.shape[2], block), bf16)
    *far, grad = whole_call(
        partial(backward_kernel, per_col, width, n),
        "backward",
        [act_t, pre, kept, sib, gain, own, other],
        [term, term, grad],
        scratch=[pltpu.VMEM((2, 2, rows, block), f32)],
        scalars=[scal],
        cost=(4 * rows * wide * per_col * rows_in, 16 * 2**20),
    )
    return far, grad


def other_terms(scal, act_t, grad, far, shard):
    half_cols, per_col, rows_in, block = shard
    n = block // rows_in
    near = whole_call(
        partial(terms_kernel, per_col, n),
        "terms",
        [act_t, grad],
        [jax.ShapeDtypeStruct(shard, bf16)] * (2 * n - 2),
        scalars=[scal],
        cost=(2 * grad.size * per_col * block, 16 * 2**20),
    )
    slots = []
    for h, f in enumerate(far_slots(n)):
        mine = list(near[h * (n - 1) : (h + 1) * (n - 1)])
        slots.append(mine[:f] + [far[h]] + mine[f:])
    return slots


def gossip_hops():
    devices = lax.axis_size("rep")
    hops = {}
    for entry, stride in enumerate((1, 2, 4)):
        if stride % devices:
            hops.setdefault(stride % devices, []).append(entry)
    return hops


def partner_of(taken, low):
    devices = lax.axis_size("rep")
    partner = None
    for hop, chosen in taken.items():
        shift = [(i, (i + hop) % devices) for i in range(devices)]
        moved = lambda x, last, shift=shift: lax.ppermute(x, "rep", shift)
        if partner is None:
            partner = lax.cond(chosen, moved, lambda x, last: jnp.zeros_like(x), low, 0)
        else:
            partner = lax.cond(chosen, moved, lambda x, last: last, low, partner)
    return low if partner is None else partner


def mixed(taken, weight):
    devices = lax.axis_size("rep")
    for hop, chosen in taken.items():
        shift = [(i, (i + hop) % devices) for i in range(devices)]

        def mean(own, shift=shift):
            return 0.5 * (own + lax.ppermute(own.astype(bf16), "rep", shift).astype(f32))

        weight = lax.cond(chosen, mean, lambda own: own, weight)
    return weight


def body(activations, residual, upstream, norm_gain, params, momentum, pattern, step_index):
    steps, rows, features = activations.shape[1:]
    width = residual.shape[3]
    own_rows, out_blocks, per_col, block = params.shape[1:]
    scaling = 1.0 / math.sqrt(per_col * block)
    ring = Ring(lax.axis_size("fsdp"))
    n = ring.chips
    columns = out_blocks // 2
    half_cols = columns // 2

    core = this_core()
    place = ring_place(n, lax.div(lax.axis_index("fsdp"), jnp.int32(2)))
    places = place + jnp.arange(n, dtype=jnp.int32)
    chips = chip_at(n, jnp.where(places < n, places, places - n))
    used = lax.dynamic_slice_in_dim(pattern, core * columns, columns, 0)
    scal = jnp.concatenate([chips, used.reshape(-1), core[None] * columns]).astype(jnp.int32)
    gain = norm_gain.reshape(out_blocks, 1, block)

    taken, keeps = [], []
    hops = gossip_hops()
    for s in range(steps):
        entry = lax.rem(step_index[0] + s, jnp.int32(3))
        chosen = {hop: [entry == e for e in entries] for hop, entries in hops.items()}
        taken.append({hop: functools.reduce(jnp.logical_or, flags) for hop, flags in chosen.items()})
        moved = functools.reduce(jnp.logical_or, taken[s].values(), jnp.bool_(False))
        keeps.append(jnp.where(moved, 0.5, 1.0).astype(f32).reshape(1))

    shard = (half_cols, per_col, 2 * own_rows, block)
    mine, theirs = split(params[0])
    theirs = ring.swap(theirs)
    weights = [mine, theirs]
    scal, gain, taken, keeps = lax.optimization_barrier((scal, gain, taken, keeps))
    tokens = (activations, residual, upstream)

    def picked(s, mine, arrived):
        arrays = tokens[1:] if mine else tokens
        return pick(s, mine, features, *[after(x, arrived) for x in arrays])

    given = picked(0, False, scal)
    halves = list(merge(*weights, shard))
    halves[0] = after(halves[0], scal)
    sib = ring.swap(after(given, theirs))
    state = {}

    def keep(name, make):
        def work(arrived):
            state[name] = make(arrived)
            return jax.tree.leaves(state[name])

        return work

    for s in range(steps):
        last = s == steps - 1
        beside = {2: keep("kept", lambda arrived: picked(s, True, arrived))}
        if not last:
            beside[3] = keep("later", lambda arrived: picked(s + 1, False, arrived))
        beside[4] = keep("turned", lambda arrived: turn(after(scal, arrived), given, sib, block, n))
        slots = ring.gather(halves, beside)
        for i, work in beside.items():
            if i >= len(ring.rounds()):
                work(halves[0])
        kept, act_t = state["kept"], state["turned"]
        part = forward(scal, act_t, kept, sib, slots, scaling)
        pre, own = norm(scal, act_t, part, kept, sib, gain, slots, scaling)
        other = ring.swap(own)
        if s == 0:
            moments = split(after(momentum, own)[0])
            other = after(other, *moments)
        first, grad = backward(scal, act_t, pre, kept, sib, gain, own, other, shard, float(width))
        ready = []
        if not last:
            given = state["later"]
            sib = ring.swap(after(given, other))
        if s == 0:
            moments = [moments[0], ring.swap(after(moments[1], sib))]
        if last:
            moments = [moments[0], ring.swap(after(moments[1], other))]
            weights = [weights[0], ring.swap(after(weights[1], other))]
            ready += [moments[1], weights[1]]
        if ready:
            first = lax.optimization_barrier((*first, *ready))[:2]
        terms = other_terms(scal, act_t, grad, first, shard)
        if not last:
            third = max(n // 2 - 1, 1)
            terms[0][third] = after(terms[0][third], sib)
        parts = ring.scatter_sum(terms)
        if not last:
            moments, weights, low = update(parts, moments, weights, scaling, shard)
            partner = partner_of(after(taken[s], low), low)
            weights, halves = blend(keeps[s], weights, partner, shard)
    mine, theirs = last_sum(parts, shard)
    weight, moment = finish([mine, ring.swap(theirs)], moments, weights, scaling)
    return (mixed(after(taken[-1], weight), weight)[None], moment[None])


def solution(mesh):
    in_specs = (
        P("rep", None, "fsdp", None),
        P("rep", None, "fsdp", None),
        P("rep", None, "fsdp", None),
        P(),
        P("rep", "fsdp", None, None, None),
        P("rep", "fsdp", None, None, None),
        P(),
        P(),
    )
    out_specs = (P("rep", "fsdp", None, None, None), P("rep", "fsdp", None, None, None))
    return jax.shard_map(body, mesh=mesh, in_specs=in_specs, out_specs=out_specs, check_vma=False)
```

```python
import functools
import math
from functools import partial

import jax
import jax.numpy as jnp
import numpy as np
from jax import lax
from jax.experimental import pallas as pl
from jax.experimental.pallas import tpu as pltpu
from jax.sharding import PartitionSpec as P

learn_rate = 0.1
momentum_beta = 0.9
decay_keep = 0.999
epsilon = 1e-06

f32 = jnp.float32
bf16 = jnp.bfloat16
WHOLE = pl.BlockSpec(memory_space=pltpu.VMEM)
SCALARS = pl.BlockSpec(memory_space=pltpu.SMEM)
PARAMS = pltpu.CompilerParams(vmem_limit_bytes=16 * 2**20)


def vmem(x):
    return pltpu.with_memory_space_constraint(x, pltpu.VMEM)


def in_vmem(shape):
    return pltpu.VMEM(shape.shape, shape.dtype)


def after(x, *others):
    if not others:
        return x
    return lax.optimization_barrier((x, *others))[0]


def ring_order(chips):
    if chips % 2:
        return list(range(chips))
    return list(range(0, chips, 2)) + list(range(chips - 1, 0, -2))


def ring_place(chips, chip):
    if chips % 2:
        return chip
    up = lax.div(chip, jnp.int32(2))
    return jnp.where(lax.rem(chip, jnp.int32(2)) == 0, up, chips - 1 - up)


def chip_at(chips, place):
    if chips % 2:
        return place
    return jnp.where(place < chips // 2, 2 * place, 2 * (chips - 1 - place) + 1)


def this_core():
    return lax.rem(lax.axis_index("fsdp"), jnp.int32(2))


class Ring:
    def __init__(self, devices):
        self.chips = devices // 2
        order = ring_order(self.chips)
        n = self.chips
        self.to_right = [
            (2 * order[p] + k, 2 * order[(p + 1) % n] + k) for p in range(n) for k in (0, 1)
        ]
        self.to_left = [(b, a) for a, b in self.to_right]
        self.pair = [(i, i ^ 1) for i in range(devices)]

    def swap(self, x):
        return lax.ppermute(x, "fsdp", self.pair)

    def rounds(self):
        n = self.chips
        short = (n - 1) // 2
        rounds = []
        for s in range(1, n // 2 + 1):
            if s <= n - 1 - short:
                rounds.append([(0, 0, s), (1, 1, s)])
            if s <= short:
                rounds.append([(1, 0, s), (0, 1, s)])
        return rounds

    def move(self, x, direction):
        return lax.ppermute(x, "fsdp", self.to_left if direction else self.to_right)

    def gather(self, halves, beside):
        n = self.chips
        slots = [[x] + [None] * (n - 1) for x in halves]
        arrived = []
        for i, pair in enumerate(self.rounds()):
            ready = beside[i](arrived[i - 3] if i >= 3 else halves[0]) if i in beside else []
            for h, d, s in pair:
                x = after(slots[h][s - 1 if d else (1 - s) % n], *ready)
                slots[h][s if d else n - s] = self.move(x, d)
                ready = []
            arrived.append(slots[pair[0][0]][n - pair[0][2]])
        return slots

    def scatter_sum(self, slots):
        n = self.chips
        moving = {}
        for pair in sorted(self.rounds(), key=lambda pair: -pair[0][2]):
            for h, d, s in pair:
                term = slots[h][n - s if d else s]
                if (h, d) in moving:
                    term = add_low(moving[h, d], term)
                moving[h, d] = self.move(term, d)
        return [
            [slots[h][0]] + [moving[h, d] for d in range(2) if (h, d) in moving]
            for h in range(len(slots))
        ]


def add_kernel(a, b, out):
    out[...] = (a[...].astype(f32) + b[...].astype(f32)).astype(bf16)


def add_low(a, b):
    return pl.pallas_call(
        add_kernel,
        in_specs=[WHOLE, WHOLE],
        out_specs=WHOLE,
        out_shape=in_vmem(a),
        compiler_params=PARAMS,
        cost_estimate=pl.CostEstimate(flops=a.size, bytes_accessed=6 * a.size, transcendentals=0),
        name="add",
    )(vmem(a), vmem(b))


def whole_call(kernel, name, operands, outs, scratch=(), scalars=(), raw=(), cost=(0, 0)):
    return pl.pallas_call(
        kernel,
        in_specs=[SCALARS] * len(scalars)
        + [pl.BlockSpec(memory_space=pl.ANY)] * len(raw)
        + [WHOLE] * len(operands),
        out_specs=[WHOLE] * len(outs),
        out_shape=[in_vmem(x) for x in outs],
        scratch_shapes=list(scratch),
        compiler_params=PARAMS,
        cost_estimate=pl.CostEstimate(flops=cost[0], bytes_accessed=cost[1], transcendentals=0),
        name=name,
    )(
        *scalars,
        *[pltpu.with_memory_space_constraint(x, pltpu.HBM) for x in raw],
        *[vmem(x) for x in operands],
    )


def by_core(body):
    core = this_core()
    for c in range(2):
        pl.when(core == c)(partial(body, c))


def columns_loop(columns, column):
    lax.fori_loop(0, columns, lambda c, _: column(c) or 0, 0, unroll=2 if columns % 2 == 0 else 1)


def halves_of(mine, theirs, core):
    return jnp.concatenate([theirs, mine] if core else [mine, theirs], axis=-2)


def rows_of(x, core):
    rows = x.shape[-2] // 2
    low, high = x[..., :rows, :], x[..., rows:, :]
    return (high, low) if core else (low, high)


def shapes_of(shard):
    half_cols, per_col, rows_in, block = shard
    rows = jax.ShapeDtypeStruct((2 * half_cols, per_col, rows_in // 2, block), f32)
    return rows, jax.ShapeDtypeStruct(shard, bf16)


def merge_kernel(mine, theirs, low_a, low_b):
    half_cols = low_a.shape[0]

    def body(core):
        for h, out in enumerate((low_a, low_b)):

            def column(c, h=h, out=out):
                at = h * half_cols + c
                out[c] = halves_of(mine[at], theirs[at], core).astype(bf16)

            columns_loop(half_cols, column)

    by_core(body)


def merge(mine, theirs, shard):
    low = shapes_of(shard)[1]
    return whole_call(merge_kernel, "merge", [mine, theirs], [low, low], cost=(0, mine.size * 12))


def gathered_sum(parts, c):
    return sum(part[c].astype(f32) for part in parts)


def update_kernel(count, scaling, *refs):
    parts = refs[:count], refs[count : 2 * count]
    moments, weights = refs[2 * count : 2 * count + 2], refs[2 * count + 2 : 2 * count + 4]
    far = refs[2 * count + 4 : 2 * count + 9]
    near, sems = refs[2 * count + 9 : 2 * count + 14], refs[-1]
    moments_out, weights_out, low = near[:2], near[2:4], near[4]
    half_cols = low.shape[0] // 2

    cuts = [pl.ds(h * half_cols, half_cols) for h in range(2)]
    copies = [
        pltpu.make_async_copy(near[i].at[cut], far[i].at[cut], sems.at[i, h])
        for h, cut in enumerate(cuts)
        for i in range(5)
    ]

    def body(core):
        for h in range(2):

            def column(c, h=h):
                at = h * half_cols + c
                news = []
                for r, gradient in enumerate(rows_of(gathered_sum(parts[h], c), core)):
                    moment = momentum_beta * moments[r][at] + scaling * gradient
                    moments_out[r][at] = moment
                    news.append(decay_keep * weights[r][at] - learn_rate * moment)
                    weights_out[r][at] = news[r]
                low[at] = halves_of(*news, core).astype(bf16)

            columns_loop(half_cols, column)
            for copy in copies[5 * h : 5 * h + 5]:
                copy.start()

    by_core(body)
    for copy in copies:
        copy.wait()


def update(parts, moments, weights, scaling, shard):
    rows = shapes_of(shard)[0]
    low = jax.ShapeDtypeStruct((2 * shard[0], *shard[1:]), bf16)
    outs = [rows] * 4 + [low]
    operands = [*parts[0], *parts[1], *moments, *weights]
    out = pl.pallas_call(
        partial(update_kernel, len(parts[0]), scaling),
        in_specs=[WHOLE] * len(operands),
        out_specs=[pl.BlockSpec(memory_space=pl.ANY)] * 5,
        out_shape=[pltpu.HBM(x.shape, x.dtype) for x in outs],
        scratch_shapes=[pltpu.VMEM(x.shape, x.dtype) for x in outs]
        + [pltpu.SemaphoreType.DMA((5, 2))],
        compiler_params=PARAMS,
        cost_estimate=pl.CostEstimate(
            flops=rows.size * 20, bytes_accessed=rows.size * 60, transcendentals=0
        ),
        name="update",
    )(*[vmem(x) for x in operands])
    return out[:2], out[2:4], out[4]


def blend_kernel(keep, *refs):
    far, outs, (low_a, low_b) = refs[:3], refs[3:5], refs[5:7]
    near, sems = refs[7:10], refs[10]
    mine, theirs, part = near
    half_cols = low_a.shape[0]
    share = keep[0]
    copies = [pltpu.make_async_copy(far[i], near[i], sems.at[i]) for i in range(3)]
    for copy in copies:
        copy.start()
    for copy in copies:
        copy.wait()

    def body(core):
        for h, low in enumerate((low_a, low_b)):

            def column(c, h=h, low=low):
                at = h * half_cols + c
                news = []
                for own, to, other in zip(
                    (mine, theirs), outs, rows_of(part[at].astype(f32), core)
                ):
                    news.append(share * own[at] + (1.0 - share) * other)
                    to[at] = news[-1]
                low[c] = halves_of(*news, core).astype(bf16)

            columns_loop(half_cols, column)

    by_core(body)


def blend(keep, weights, partner, shard):
    rows, low = shapes_of(shard)
    outs = [rows, rows, low, low]
    raw = pl.BlockSpec(memory_space=pl.ANY)
    out = pl.pallas_call(
        blend_kernel,
        in_specs=[SCALARS] + [raw] * 3,
        out_specs=[WHOLE] * 4,
        out_shape=[in_vmem(x) for x in outs],
        scratch_shapes=[
            pltpu.VMEM(rows.shape, f32),
            pltpu.VMEM(rows.shape, f32),
            pltpu.VMEM(partner.shape, bf16),
            pltpu.SemaphoreType.DMA((3,)),
        ],
        compiler_params=PARAMS,
        cost_estimate=pl.CostEstimate(
            flops=rows.size * 6, bytes_accessed=rows.size * 24, transcendentals=0
        ),
        name="blend",
    )(keep, *[pltpu.with_memory_space_constraint(x, pltpu.HBM) for x in (*weights, partner)])
    return out[:2], list(out[2:])


def last_sum_kernel(count, *refs):
    parts = refs[:count], refs[count : 2 * count]
    outs = refs[2 * count :]
    half_cols = parts[0][0].shape[0]

    def body(core):
        for h in range(2):

            def column(c, h=h):
                for out, rows in zip(outs, rows_of(gathered_sum(parts[h], c), core)):
                    out[h * half_cols + c] = rows

            columns_loop(half_cols, column)

    by_core(body)


def last_sum(parts, shard):
    rows = shapes_of(shard)[0]
    return whole_call(
        partial(last_sum_kernel, len(parts[0])),
        "last_sum",
        [*parts[0], *parts[1]],
        [rows, rows],
        cost=(rows.size * 4, rows.size * 20),
    )


def finish_kernel(scaling, *refs):
    gradients, moments, weights = refs[:2], refs[2:4], refs[4:6]
    outs, near, sems = refs[6:8], refs[8:10], refs[10]
    columns, per_col, rows = gradients[0].shape[:3]
    core = this_core()
    copies = []
    for k in range(per_col):

        def column(c, k=k):
            for side, owner in enumerate((core, 1 - core)):
                at = pl.ds(owner * columns + c, rows, stride=2 * columns)
                moment = momentum_beta * moments[side][c, k] + scaling * gradients[side][c, k]
                near[0][k, at, :] = decay_keep * weights[side][c, k] - learn_rate * moment
                near[1][k, at, :] = moment

        columns_loop(columns, column)
        for i in range(2):
            for r in range(rows):
                rows_of_k = near[i].at[k, pl.ds(r * 2 * columns, 2 * columns)]
                copy = pltpu.make_async_copy(rows_of_k, outs[i].at[r, k], sems.at[i, k])
                copy.start()
                copies.append(copy)
    for copy in copies:
        copy.wait()


def finish(gradients, moments, weights, scaling):
    columns, per_col, rows, block = gradients[0].shape
    operands = [*gradients, *moments, *weights]
    out = pltpu.HBM((rows, per_col, 2 * columns, block), f32)
    weight, moment = pl.pallas_call(
        partial(finish_kernel, scaling),
        in_specs=[WHOLE] * len(operands),
        out_specs=[pl.BlockSpec(memory_space=pl.ANY)] * 2,
        out_shape=[out, out],
        scratch_shapes=[pltpu.VMEM((per_col, rows * 2 * columns, block), f32)] * 2
        + [pltpu.SemaphoreType.DMA((2, per_col))],
        compiler_params=PARAMS,
        cost_estimate=pl.CostEstimate(
            flops=12 * gradients[0].size, bytes_accessed=80 * gradients[0].size, transcendentals=0
        ),
        name="finish",
    )(*[vmem(x) for x in operands])
    return [x.transpose(0, 2, 1, 3) for x in (weight, moment)]


def split_kernel(out_blocks, raw, kept, given, x, sem):
    columns, per_col, rows = kept.shape[:3]
    core = this_core()
    copy = pltpu.make_async_copy(raw, x, sem)
    copy.start()
    copy.wait()

    def column(c):
        for k in range(per_col):
            for out, owner in ((given, 1 - core), (kept, core)):
                start = k * out_blocks + owner * columns + c
                out[c, k] = x[pl.ds(start, rows, stride=per_col * out_blocks), :]

    columns_loop(columns, column)


def split(x):
    rows, out_blocks, per_col, block = x.shape
    flat = x.transpose(0, 2, 1, 3).reshape(-1, block)
    half = jax.ShapeDtypeStruct((out_blocks // 2, per_col, rows, block), f32)
    return whole_call(
        partial(split_kernel, out_blocks),
        "split",
        [],
        [half, half],
        scratch=[pltpu.VMEM(flat.shape, f32), pltpu.SemaphoreType.DMA(())],
        raw=[flat],
        cost=(0, 8 * x.size),
    )


def row_cuts(rows):
    if rows % 16:
        return [pl.ds(0, rows)]
    tiles = rows // 16
    pieces = min(4, tiles)
    edges = [16 * (tiles * i // pieces) for i in range(pieces + 1)]
    return [pl.ds(a, b - a) for a, b in zip(edges, edges[1:])]


def pick_kernel(s, mine, raws, outs, sems):
    core = this_core()
    half = core if mine else 1 - core
    copies = []
    _, rows, wide = outs.shape
    for i, raw in enumerate(raws):
        lanes = pl.ds(0, wide)
        if raw.shape[3] != wide:
            lanes = pl.ds(pl.multiple_of(half * wide, wide), wide)
        for j, cut in enumerate(row_cuts(rows)):
            copies.append(
                pltpu.make_async_copy(raw.at[0, s, cut, lanes], outs.at[i, cut], sems.at[i, j])
            )
    for copy in copies:
        copy.start()
    for copy in copies:
        copy.wait()


def pick(s, mine, wide, *raws):
    rows = raws[0].shape[2]
    count = len(raws)

    def kernel(*refs):
        pick_kernel(s, mine, refs[:count], refs[count], refs[count + 1])

    (out,) = whole_call(
        kernel,
        "pick",
        [],
        [jax.ShapeDtypeStruct((count, rows, wide), bf16)],
        scratch=[pltpu.SemaphoreType.DMA((count, len(row_cuts(rows))))],
        raw=raws,
        cost=(0, 4 * count * rows * wide),
    )
    return out


def turn_kernel(n, scal, own, sib, out, turned):
    in_blocks, block, room = out.shape
    rows = own.shape[1]
    rest = jnp.zeros((room - 2 * rows, block), bf16)
    piece = block // n

    def one(p, carry):
        lane = pl.ds(pl.multiple_of(p * block, block), block)
        x = jnp.concatenate([own[0, :, lane], sib[0, :, lane], rest], axis=0)
        turned[p % 2] = x.T.reshape(n, piece, room)
        for r in range(n):
            out[p, r * piece : (r + 1) * piece] = turned[p % 2, scal[r]]
        return carry

    lax.fori_loop(0, in_blocks, one, 0, unroll=2 if in_blocks % 2 == 0 else 1)


def turn(scal, own, sib, block, n):
    _, rows, features = own.shape
    room = -(-2 * rows // block) * block
    (out,) = whole_call(
        partial(turn_kernel, n),
        "turn",
        [own, sib],
        [jax.ShapeDtypeStruct((features // block, block, room), bf16)],
        scratch=[pltpu.VMEM((2, n, block // n, room), bf16)],
        scalars=[scal],
        cost=(0, 8 * rows * features),
    )
    return out


def far_slots(n):
    return n // 2, n - n // 2


def features_of(act_t, scal, n, at, per_col, slots):
    piece = act_t.shape[1] // n
    runs = []
    for r in slots:
        if runs and runs[-1][1] == r * piece:
            runs[-1][1] += piece
        else:
            runs.append([r * piece, (r + 1) * piece])
    return jnp.concatenate(
        [act_t[scal[n + at * per_col + k], a:b] for k in range(per_col) for a, b in runs], axis=0
    )


def project(act_t, scal, n, at, weights, j):
    per_col = weights[min(weights)].shape[1]
    x = features_of(act_t, scal, n, at, per_col, sorted(weights))
    w = jnp.concatenate(
        [weights[r][j, k] for k in range(per_col) for r in sorted(weights)], axis=0
    )
    return lax.dot_general(x, w, (((0,), (0,)), ((), ())), preferred_element_type=f32)


def forward_kernel(scaling, n, scal, act_t, kept, sib, *refs):
    near = [[r for r in range(n) if r != f] for f in far_slots(n)]
    slots = [dict(zip(near[0], refs)), dict(zip(near[1], refs[n - 1 :]))]
    part = refs[-1]
    half_cols, _, _, block = refs[0].shape
    rows = part.shape[1]
    for c in range(2 * half_cols):
        h, at = c // half_cols, c % half_cols
        cut = slice(c * block, (c + 1) * block)
        out = scaling * project(act_t, scal, n, c, slots[h], at)
        for t, res in enumerate((kept.at[0], sib.at[1])):
            part[t, :, cut] = res[:, cut].astype(f32) + out[t * rows : (t + 1) * rows]


def interleaved(main, side):
    done = 0
    for i, step in enumerate(main):
        step()
        upto = len(side) * (i + 1) // len(main)
        for other in side[done:upto]:
            other()
        done = upto


def norm_kernel(per_col, scaling, n, scal, act_t, part, kept, sib, gain, far_a, far_b, *refs):
    pre, stats, sums, share = refs
    half_cols, _, _, block = far_a.shape
    rows = pre.shape[1]
    cols = group_columns(half_cols)
    base = scal[n + 2 * half_cols * per_col]
    sums[...] = jnp.zeros_like(sums)

    size = 16 if rows % 16 == 0 else rows

    def product(c):
        h = c // half_cols
        f, far = far_slots(n)[h], (far_a, far_b)[h]
        share[c // cols % 2, c % cols] = project(act_t, scal, n, c, {f: far}, c % half_cols)

    def add_up(g, t, at):
        chunk = slice(at, at + size)
        square, inner = sums[t, 0, chunk], sums[t, 1, chunk]
        for j in range(cols):
            c = g * cols + j
            cut = slice(c * block, (c + 1) * block)
            own = share[g % 2, j, t * rows + at : t * rows + at + size]
            value = part[t, chunk, cut] + scaling * own
            pre[t, chunk, cut] = value
            up = (sib.at[2] if t else kept.at[1])[chunk, cut].astype(f32)
            square += value * value
            inner += value * (gain[base + c] * up)
        sums[t, 0, chunk], sums[t, 1, chunk] = square, inner

    groups = 2 * half_cols // cols
    for g in range(groups + 1):
        side = []
        if g > 0:
            side = [partial(add_up, g - 1, t, at) for t in range(2) for at in range(0, rows, size)]
        main = [partial(product, c) for c in range(g * cols, (g + 1) * cols) if g < groups]
        interleaved(main or [lambda: None], side)

    lane = lax.broadcasted_iota(jnp.int32, stats.shape[1:], 1)
    for t in range(2):
        square = jnp.sum(sums[t, 0], axis=1, keepdims=True)
        inner = jnp.sum(sums[t, 1], axis=1, keepdims=True)
        stats[t] = jnp.where(lane < block // 2, square, inner)


def backward_kernel(per_col, width, n, scal, act_t, pre, kept, sib, gain, own, other, *refs):
    outs, grad, scales = refs[:2], refs[2], refs[3]
    half_cols, _, rows_in, block = outs[0].shape
    rows = pre.shape[1]
    cols = group_columns(half_cols)
    size = 16 if rows % 16 == 0 else rows
    base = scal[n + 2 * half_cols * per_col]

    for t in range(2):
        total = own[t] + other[1 - t]
        square, inner = total[:, 0:1], total[:, block // 2 : block // 2 + 1]
        inv = lax.rsqrt(square / width + epsilon)
        scales[t, 0] = jnp.broadcast_to(inv, scales.shape[2:])
        scales[t, 1] = jnp.broadcast_to(inv * inv * inv * (inner / width), scales.shape[2:])
    grad[:, 2 * rows :] = jnp.zeros((2 * half_cols, grad.shape[1] - 2 * rows, block), bf16)

    def gradients(g, t, at):
        up = sib.at[2] if t else kept.at[1]
        chunk = slice(at, at + size)
        inv, inner = scales[t, 0, chunk], scales[t, 1, chunk]
        for c in range(g * cols, (g + 1) * cols):
            cut = slice(c * block, (c + 1) * block)
            weighted = gain[base + c] * up[chunk, cut].astype(f32)
            to = slice(t * rows + at, t * rows + at + size)
            grad[c, to] = (inv * weighted - pre[t, chunk, cut] * inner).astype(bf16)

    def product(c):
        h = c // half_cols
        x = features_of(act_t, scal, n, c, per_col, [far_slots(n)[h]])
        term = jnp.dot(x, grad[c], preferred_element_type=f32).astype(bf16)
        outs[h][c % half_cols] = term.reshape(per_col, rows_in, block)

    groups = 2 * half_cols // cols
    for g in range(groups + 1):
        side = []
        if g < groups:
            side = [partial(gradients, g, t, at) for t in range(2) for at in range(0, rows, size)]
        main = [partial(product, c) for c in range(max(g - 1, 0) * cols, g * cols)]
        interleaved(main or [lambda: None], side)


def terms_kernel(per_col, n, scal, act_t, grad, *outs):
    near = [[r for r in range(n) if r != f] for f in far_slots(n)]
    outs = [dict(zip(near[0], outs)), dict(zip(near[1], outs[n - 1 :]))]
    half_cols, _, rows_in, block = outs[0][near[0][0]].shape
    for c in range(2 * half_cols):
        h, at = c // half_cols, c % half_cols
        x = features_of(act_t, scal, n, c, per_col, range(n))
        term = jnp.dot(x, grad[c], preferred_element_type=f32)
        term = term.astype(bf16).reshape(per_col, n, rows_in, block)
        for r in near[h]:
            outs[h][r][at] = term[:, r]


def group_columns(half_cols):
    return max(c for c in range(1, 6) if half_cols % c == 0)


def forward(scal, act_t, kept, sib, slots, scaling):
    n = len(slots[0])
    half_cols, per_col, rows_in, block = slots[0][0].shape
    _, rows, wide = kept.shape
    near = [x for h, f in enumerate(far_slots(n)) for r, x in enumerate(slots[h]) if r != f]
    (part,) = whole_call(
        partial(forward_kernel, scaling, n),
        "forward",
        [act_t, kept, sib, *near],
        [jax.ShapeDtypeStruct((2, rows, wide), f32)],
        scalars=[scal],
        cost=(4 * rows * wide * per_col * block, 16 * 2**20),
    )
    return part


def norm(scal, act_t, part, kept, sib, gain, slots, scaling):
    n = len(slots[0])
    half_cols, per_col, rows_in, block = slots[0][0].shape
    _, rows, wide = part.shape
    far = [slots[h][f] for h, f in enumerate(far_slots(n))]
    return whole_call(
        partial(norm_kernel, per_col, scaling, n),
        "norm",
        [act_t, part, kept, sib, gain, *far],
        [jax.ShapeDtypeStruct(part.shape, f32), jax.ShapeDtypeStruct((2, rows, block), f32)],
        scratch=[
            pltpu.VMEM((2, 2, rows, block), f32),
            pltpu.VMEM((2, group_columns(half_cols), act_t.shape[2], block), f32),
        ],
        scalars=[scal],
        cost=(4 * rows * wide * per_col * rows_in, 16 * 2**20),
    )


def backward(scal, act_t, pre, kept, sib, gain, own, other, shard, width):
    half_cols, per_col, rows_in, block = shard
    n = block // rows_in
    rows, wide = pre.shape[1:]
    term = jax.ShapeDtypeStruct(shard, bf16)
    grad = jax.ShapeDtypeStruct((2 * half_cols, act_t.shape[2], block), bf16)
    *far, grad = whole_call(
        partial(backward_kernel, per_col, width, n),
        "backward",
        [act_t, pre, kept, sib, gain, own, other],
        [term, term, grad],
        scratch=[pltpu.VMEM((2, 2, rows, block), f32)],
        scalars=[scal],
        cost=(4 * rows * wide * per_col * rows_in, 16 * 2**20),
    )
    return far, grad


def other_terms(scal, act_t, grad, far, shard):
    half_cols, per_col, rows_in, block = shard
    n = block // rows_in
    near = whole_call(
        partial(terms_kernel, per_col, n),
        "terms",
        [act_t, grad],
        [jax.ShapeDtypeStruct(shard, bf16)] * (2 * n - 2),
        scalars=[scal],
        cost=(2 * grad.size * per_col * block, 16 * 2**20),
    )
    slots = []
    for h, f in enumerate(far_slots(n)):
        mine = list(near[h * (n - 1) : (h + 1) * (n - 1)])
        slots.append(mine[:f] + [far[h]] + mine[f:])
    return slots


def gossip_hops():
    devices = lax.axis_size("rep")
    hops = {}
    for entry, stride in enumerate((1, 2, 4)):
        if stride % devices:
            hops.setdefault(stride % devices, []).append(entry)
    return hops


def partner_of(taken, low):
    devices = lax.axis_size("rep")
    partner = None
    for hop, chosen in taken.items():
        shift = [(i, (i + hop) % devices) for i in range(devices)]
        moved = lambda x, last, shift=shift: lax.ppermute(x, "rep", shift)
        if partner is None:
            partner = lax.cond(chosen, moved, lambda x, last: jnp.zeros_like(x), low, 0)
        else:
            partner = lax.cond(chosen, moved, lambda x, last: last, low, partner)
    return low if partner is None else partner


def mixed(taken, weight):
    devices = lax.axis_size("rep")
    for hop, chosen in taken.items():
        shift = [(i, (i + hop) % devices) for i in range(devices)]

        def mean(own, shift=shift):
            return 0.5 * (own + lax.ppermute(own.astype(bf16), "rep", shift).astype(f32))

        weight = lax.cond(chosen, mean, lambda own: own, weight)
    return weight


def body(activations, residual, upstream, norm_gain, params, momentum, pattern, step_index):
    steps, rows, features = activations.shape[1:]
    width = residual.shape[3]
    own_rows, out_blocks, per_col, block = params.shape[1:]
    scaling = 1.0 / math.sqrt(per_col * block)
    ring = Ring(lax.axis_size("fsdp"))
    n = ring.chips
    columns = out_blocks // 2
    half_cols = columns // 2

    core = this_core()
    place = ring_place(n, lax.div(lax.axis_index("fsdp"), jnp.int32(2)))
    places = place + jnp.arange(n, dtype=jnp.int32)
    chips = chip_at(n, jnp.where(places < n, places, places - n))
    used = lax.dynamic_slice_in_dim(pattern, core * columns, columns, 0)
    scal = jnp.concatenate([chips, used.reshape(-1), core[None] * columns]).astype(jnp.int32)
    gain = norm_gain.reshape(out_blocks, 1, block)

    taken, keeps = [], []
    hops = gossip_hops()
    for s in range(steps):
        entry = lax.rem(step_index[0] + s, jnp.int32(3))
        chosen = {hop: [entry == e for e in entries] for hop, entries in hops.items()}
        taken.append({hop: functools.reduce(jnp.logical_or, flags) for hop, flags in chosen.items()})
        moved = functools.reduce(jnp.logical_or, taken[s].values(), jnp.bool_(False))
        keeps.append(jnp.where(moved, 0.5, 1.0).astype(f32).reshape(1))

    shard = (half_cols, per_col, 2 * own_rows, block)
    mine, theirs = split(params[0])
    theirs = ring.swap(theirs)
    weights = [mine, theirs]
    scal, gain, taken, keeps = lax.optimization_barrier((scal, gain, taken, keeps))
    tokens = (activations, residual, upstream)

    def picked(s, mine, arrived):
        arrays = tokens[1:] if mine else tokens
        return pick(s, mine, features, *[after(x, arrived) for x in arrays])

    given = picked(0, False, scal)
    halves = list(merge(*weights, shard))
    halves[0] = after(halves[0], scal)
    sib = ring.swap(after(given, theirs))
    state = {}

    def keep(name, make):
        def work(arrived):
            state[name] = make(arrived)
            return jax.tree.leaves(state[name])

        return work

    for s in range(steps):
        last = s == steps - 1
        beside = {2: keep("kept", lambda arrived: picked(s, True, arrived))}
        if not last:
            beside[4] = keep("later", lambda arrived: picked(s + 1, False, arrived))
        beside[5] = keep("turned", lambda arrived: turn(after(scal, arrived), given, sib, block, n))
        slots = ring.gather(halves, beside)
        for i, work in beside.items():
            if i >= len(ring.rounds()):
                work(halves[0])
        kept, act_t = state["kept"], state["turned"]
        part = forward(scal, act_t, kept, sib, slots, scaling)
        pre, own = norm(scal, act_t, part, kept, sib, gain, slots, scaling)
        other = ring.swap(own)
        if s == 0:
            moments = split(after(momentum, own)[0])
            other = after(other, *moments)
        first, grad = backward(scal, act_t, pre, kept, sib, gain, own, other, shard, float(width))
        ready = []
        if not last:
            given = state["later"]
            sib = ring.swap(after(given, other))
        if s == 0:
            moments = [moments[0], ring.swap(after(moments[1], sib))]
        if last:
            moments = [moments[0], ring.swap(after(moments[1], other))]
            weights = [weights[0], ring.swap(after(weights[1], other))]
            ready += [moments[1], weights[1]]
        if ready:
            first = lax.optimization_barrier((*first, *ready))[:2]
        terms = other_terms(scal, act_t, grad, first, shard)
        if not last:
            third = max(n // 2 - 1, 1)
            terms[0][third] = after(terms[0][third], sib)
        parts = ring.scatter_sum(terms)
        if not last:
            moments, weights, low = update(parts, moments, weights, scaling, shard)
            partner = partner_of(after(taken[s], low), low)
            weights, halves = blend(keeps[s], weights, partner, shard)
    mine, theirs = last_sum(parts, shard)
    weight, moment = finish([mine, ring.swap(theirs)], moments, weights, scaling)
    return (mixed(after(taken[-1], weight), weight)[None], moment[None])


def solution(mesh):
    in_specs = (
        P("rep", None, "fsdp", None),
        P("rep", None, "fsdp", None),
        P("rep", None, "fsdp", None),
        P(),
        P("rep", "fsdp", None, None, None),
        P("rep", "fsdp", None, None, None),
        P(),
        P(),
    )
    out_specs = (P("rep", "fsdp", None, None, None), P("rep", "fsdp", None, None, None))
    return jax.shard_map(body, mesh=mesh, in_specs=in_specs, out_specs=out_specs, check_vma=False)
```

```python
import functools
import math
from functools import partial

import jax
import jax.numpy as jnp
import numpy as np
from jax import lax
from jax.experimental import pallas as pl
from jax.experimental.pallas import tpu as pltpu
from jax.sharding import PartitionSpec as P

learn_rate = 0.1
momentum_beta = 0.9
decay_keep = 0.999
epsilon = 1e-06

f32 = jnp.float32
bf16 = jnp.bfloat16
WHOLE = pl.BlockSpec(memory_space=pltpu.VMEM)
SCALARS = pl.BlockSpec(memory_space=pltpu.SMEM)
PARAMS = pltpu.CompilerParams(vmem_limit_bytes=16 * 2**20)


def vmem(x):
    return pltpu.with_memory_space_constraint(x, pltpu.VMEM)


def in_vmem(shape):
    return pltpu.VMEM(shape.shape, shape.dtype)


def after(x, *others):
    if not others:
        return x
    return lax.optimization_barrier((x, *others))[0]


def ring_order(chips):
    if chips % 2:
        return list(range(chips))
    return list(range(0, chips, 2)) + list(range(chips - 1, 0, -2))


def ring_place(chips, chip):
    if chips % 2:
        return chip
    up = lax.div(chip, jnp.int32(2))
    return jnp.where(lax.rem(chip, jnp.int32(2)) == 0, up, chips - 1 - up)


def chip_at(chips, place):
    if chips % 2:
        return place
    return jnp.where(place < chips // 2, 2 * place, 2 * (chips - 1 - place) + 1)


def this_core():
    return lax.rem(lax.axis_index("fsdp"), jnp.int32(2))


class Ring:
    def __init__(self, devices):
        self.chips = devices // 2
        order = ring_order(self.chips)
        n = self.chips
        self.to_right = [
            (2 * order[p] + k, 2 * order[(p + 1) % n] + k) for p in range(n) for k in (0, 1)
        ]
        self.to_left = [(b, a) for a, b in self.to_right]
        self.pair = [(i, i ^ 1) for i in range(devices)]

    def swap(self, x):
        return lax.ppermute(x, "fsdp", self.pair)

    def rounds(self):
        n = self.chips
        short = (n - 1) // 2
        rounds = []
        for s in range(1, n // 2 + 1):
            if s <= n - 1 - short:
                rounds.append([(0, 0, s), (1, 1, s)])
            if s <= short:
                rounds.append([(1, 0, s), (0, 1, s)])
        return rounds

    def move(self, x, direction):
        return lax.ppermute(x, "fsdp", self.to_left if direction else self.to_right)

    def gather(self, halves, beside):
        n = self.chips
        slots = [[x] + [None] * (n - 1) for x in halves]
        arrived = []
        for i, pair in enumerate(self.rounds()):
            ready = beside[i](arrived[i - 3] if i >= 3 else halves[0]) if i in beside else []
            for h, d, s in pair:
                x = after(slots[h][s - 1 if d else (1 - s) % n], *ready)
                slots[h][s if d else n - s] = self.move(x, d)
                ready = []
            arrived.append(slots[pair[0][0]][n - pair[0][2]])
        return slots

    def scatter_sum(self, slots):
        n = self.chips
        moving = {}
        for pair in sorted(self.rounds(), key=lambda pair: -pair[0][2]):
            for h, d, s in pair:
                term = slots[h][n - s if d else s]
                if (h, d) in moving:
                    term = add_low(moving[h, d], term)
                moving[h, d] = self.move(term, d)
        return [
            [slots[h][0]] + [moving[h, d] for d in range(2) if (h, d) in moving]
            for h in range(len(slots))
        ]


def add_kernel(a, b, out):
    out[...] = (a[...].astype(f32) + b[...].astype(f32)).astype(bf16)


def add_low(a, b):
    return pl.pallas_call(
        add_kernel,
        in_specs=[WHOLE, WHOLE],
        out_specs=WHOLE,
        out_shape=in_vmem(a),
        compiler_params=PARAMS,
        cost_estimate=pl.CostEstimate(flops=a.size, bytes_accessed=6 * a.size, transcendentals=0),
        name="add",
    )(vmem(a), vmem(b))


def whole_call(kernel, name, operands, outs, scratch=(), scalars=(), raw=(), cost=(0, 0)):
    return pl.pallas_call(
        kernel,
        in_specs=[SCALARS] * len(scalars)
        + [pl.BlockSpec(memory_space=pl.ANY)] * len(raw)
        + [WHOLE] * len(operands),
        out_specs=[WHOLE] * len(outs),
        out_shape=[in_vmem(x) for x in outs],
        scratch_shapes=list(scratch),
        compiler_params=PARAMS,
        cost_estimate=pl.CostEstimate(flops=cost[0], bytes_accessed=cost[1], transcendentals=0),
        name=name,
    )(
        *scalars,
        *[pltpu.with_memory_space_constraint(x, pltpu.HBM) for x in raw],
        *[vmem(x) for x in operands],
    )


def by_core(body):
    core = this_core()
    for c in range(2):
        pl.when(core == c)(partial(body, c))


def columns_loop(columns, column):
    lax.fori_loop(0, columns, lambda c, _: column(c) or 0, 0, unroll=2 if columns % 2 == 0 else 1)


def halves_of(mine, theirs, core):
    return jnp.concatenate([theirs, mine] if core else [mine, theirs], axis=-2)


def rows_of(x, core):
    rows = x.shape[-2] // 2
    low, high = x[..., :rows, :], x[..., rows:, :]
    return (high, low) if core else (low, high)


def shapes_of(shard):
    half_cols, per_col, rows_in, block = shard
    rows = jax.ShapeDtypeStruct((2 * half_cols, per_col, rows_in // 2, block), f32)
    return rows, jax.ShapeDtypeStruct(shard, bf16)


def merge_kernel(mine, theirs, low_a, low_b):
    half_cols = low_a.shape[0]

    def body(core):
        for h, out in enumerate((low_a, low_b)):

            def column(c, h=h, out=out):
                at = h * half_cols + c
                out[c] = halves_of(mine[at], theirs[at], core).astype(bf16)

            columns_loop(half_cols, column)

    by_core(body)


def merge(mine, theirs, shard):
    low = shapes_of(shard)[1]
    return whole_call(merge_kernel, "merge", [mine, theirs], [low, low], cost=(0, mine.size * 12))


def gathered_sum(parts, c):
    return sum(part[c].astype(f32) for part in parts)


def update_kernel(count, scaling, *refs):
    parts = refs[:count], refs[count : 2 * count]
    moments, weights = refs[2 * count : 2 * count + 2], refs[2 * count + 2 : 2 * count + 4]
    far = refs[2 * count + 4 : 2 * count + 9]
    near, sems = refs[2 * count + 9 : 2 * count + 14], refs[-1]
    moments_out, weights_out, low = near[:2], near[2:4], near[4]
    half_cols = low.shape[0] // 2

    cuts = [pl.ds(h * half_cols, half_cols) for h in range(2)]
    copies = [
        pltpu.make_async_copy(near[i].at[cut], far[i].at[cut], sems.at[i, h])
        for h, cut in enumerate(cuts)
        for i in range(5)
    ]

    def body(core):
        for h in range(2):

            def column(c, h=h):
                at = h * half_cols + c
                news = []
                for r, gradient in enumerate(rows_of(gathered_sum(parts[h], c), core)):
                    moment = momentum_beta * moments[r][at] + scaling * gradient
                    moments_out[r][at] = moment
                    news.append(decay_keep * weights[r][at] - learn_rate * moment)
                    weights_out[r][at] = news[r]
                low[at] = halves_of(*news, core).astype(bf16)

            columns_loop(half_cols, column)
            for copy in copies[5 * h : 5 * h + 5]:
                copy.start()

    by_core(body)
    for copy in copies:
        copy.wait()


def update(parts, moments, weights, scaling, shard):
    rows = shapes_of(shard)[0]
    low = jax.ShapeDtypeStruct((2 * shard[0], *shard[1:]), bf16)
    outs = [rows] * 4 + [low]
    operands = [*parts[0], *parts[1], *moments, *weights]
    out = pl.pallas_call(
        partial(update_kernel, len(parts[0]), scaling),
        in_specs=[WHOLE] * len(operands),
        out_specs=[pl.BlockSpec(memory_space=pl.ANY)] * 5,
        out_shape=[pltpu.HBM(x.shape, x.dtype) for x in outs],
        scratch_shapes=[pltpu.VMEM(x.shape, x.dtype) for x in outs]
        + [pltpu.SemaphoreType.DMA((5, 2))],
        compiler_params=PARAMS,
        cost_estimate=pl.CostEstimate(
            flops=rows.size * 20, bytes_accessed=rows.size * 60, transcendentals=0
        ),
        name="update",
    )(*[vmem(x) for x in operands])
    return out[:2], out[2:4], out[4]


def blend_kernel(keep, *refs):
    far, outs, (low_a, low_b) = refs[:3], refs[3:5], refs[5:7]
    near, sems = refs[7:10], refs[10]
    mine, theirs, part = near
    half_cols = low_a.shape[0]
    share = keep[0]
    copies = [pltpu.make_async_copy(far[i], near[i], sems.at[i]) for i in range(3)]
    for copy in copies:
        copy.start()
    for copy in copies:
        copy.wait()

    def body(core):
        for h, low in enumerate((low_a, low_b)):

            def column(c, h=h, low=low):
                at = h * half_cols + c
                news = []
                for own, to, other in zip(
                    (mine, theirs), outs, rows_of(part[at].astype(f32), core)
                ):
                    news.append(share * own[at] + (1.0 - share) * other)
                    to[at] = news[-1]
                low[c] = halves_of(*news, core).astype(bf16)

            columns_loop(half_cols, column)

    by_core(body)


def blend(keep, weights, partner, shard):
    rows, low = shapes_of(shard)
    outs = [rows, rows, low, low]
    raw = pl.BlockSpec(memory_space=pl.ANY)
    out = pl.pallas_call(
        blend_kernel,
        in_specs=[SCALARS] + [raw] * 3,
        out_specs=[WHOLE] * 4,
        out_shape=[in_vmem(x) for x in outs],
        scratch_shapes=[
            pltpu.VMEM(rows.shape, f32),
            pltpu.VMEM(rows.shape, f32),
            pltpu.VMEM(partner.shape, bf16),
            pltpu.SemaphoreType.DMA((3,)),
        ],
        compiler_params=PARAMS,
        cost_estimate=pl.CostEstimate(
            flops=rows.size * 6, bytes_accessed=rows.size * 24, transcendentals=0
        ),
        name="blend",
    )(keep, *[pltpu.with_memory_space_constraint(x, pltpu.HBM) for x in (*weights, partner)])
    return out[:2], list(out[2:])


def last_sum_kernel(count, *refs):
    parts = refs[:count], refs[count : 2 * count]
    outs = refs[2 * count :]
    half_cols = parts[0][0].shape[0]

    def body(core):
        for h in range(2):

            def column(c, h=h):
                for out, rows in zip(outs, rows_of(gathered_sum(parts[h], c), core)):
                    out[h * half_cols + c] = rows

            columns_loop(half_cols, column)

    by_core(body)


def last_sum(parts, shard):
    rows = shapes_of(shard)[0]
    return whole_call(
        partial(last_sum_kernel, len(parts[0])),
        "last_sum",
        [*parts[0], *parts[1]],
        [rows, rows],
        cost=(rows.size * 4, rows.size * 20),
    )


def finish_kernel(scaling, *refs):
    gradients, moments, weights = refs[:2], refs[2:4], refs[4:6]
    outs, near, sems = refs[6:8], refs[8:10], refs[10]
    columns, per_col, rows = gradients[0].shape[:3]
    core = this_core()
    copies = []
    for k in range(per_col):

        def column(c, k=k):
            for side, owner in enumerate((core, 1 - core)):
                at = pl.ds(owner * columns + c, rows, stride=2 * columns)
                moment = momentum_beta * moments[side][c, k] + scaling * gradients[side][c, k]
                near[0][k, at, :] = decay_keep * weights[side][c, k] - learn_rate * moment
                near[1][k, at, :] = moment

        columns_loop(columns, column)
        for i in range(2):
            for r in range(rows):
                rows_of_k = near[i].at[k, pl.ds(r * 2 * columns, 2 * columns)]
                copy = pltpu.make_async_copy(rows_of_k, outs[i].at[r, k], sems.at[i, k])
                copy.start()
                copies.append(copy)
    for copy in copies:
        copy.wait()


def finish(gradients, moments, weights, scaling):
    columns, per_col, rows, block = gradients[0].shape
    operands = [*gradients, *moments, *weights]
    out = pltpu.HBM((rows, per_col, 2 * columns, block), f32)
    weight, moment = pl.pallas_call(
        partial(finish_kernel, scaling),
        in_specs=[WHOLE] * len(operands),
        out_specs=[pl.BlockSpec(memory_space=pl.ANY)] * 2,
        out_shape=[out, out],
        scratch_shapes=[pltpu.VMEM((per_col, rows * 2 * columns, block), f32)] * 2
        + [pltpu.SemaphoreType.DMA((2, per_col))],
        compiler_params=PARAMS,
        cost_estimate=pl.CostEstimate(
            flops=12 * gradients[0].size, bytes_accessed=80 * gradients[0].size, transcendentals=0
        ),
        name="finish",
    )(*[vmem(x) for x in operands])
    return [x.transpose(0, 2, 1, 3) for x in (weight, moment)]


def split_kernel(out_blocks, raw, kept, given, x, sem):
    columns, per_col, rows = kept.shape[:3]
    core = this_core()
    copy = pltpu.make_async_copy(raw, x, sem)
    copy.start()
    copy.wait()

    def column(c):
        for k in range(per_col):
            for out, owner in ((given, 1 - core), (kept, core)):
                start = k * out_blocks + owner * columns + c
                out[c, k] = x[pl.ds(start, rows, stride=per_col * out_blocks), :]

    columns_loop(columns, column)


def split(x):
    rows, out_blocks, per_col, block = x.shape
    flat = x.transpose(0, 2, 1, 3).reshape(-1, block)
    half = jax.ShapeDtypeStruct((out_blocks // 2, per_col, rows, block), f32)
    return whole_call(
        partial(split_kernel, out_blocks),
        "split",
        [],
        [half, half],
        scratch=[pltpu.VMEM(flat.shape, f32), pltpu.SemaphoreType.DMA(())],
        raw=[flat],
        cost=(0, 8 * x.size),
    )


def row_cuts(rows):
    if rows % 16:
        return [pl.ds(0, rows)]
    tiles = rows // 16
    pieces = min(4, tiles)
    edges = [16 * (tiles * i // pieces) for i in range(pieces + 1)]
    return [pl.ds(a, b - a) for a, b in zip(edges, edges[1:])]


def pick_kernel(s, mine, raws, outs, sems):
    core = this_core()
    half = core if mine else 1 - core
    copies = []
    _, rows, wide = outs.shape
    for i, raw in enumerate(raws):
        lanes = pl.ds(0, wide)
        if raw.shape[3] != wide:
            lanes = pl.ds(pl.multiple_of(half * wide, wide), wide)
        for j, cut in enumerate(row_cuts(rows)):
            copies.append(
                pltpu.make_async_copy(raw.at[0, s, cut, lanes], outs.at[i, cut], sems.at[i, j])
            )
    for copy in copies:
        copy.start()
    for copy in copies:
        copy.wait()


def pick(s, mine, wide, *raws):
    rows = raws[0].shape[2]
    count = len(raws)

    def kernel(*refs):
        pick_kernel(s, mine, refs[:count], refs[count], refs[count + 1])

    (out,) = whole_call(
        kernel,
        "pick",
        [],
        [jax.ShapeDtypeStruct((count, rows, wide), bf16)],
        scratch=[pltpu.SemaphoreType.DMA((count, len(row_cuts(rows))))],
        raw=raws,
        cost=(0, 4 * count * rows * wide),
    )
    return out


def turn_kernel(n, scal, own, sib, out, turned):
    in_blocks, block, room = out.shape
    rows = own.shape[1]
    rest = jnp.zeros((room - 2 * rows, block), bf16)
    piece = block // n

    def one(p, carry):
        lane = pl.ds(pl.multiple_of(p * block, block), block)
        x = jnp.concatenate([own[0, :, lane], sib[0, :, lane], rest], axis=0)
        turned[p % 2] = x.T.reshape(n, piece, room)
        for r in range(n):
            out[p, r * piece : (r + 1) * piece] = turned[p % 2, scal[r]]
        return carry

    lax.fori_loop(0, in_blocks, one, 0, unroll=2 if in_blocks % 2 == 0 else 1)


def turn(scal, own, sib, block, n):
    _, rows, features = own.shape
    room = -(-2 * rows // block) * block
    (out,) = whole_call(
        partial(turn_kernel, n),
        "turn",
        [own, sib],
        [jax.ShapeDtypeStruct((features // block, block, room), bf16)],
        scratch=[pltpu.VMEM((2, n, block // n, room), bf16)],
        scalars=[scal],
        cost=(0, 8 * rows * features),
    )
    return out


def far_slots(n):
    return n // 2, n - n // 2


def features_of(act_t, scal, n, at, per_col, slots):
    piece = act_t.shape[1] // n
    runs = []
    for r in slots:
        if runs and runs[-1][1] == r * piece:
            runs[-1][1] += piece
        else:
            runs.append([r * piece, (r + 1) * piece])
    return jnp.concatenate(
        [act_t[scal[n + at * per_col + k], a:b] for k in range(per_col) for a, b in runs], axis=0
    )


def project(act_t, scal, n, at, weights, j):
    per_col = weights[min(weights)].shape[1]
    x = features_of(act_t, scal, n, at, per_col, sorted(weights))
    w = jnp.concatenate(
        [weights[r][j, k] for k in range(per_col) for r in sorted(weights)], axis=0
    )
    return lax.dot_general(x, w, (((0,), (0,)), ((), ())), preferred_element_type=f32)


def forward_kernel(scaling, n, scal, act_t, kept, sib, *refs):
    near = [[r for r in range(n) if r != f] for f in far_slots(n)]
    slots = [dict(zip(near[0], refs)), dict(zip(near[1], refs[n - 1 :]))]
    part = refs[-1]
    half_cols, _, _, block = refs[0].shape
    rows = part.shape[1]
    for c in range(2 * half_cols):
        h, at = c // half_cols, c % half_cols
        cut = slice(c * block, (c + 1) * block)
        out = scaling * project(act_t, scal, n, c, slots[h], at)
        for t, res in enumerate((kept.at[0], sib.at[1])):
            part[t, :, cut] = res[:, cut].astype(f32) + out[t * rows : (t + 1) * rows]


def interleaved(main, side):
    done = 0
    for i, step in enumerate(main):
        step()
        upto = len(side) * (i + 1) // len(main)
        for other in side[done:upto]:
            other()
        done = upto


def norm_kernel(per_col, scaling, n, scal, act_t, part, kept, sib, gain, far_a, far_b, *refs):
    pre, stats, sums, share = refs
    half_cols, _, _, block = far_a.shape
    rows = pre.shape[1]
    cols = group_columns(half_cols)
    base = scal[n + 2 * half_cols * per_col]
    sums[...] = jnp.zeros_like(sums)

    size = 16 if rows % 16 == 0 else rows

    def product(c):
        h = c // half_cols
        f, far = far_slots(n)[h], (far_a, far_b)[h]
        share[c // cols % 2, c % cols] = project(act_t, scal, n, c, {f: far}, c % half_cols)

    def add_up(g, t, at):
        chunk = slice(at, at + size)
        square, inner = sums[t, 0, chunk], sums[t, 1, chunk]
        for j in range(cols):
            c = g * cols + j
            cut = slice(c * block, (c + 1) * block)
            own = share[g % 2, j, t * rows + at : t * rows + at + size]
            value = part[t, chunk, cut] + scaling * own
            pre[t, chunk, cut] = value
            up = (sib.at[2] if t else kept.at[1])[chunk, cut].astype(f32)
            square += value * value
            inner += value * (gain[base + c] * up)
        sums[t, 0, chunk], sums[t, 1, chunk] = square, inner

    groups = 2 * half_cols // cols
    for g in range(groups + 1):
        side = []
        if g > 0:
            side = [partial(add_up, g - 1, t, at) for t in range(2) for at in range(0, rows, size)]
        main = [partial(product, c) for c in range(g * cols, (g + 1) * cols) if g < groups]
        interleaved(main or [lambda: None], side)

    lane = lax.broadcasted_iota(jnp.int32, stats.shape[1:], 1)
    for t in range(2):
        square = jnp.sum(sums[t, 0], axis=1, keepdims=True)
        inner = jnp.sum(sums[t, 1], axis=1, keepdims=True)
        stats[t] = jnp.where(lane < block // 2, square, inner)


def backward_kernel(per_col, width, n, scal, act_t, pre, kept, sib, gain, own, other, *refs):
    outs, grad, scales = refs[:2], refs[2], refs[3]
    half_cols, _, rows_in, block = outs[0].shape
    rows = pre.shape[1]
    cols = group_columns(half_cols)
    size = 16 if rows % 16 == 0 else rows
    base = scal[n + 2 * half_cols * per_col]

    for t in range(2):
        total = own[t] + other[1 - t]
        square, inner = total[:, 0:1], total[:, block // 2 : block // 2 + 1]
        inv = lax.rsqrt(square / width + epsilon)
        scales[t, 0] = jnp.broadcast_to(inv, scales.shape[2:])
        scales[t, 1] = jnp.broadcast_to(inv * inv * inv * (inner / width), scales.shape[2:])
    grad[:, 2 * rows :] = jnp.zeros((2 * half_cols, grad.shape[1] - 2 * rows, block), bf16)

    def gradients(g, t, at):
        up = sib.at[2] if t else kept.at[1]
        chunk = slice(at, at + size)
        inv, inner = scales[t, 0, chunk], scales[t, 1, chunk]
        for c in range(g * cols, (g + 1) * cols):
            cut = slice(c * block, (c + 1) * block)
            weighted = gain[base + c] * up[chunk, cut].astype(f32)
            to = slice(t * rows + at, t * rows + at + size)
            grad[c, to] = (inv * weighted - pre[t, chunk, cut] * inner).astype(bf16)

    def product(c):
        h = c // half_cols
        x = features_of(act_t, scal, n, c, per_col, [far_slots(n)[h]])
        term = jnp.dot(x, grad[c], preferred_element_type=f32).astype(bf16)
        outs[h][c % half_cols] = term.reshape(per_col, rows_in, block)

    groups = 2 * half_cols // cols
    for g in range(groups + 1):
        side = []
        if g < groups:
            side = [partial(gradients, g, t, at) for t in range(2) for at in range(0, rows, size)]
        main = [partial(product, c) for c in range(max(g - 1, 0) * cols, g * cols)]
        interleaved(main or [lambda: None], side)


def terms_kernel(per_col, n, scal, act_t, grad, *outs):
    near = [[r for r in range(n) if r != f] for f in far_slots(n)]
    outs = [dict(zip(near[0], outs)), dict(zip(near[1], outs[n - 1 :]))]
    half_cols, _, rows_in, block = outs[0][near[0][0]].shape
    for c in range(2 * half_cols):
        h, at = c // half_cols, c % half_cols
        x = features_of(act_t, scal, n, c, per_col, range(n))
        term = jnp.dot(x, grad[c], preferred_element_type=f32)
        term = term.astype(bf16).reshape(per_col, n, rows_in, block)
        for r in near[h]:
            outs[h][r][at] = term[:, r]


def group_columns(half_cols):
    return max(c for c in range(1, 6) if half_cols % c == 0)


def forward(scal, act_t, kept, sib, slots, scaling):
    n = len(slots[0])
    half_cols, per_col, rows_in, block = slots[0][0].shape
    _, rows, wide = kept.shape
    near = [x for h, f in enumerate(far_slots(n)) for r, x in enumerate(slots[h]) if r != f]
    (part,) = whole_call(
        partial(forward_kernel, scaling, n),
        "forward",
        [act_t, kept, sib, *near],
        [jax.ShapeDtypeStruct((2, rows, wide), f32)],
        scalars=[scal],
        cost=(4 * rows * wide * per_col * block, 16 * 2**20),
    )
    return part


def norm(scal, act_t, part, kept, sib, gain, slots, scaling):
    n = len(slots[0])
    half_cols, per_col, rows_in, block = slots[0][0].shape
    _, rows, wide = part.shape
    far = [slots[h][f] for h, f in enumerate(far_slots(n))]
    return whole_call(
        partial(norm_kernel, per_col, scaling, n),
        "norm",
        [act_t, part, kept, sib, gain, *far],
        [jax.ShapeDtypeStruct(part.shape, f32), jax.ShapeDtypeStruct((2, rows, block), f32)],
        scratch=[
            pltpu.VMEM((2, 2, rows, block), f32),
            pltpu.VMEM((2, group_columns(half_cols), act_t.shape[2], block), f32),
        ],
        scalars=[scal],
        cost=(4 * rows * wide * per_col * rows_in, 16 * 2**20),
    )


def backward(scal, act_t, pre, kept, sib, gain, own, other, shard, width):
    half_cols, per_col, rows_in, block = shard
    n = block // rows_in
    rows, wide = pre.shape[1:]
    term = jax.ShapeDtypeStruct(shard, bf16)
    grad = jax.ShapeDtypeStruct((2 * half_cols, act_t.shape[2], block), bf16)
    *far, grad = whole_call(
        partial(backward_kernel, per_col, width, n),
        "backward",
        [act_t, pre, kept, sib, gain, own, other],
        [term, term, grad],
        scratch=[pltpu.VMEM((2, 2, rows, block), f32)],
        scalars=[scal],
        cost=(4 * rows * wide * per_col * rows_in, 16 * 2**20),
    )
    return far, grad


def other_terms(scal, act_t, grad, far, shard):
    half_cols, per_col, rows_in, block = shard
    n = block // rows_in
    near = whole_call(
        partial(terms_kernel, per_col, n),
        "terms",
        [act_t, grad],
        [jax.ShapeDtypeStruct(shard, bf16)] * (2 * n - 2),
        scalars=[scal],
        cost=(2 * grad.size * per_col * block, 16 * 2**20),
    )
    slots = []
    for h, f in enumerate(far_slots(n)):
        mine = list(near[h * (n - 1) : (h + 1) * (n - 1)])
        slots.append(mine[:f] + [far[h]] + mine[f:])
    return slots


def gossip_hops():
    devices = lax.axis_size("rep")
    hops = {}
    for entry, stride in enumerate((1, 2, 4)):
        if stride % devices:
            hops.setdefault(stride % devices, []).append(entry)
    return hops


def partner_of(taken, low):
    devices = lax.axis_size("rep")
    partner = None
    for hop, chosen in taken.items():
        shift = [(i, (i + hop) % devices) for i in range(devices)]
        moved = lambda x, last, shift=shift: lax.ppermute(x, "rep", shift)
        if partner is None:
            partner = lax.cond(chosen, moved, lambda x, last: jnp.zeros_like(x), low, 0)
        else:
            partner = lax.cond(chosen, moved, lambda x, last: last, low, partner)
    return low if partner is None else partner


def mixed(taken, weight):
    devices = lax.axis_size("rep")
    for hop, chosen in taken.items():
        shift = [(i, (i + hop) % devices) for i in range(devices)]

        def mean(own, shift=shift):
            return 0.5 * (own + lax.ppermute(own.astype(bf16), "rep", shift).astype(f32))

        weight = lax.cond(chosen, mean, lambda own: own, weight)
    return weight


def body(activations, residual, upstream, norm_gain, params, momentum, pattern, step_index):
    steps, rows, features = activations.shape[1:]
    width = residual.shape[3]
    own_rows, out_blocks, per_col, block = params.shape[1:]
    scaling = 1.0 / math.sqrt(per_col * block)
    ring = Ring(lax.axis_size("fsdp"))
    n = ring.chips
    columns = out_blocks // 2
    half_cols = columns // 2

    core = this_core()
    place = ring_place(n, lax.div(lax.axis_index("fsdp"), jnp.int32(2)))
    places = place + jnp.arange(n, dtype=jnp.int32)
    chips = chip_at(n, jnp.where(places < n, places, places - n))
    used = lax.dynamic_slice_in_dim(pattern, core * columns, columns, 0)
    scal = jnp.concatenate([chips, used.reshape(-1), core[None] * columns]).astype(jnp.int32)
    gain = norm_gain.reshape(out_blocks, 1, block)

    taken, keeps = [], []
    hops = gossip_hops()
    for s in range(steps):
        entry = lax.rem(step_index[0] + s, jnp.int32(3))
        chosen = {hop: [entry == e for e in entries] for hop, entries in hops.items()}
        taken.append({hop: functools.reduce(jnp.logical_or, flags) for hop, flags in chosen.items()})
        moved = functools.reduce(jnp.logical_or, taken[s].values(), jnp.bool_(False))
        keeps.append(jnp.where(moved, 0.5, 1.0).astype(f32).reshape(1))

    shard = (half_cols, per_col, 2 * own_rows, block)
    mine, theirs = split(params[0])
    theirs = ring.swap(theirs)
    weights = [mine, theirs]
    scal, gain, taken, keeps = lax.optimization_barrier((scal, gain, taken, keeps))
    tokens = (activations, residual, upstream)

    def picked(s, mine, arrived):
        arrays = tokens[1:] if mine else tokens
        return pick(s, mine, features, *[after(x, arrived) for x in arrays])

    given = picked(0, False, scal)
    halves = list(merge(*weights, shard))
    halves[0] = after(halves[0], scal)
    sib = ring.swap(after(given, theirs))
    state = {}

    def keep(name, make):
        def work(arrived):
            state[name] = make(arrived)
            return jax.tree.leaves(state[name])

        return work

    for s in range(steps):
        last = s == steps - 1
        beside = {3: keep("kept", lambda arrived: picked(s, True, arrived))}
        if not last:
            beside[4] = keep("later", lambda arrived: picked(s + 1, False, arrived))
        beside[5] = keep("turned", lambda arrived: turn(after(scal, arrived), given, sib, block, n))
        slots = ring.gather(halves, beside)
        for i, work in beside.items():
            if i >= len(ring.rounds()):
                work(halves[0])
        kept, act_t = state["kept"], state["turned"]
        part = forward(scal, act_t, kept, sib, slots, scaling)
        pre, own = norm(scal, act_t, part, kept, sib, gain, slots, scaling)
        other = ring.swap(own)
        if s == 0:
            moments = split(after(momentum, own)[0])
            other = after(other, *moments)
        first, grad = backward(scal, act_t, pre, kept, sib, gain, own, other, shard, float(width))
        ready = []
        if not last:
            given = state["later"]
            sib = ring.swap(after(given, other))
        if s == 0:
            moments = [moments[0], ring.swap(after(moments[1], sib))]
        if last:
            moments = [moments[0], ring.swap(after(moments[1], other))]
            weights = [weights[0], ring.swap(after(weights[1], other))]
            ready += [moments[1], weights[1]]
        if ready:
            first = lax.optimization_barrier((*first, *ready))[:2]
        terms = other_terms(scal, act_t, grad, first, shard)
        if not last:
            third = max(n // 2 - 1, 1)
            terms[0][third] = after(terms[0][third], sib)
        parts = ring.scatter_sum(terms)
        if not last:
            moments, weights, low = update(parts, moments, weights, scaling, shard)
            partner = partner_of(after(taken[s], low), low)
            weights, halves = blend(keeps[s], weights, partner, shard)
    mine, theirs = last_sum(parts, shard)
    weight, moment = finish([mine, ring.swap(theirs)], moments, weights, scaling)
    return (mixed(after(taken[-1], weight), weight)[None], moment[None])


def solution(mesh):
    in_specs = (
        P("rep", None, "fsdp", None),
        P("rep", None, "fsdp", None),
        P("rep", None, "fsdp", None),
        P(),
        P("rep", "fsdp", None, None, None),
        P("rep", "fsdp", None, None, None),
        P(),
        P(),
    )
    out_specs = (P("rep", "fsdp", None, None, None), P("rep", "fsdp", None, None, None))
    return jax.shard_map(body, mesh=mesh, in_specs=in_specs, out_specs=out_specs, check_vma=False)
```
